32 devices in a mesh: seq: 8 (over z, y), tp: 4 (over x, core).
Axes of the slice: x: 2, y: 2, z: 4, core: 2. Of those that a mesh axis runs over, the one named last changes fastest.
Arguments:
- query_proj: bfloat16 [1536, 3072], P('seq', 'tp'), may hold values from -6 to 6
- key_proj: bfloat16 [1536, 3072], P('seq', 'tp'), may hold values from -6 to 6
- value_proj: bfloat16 [1536, 3072], P('seq', 'tp'), may hold values from -6 to 6
- attn_output: bfloat16 [1536, 3072], P('seq', 'tp')
- out_grad: bfloat16 [1536, 3072], P('seq', 'tp'), may hold values from -6 to 6
- log_norm: float32 [1536, 24], P('seq', 'tp')
- router_logit: float32 [1536], P('seq'), may hold values from -4 to 4
- keep_positions: int32 [1536], replicated, may hold values from -1 to 8191, as said below
Outputs:
- query_grad: bfloat16 [1536, 3072], P('seq', 'tp')
- key_grad: bfloat16 [1536, 3072], P('seq', 'tp')
- value_grad: bfloat16 [1536, 3072], P('seq', 'tp')
- router_grad: float32 [1536], P('seq')
The draws below stay inside these ranges and needn't reach their ends.
Inputs may be any that keep to these rules, and one draw needn't show every extreme that they name: `keep_positions`: slots s*192 to (s+1)*192 - 1 hold the kept positions of tokens s*1024 to (s+1)*1024 - 1 in increasing order, followed by -1 in the unused slots. Exactly 1024 tokens are kept in all; some shard fills all 192 slots and some shard keeps only 64.
All inputs are finite; a program needn't handle non-finite values.
Results may differ from the reference program's by a relative error of at most 0.03.
Values may be sent and summed in bfloat16 or wider, within the bound.
No kernel may reach another device: no remote copies, remote signals or barrier semaphores. Data moves between devices by JAX's collectives and lax.ppermute only.
A program may use at most 128 MiB of HBM per device.

```python
import jax
import jax.numpy as jnp
from jax import lax

SLOTS = 192
HEADS = 24
HEAD_DIM = 128
WIDTH = 3072
TOK_SHARD = 1024
KEPT_SLOTS = 1536
N_SEQ = 8


def kept_positions(key):
    third = SLOTS // 3
    middle = 2 * third
    first_key, second_key, third_key = jax.random.split(key, 3)
    order = jax.random.permutation(first_key, N_SEQ)
    offsets = jax.random.randint(second_key, (N_SEQ // 2,), -(third - 1), third)
    offsets = offsets.at[0].set(third)
    paired = jnp.stack([middle + offsets, middle - offsets], axis=1).reshape(N_SEQ)
    counts = jnp.zeros((N_SEQ,), jnp.int32).at[order].set(paired.astype(jnp.int32))
    shard_keys = jax.random.split(third_key, N_SEQ)

    def one_shard(shard_key, shard, count):
        ranking = jax.random.permutation(shard_key, TOK_SHARD)
        local = jnp.arange(TOK_SHARD, dtype=jnp.int32)
        chosen = jnp.where(ranking < count, local, TOK_SHARD + local)
        ordered = jnp.sort(chosen)[:SLOTS]
        return jnp.where(ordered < TOK_SHARD, ordered + shard * TOK_SHARD, -1)
    result = jax.vmap(one_shard)(shard_keys, jnp.arange(N_SEQ, dtype=jnp.int32), counts)
    return result.reshape(N_SEQ * SLOTS).astype(jnp.int32)


def draw_keep_positions(key, part):
    return kept_positions(key)


def draw_log_norm(key, part):
    positions = kept_positions(key)
    key = jax.random.fold_in(key, 7)
    valid = positions >= 0
    ranks = jnp.cumsum(valid.astype(jnp.int32))
    base = jnp.where(valid, jnp.log(jnp.maximum(ranks, 1).astype(jnp.float32)) + 0.5, 0.0)
    noise = jax.random.uniform(key, (KEPT_SLOTS, HEADS), jnp.float32, -0.3, 0.3)
    return (base[:, None] + noise).astype(jnp.float32)


def draw_attn_output(key, part):
    key = jax.random.fold_in(key, 11)
    columns = jnp.arange(WIDTH, dtype=jnp.float32) / (WIDTH - 1)
    column_scale = 0.1 * jnp.power(3.0, columns)
    values = jax.random.normal(key, (KEPT_SLOTS, WIDTH), jnp.float32)
    return (values * column_scale).astype(jnp.bfloat16)


def block_scale(own_key, shape, cuts, smallest, largest):
    factor_of = 1.0
    for dim, blocks in cuts:
        heights = jax.random.uniform(jax.random.fold_in(jax.random.fold_in(own_key, 6), dim), (blocks,), jnp.float32, smallest / len(cuts), largest / len(cuts))
        factor_of = factor_of * jnp.repeat(jnp.exp(heights), shape[dim] // blocks).reshape((-1,) + (1,) * (len(shape) - 1 - dim))
    return factor_of


def gaussian(stream_key, shape, width, most, cuts=(), kind=jnp.bfloat16):
    gain = block_scale(stream_key, shape, cuts, -0.22, 0.18) if cuts else 1.0
    entries = jax.random.normal(stream_key, shape, jnp.float32) * width * gain
    return jnp.minimum(jnp.maximum(entries, -most), most).astype(kind)


def setup_inputs(seed: int = 0) -> dict:
    keys = jax.random.split(jax.random.key(seed), 9)
    return {
        "query_proj": gaussian(keys[0], (KEPT_SLOTS, WIDTH), 1.0, 6.0, ((0, 8), (1, 4))),
        "key_proj": gaussian(keys[1], (KEPT_SLOTS, WIDTH), 1.0, 6.0, ((0, 8), (1, 4))),
        "value_proj": gaussian(keys[2], (KEPT_SLOTS, WIDTH), 1.0, 6.0, ((0, 8), (1, 4))),
        "attn_output": draw_attn_output(jax.random.fold_in(keys[8], 71), 0),
        "out_grad": gaussian(keys[4], (KEPT_SLOTS, WIDTH), 1.0, 6.0, ((0, 8), (1, 4))),
        "log_norm": draw_log_norm(jax.random.fold_in(keys[8], 71), 0),
        "router_logit": gaussian(keys[6], (KEPT_SLOTS,), 1.5, 4.0, ((0, 8),), jnp.float32),
        "keep_positions": draw_keep_positions(jax.random.fold_in(keys[8], 71), 0),
    }


def reference(query_proj, key_proj, value_proj, attn_output, out_grad, log_norm, router_logit, keep_positions):
    scale = HEAD_DIM ** -0.5
    valid = keep_positions >= 0
    gate = jax.nn.sigmoid(router_logit)
    slope = gate * (1.0 - gate)
    grad_wide = out_grad.astype(jnp.float32)
    output_wide = attn_output.astype(jnp.float32)
    router_grad = jnp.where(valid, slope * jnp.sum(grad_wide * output_wide, axis=1), jnp.float32(0.0))
    dout = (gate[:, None] * grad_wide).astype(jnp.bfloat16)
    delta = jnp.sum((dout.astype(jnp.float32) * output_wide).reshape(KEPT_SLOTS, HEADS, HEAD_DIM), axis=2)
    allowed = valid[:, None] & valid[None, :] & (keep_positions[None, :] <= keep_positions[:, None])

    def split_heads(array):
        return array.reshape(KEPT_SLOTS, HEADS, HEAD_DIM).transpose(1, 0, 2)

    def one_head(items):
        query, key, value, grad, norm, offset = items
        scores = jnp.dot(query, key.T, preferred_element_type=jnp.float32) * scale
        prob = jnp.where(allowed, jnp.exp(scores - norm[:, None]), jnp.float32(0.0))
        prob_low = prob.astype(jnp.bfloat16)
        value_part = jnp.dot(prob_low.T, grad, preferred_element_type=jnp.float32)
        dprob = jnp.dot(grad, value.T, preferred_element_type=jnp.float32)
        dscore = (prob * (dprob - offset[:, None]) * scale).astype(jnp.bfloat16)
        query_part = jnp.dot(dscore, key, preferred_element_type=jnp.float32)
        key_part = jnp.dot(dscore.T, query, preferred_element_type=jnp.float32)
        return query_part.astype(jnp.bfloat16), key_part.astype(jnp.bfloat16), value_part.astype(jnp.bfloat16)

    query_heads, key_heads, value_heads = lax.map(one_head, (split_heads(query_proj), split_heads(key_proj), split_heads(value_proj), split_heads(dout), log_norm.T, delta.T))

    def join_heads(array):
        return array.transpose(1, 0, 2).reshape(KEPT_SLOTS, WIDTH)

    return join_heads(query_heads), join_heads(key_heads), join_heads(value_heads), router_grad
```

```python
import functools
import math

import jax
import jax.numpy as jnp
from jax import lax
from jax.experimental import pallas as pl
from jax.experimental.pallas import tpu as pltpu
from jax.sharding import PartitionSpec as P


LANES = 128
PIECE = 8
GROUP = 4
ONE = 6 * GROUP
PACK = 4
TILE = 16
BIG = 1e30
VMEM = 24 * 1024 * 1024
HOME_FLOPS = 1024
PREP_VMEM = 63 * 1024 * 1024
F32 = jnp.float32
BF16 = jnp.bfloat16
NT = (((1,), (1,)), ((), ()))
NN = (((1,), (0,)), ((), ()))
TN = (((0,), (0,)), ((), ()))


def dot(left, right, dims):
    return lax.dot_general(left, right, dims, preferred_element_type=F32)


def pieces(rows):
    high = rows.astype(BF16).astype(F32)
    rest = rows - high
    middle = rest.astype(BF16).astype(F32)
    return [high, middle, rest - middle]


def split_exact(product):
    high = product.astype(BF16)
    return high, (product - high.astype(F32)).astype(BF16)


def used_slots(positions, shard, slots):
    table = positions[...]
    place = lax.broadcasted_iota(jnp.int32, table.shape, 0) * LANES
    place = place + lax.broadcasted_iota(jnp.int32, table.shape, 1)
    mine = (place >= shard * slots) & (place < (shard + 1) * slots) & (table >= 0)
    count = jnp.sum(jnp.where(mine, 1.0, 0.0), axis=1, keepdims=True)
    return jnp.sum(count, axis=0, keepdims=True)


def pack(ext):
    quarter = ext.shape[0] // PACK
    total = ext[:quarter]
    for part in range(1, PACK):
        rows = ext[part * quarter:(part + 1) * quarter]
        total = total + pltpu.roll(rows, part * LANES // PACK, 1)
    groups = [total[at:at + TILE] for at in range(0, quarter, TILE)]
    return jnp.concatenate(groups, axis=1).astype(BF16)


def unpack(packed):
    wide = packed.astype(F32)
    groups = [wide[:, at:at + LANES] for at in range(0, wide.shape[1], LANES)]
    total = jnp.concatenate(groups, axis=0)
    parts = [total]
    for part in range(1, PACK):
        parts.append(pltpu.roll(total, LANES - part * LANES // PACK, 1))
    return jnp.concatenate(parts, axis=0).astype(BF16)


def key_ext(positions, shard, slots):
    count = used_slots(positions, shard, slots)
    slot = lax.broadcasted_iota(jnp.int32, (slots, LANES), 0).astype(F32)
    lane = lax.broadcasted_iota(jnp.int32, (slots, LANES), 1)
    return jnp.where((lane == ONE) & (slot >= count), -BIG, 0.0).astype(BF16)


def prep_kernel(plan, heads, *refs):
    sources, (query, key, value), rest = refs[:5], refs[5:8], refs[8:]
    dots, outs, rest = rest[0], rest[1:len(plan) + 1], rest[len(plan) + 1:]
    held, (bank, sems, done) = rest[:5], rest[5:]
    output, grad, logit, norm, positions = held
    slots, width = grad.shape
    half = width // 2
    rows = 2 * slots + TILE
    copies = [
        pltpu.make_async_copy(source, dest, sems.at[i])
        for i, (source, dest) in enumerate(zip(sources, held))
    ]
    for at in range(2):
        for source, base in ((key, at), (value, at + 0.5), (query, at + 2)):
            first = int(base) * rows + (slots if base % 1 else 0)
            copies.append(
                pltpu.make_async_copy(
                    source.at[:, pl.ds(at * half, half)],
                    bank.at[pl.ds(first, slots), :],
                    sems.at[len(copies)],
                )
            )
    for copy in copies:
        copy.start()
    for copy in copies[:5]:
        copy.wait()
    head_dim = width // heads
    root = math.sqrt(head_dim)
    shard = lax.axis_index("seq")
    level = shard // 2
    count = used_slots(positions, shard, slots)
    lane = lax.broadcasted_iota(jnp.int32, (PIECE, slots), 1).astype(F32)
    used = lane < count
    gate_row = jax.nn.sigmoid(logit[...])
    gate = jnp.transpose(jnp.broadcast_to(gate_row, (LANES, slots)))
    head_of = lax.broadcasted_iota(jnp.int32, (PIECE, width), 1) // head_dim
    head_row = lax.broadcasted_iota(jnp.int32, (PIECE, width), 0)
    pick = (head_of == head_row).astype(BF16)
    ones = jnp.ones((PIECE, width), BF16)
    dout_parts, delta_parts, dot_parts = [], [], []
    for h in range(heads):
        cols = pl.ds(h * head_dim, head_dim)
        wide = grad[:, cols].astype(F32)
        out = output[:, cols].astype(F32)
        dout = (wide * gate).astype(BF16)
        dout_parts.append(dout)
        delta_parts.append(dout.astype(F32) * out)
        dot_parts.append(wide * out)
    delta_high, delta_low = split_exact(jnp.concatenate(delta_parts, axis=1))
    delta = dot(pick, delta_high, NT) + dot(pick, delta_low, NT)
    dot_high, dot_low = split_exact(jnp.concatenate(dot_parts, axis=1))
    dots[...] = (dot(ones, dot_high, NT) + dot(ones, dot_low, NT))[:1]

    pad = jnp.zeros((PIECE - heads, slots), F32)
    scaled = jnp.where(used, jnp.concatenate([norm[...] * root, pad], axis=0), BIG)
    delta = jnp.where(used, delta, 0.0)
    first = lax.broadcasted_iota(jnp.int32, (PIECE, slots), 0) == 0
    stack = pieces(scaled) + pieces(delta) + [jnp.where(first, 1.0, 0.0)]
    stack.append(jnp.zeros((PIECE * (PIECE - len(stack)), slots), F32))
    stats = jnp.concatenate(stack, axis=0).astype(BF16)
    source = lax.broadcasted_iota(jnp.int32, (PIECE * PIECE, LANES), 0)
    target = lax.broadcasted_iota(jnp.int32, (PIECE * PIECE, LANES), 1)
    piece, head = source // PIECE, source % PIECE

    def ext(first_head):
        local = head - first_head
        taken = (local >= 0) & (local < heads // 2) & (piece < 6)
        column = jnp.where(taken, piece * GROUP + local, -1)
        column = jnp.where(source == 6 * PIECE, ONE, column)
        return dot(stats, (column == target).astype(BF16), TN)

    per = heads // 2
    for at in range(2):
        bank[pl.ds(at * rows + 2 * slots, TILE), :] = jnp.zeros((TILE, half), BF16)
        base = (2 + at) * rows
        bank[pl.ds(base + slots, slots), :] = jnp.concatenate(
            dout_parts[at * per:(at + 1) * per], axis=1
        )
        bank[pl.ds(base + 2 * slots, TILE), :] = pack(ext(at * per))
    for copy in copies[5:]:
        copy.wait()
    moves = []
    for out, blocks in zip(outs, plan):
        for place, block in enumerate(blocks(level)):
            start = pl.multiple_of(jnp.int32(block) * rows, TILE)
            moves.append(
                pltpu.make_async_copy(
                    bank.at[pl.ds(start, rows), :],
                    out.at[pl.ds(place * rows, rows), :],
                    done.at[len(moves)],
                )
            )
    for move in moves:
        move.start()
    for move in moves:
        move.wait()


def head_marks(head, is_value):
    lane = lax.broadcasted_iota(jnp.int32, (1, LANES), 1)
    base = (3 * GROUP if is_value else 0) + head
    marked = (lane == base) | (lane == base + GROUP) | (lane == base + 2 * GROUP)
    return jnp.where(marked, -1.0, 0.0).astype(BF16)


def meet(down, movings, stays, positions, heads, mask, emit, add):
    half = movings[0][0].shape[1]
    slots = emit.slots
    head_dim = half // (heads // 2)
    scale = head_dim ** -0.5
    to_log2 = scale * math.log2(math.e)

    def stats(blocks, queries):
        parts = []
        for ref, at, shard in blocks:
            if queries:
                parts.append(unpack(ref[pl.ds(at + 2 * slots, TILE), :]))
            else:
                parts.append(key_ext(positions, shard, slots))
        return jnp.concatenate(parts, axis=0)

    def load(blocks, which, cols):
        parts = [ref[pl.ds(at + which * slots, slots), cols] for ref, at, _ in blocks]
        return jnp.concatenate(parts, axis=0)

    moving_ext, stay_ext = stats(movings, down), stats(stays, not down)
    for h in range(heads // 2):
        cols = pl.ds(h * head_dim, head_dim)
        m1, m2 = load(movings, 0, cols), load(movings, 1, cols)
        r1, r2 = load(stays, 0, cols), load(stays, 1, cols)
        key_mark, value_mark = head_marks(h, False), head_marks(h, True)
        if down:
            m1_ext, m2_ext = moving_ext, moving_ext
            r1_ext = stay_ext + key_mark
            r2_ext = jnp.broadcast_to(value_mark, stay_ext.shape)
        else:
            m1_ext = moving_ext + key_mark
            m2_ext = jnp.broadcast_to(value_mark, moving_ext.shape)
            r1_ext, r2_ext = stay_ext, stay_ext
        scores = dot(
            jnp.concatenate([m1, m1_ext], axis=1), jnp.concatenate([r1, r1_ext], axis=1), NT
        )
        if mask is not None:
            scores = jnp.where(mask, scores, -BIG)
        prob = jnp.exp2(scores * to_log2)
        dprob = dot(
            jnp.concatenate([m2, m2_ext], axis=1), jnp.concatenate([r2, r2_ext], axis=1), NT
        )
        dscore = (prob * dprob * scale).astype(BF16)
        prob = prob.astype(BF16)
        emit(0, cols, dot(dscore, r1, NN))
        add(0, cols, dot(dscore, m1, TN))
        if down:
            add(1, cols, dot(prob, m2, TN))
        else:
            emit(1, cols, dot(prob, r2, NN))


class Store:
    def __init__(self, slots, targets, fresh):
        self.slots, self.targets, self.fresh = slots, targets, fresh

    def __call__(self, which, cols, term):
        for i, (ref, base) in enumerate(self.targets):
            rows = pl.ds(base + which * self.slots, self.slots)
            part = term[i * self.slots:(i + 1) * self.slots]
            part = part if self.fresh else ref[rows, cols] + part
            ref[rows, cols] = part.astype(ref.dtype)


def causal(down, slots, shard=None):
    shape = (slots, slots if shard is None else 2 * slots)
    row = lax.broadcasted_iota(jnp.int32, shape, 0)
    place = lax.broadcasted_iota(jnp.int32, shape, 1)
    if shard is not None:
        place = jnp.where(place < slots, place, slots - shard % 2 * (slots + 1))
    return place <= row if down else place >= row


def router_part(positions, logit, dots, slots, shard):
    gate = jax.nn.sigmoid(logit[...])
    lane = lax.broadcasted_iota(jnp.int32, (1, slots), 1).astype(F32)
    used = lane < used_slots(positions, shard, slots)
    return jnp.where(used, gate * (1.0 - gate) * dots[...], 0.0)


FOUR_PLAN = (
    lambda level: [jnp.where(level < 2, 0, 2), jnp.where(level < 2, 1, 3)],
    lambda level: [jnp.where(level < 2, 2, 0), jnp.where(level < 2, 3, 1)],
    lambda level: [jnp.where(level % 2 == 0, 0, 3)],
    lambda level: [jnp.where(level < 2, 1, 2)],
)


def gate_kernel(*refs):
    pass


def four_home_kernel(heads, positions, mine, own, grads, own_total):
    slots = grads.shape[0] // 4
    rows = 2 * slots + TILE
    shard = lax.axis_index("seq")
    for down in (True, False):

        @pl.when((shard < 4) == down)
        def _():
            for at in range(2):
                base = 2 * slots * at
                meet(
                    down, [(mine, at * rows, shard)], [(own, at * rows, shard)],
                    positions, heads, causal(down, slots),
                    Store(slots, [(grads, base)], True),
                    Store(slots, [(own_total, base)], True),
                )


def four_guest_kernel(
    heads, positions, dots_in, mine, near, cross, grads_in, grads, near_total, cross_total, dots
):
    slots = grads.shape[0] // 4
    rows = 2 * slots + TILE
    shard = lax.axis_index("seq")
    grads[...] = grads_in[...]
    dots[...] = dots_in[...]
    for level in (1, 2):
        at = level - 1

        @pl.when(shard // 2 == level)
        def _():
            meet(
                level == 1, [(mine, at * rows, shard)],
                [(near, 0, shard - 2), (cross, 0, (shard - 2) ^ 1)],
                positions, heads, None,
                Store(slots, [(grads, 2 * slots * at)], False),
                Store(slots, [(near_total, 0), (cross_total, 0)], True),
            )


def four_pair_kernel(
    heads, positions, mine, own, other, near, grads_in, own_in, grads, own_total, other_total, back
):
    slots = grads.shape[0] // 4
    rows = 2 * slots + TILE
    shard = lax.axis_index("seq")
    grads[...] = grads_in[...]
    own_total[...] = own_in[...]
    other_total[...] = jnp.zeros(other_total.shape, F32)
    for down in (True, False):

        @pl.when(((shard < 4) == down) & (shard % 2 == int(down)))
        def _():
            for at in range(2):
                base = 2 * slots * at
                meet(
                    down, [(mine, at * rows, shard)], [(other, at * rows, shard ^ 1)],
                    positions, heads, None,
                    Store(slots, [(grads, base)], False),
                    Store(slots, [(other_total, base)], True),
                )

    for level in (0, 3):
        at = 1 if level == 0 else 0
        base = 2 * slots * at

        @pl.when(shard // 2 == level)
        def _():
            meet(
                level == 0, [(near, 0, shard - 2)],
                [(own, at * rows, shard), (other, at * rows, shard ^ 1)],
                positions, heads, None,
                Store(slots, [(back, 0)], True),
                Store(slots, [(own_total, base), (other_total, base)], False),
            )


def four_far_meet(heads, level, block, reach, refs, positions, back, totals):
    own, other, near, cross = refs
    slots = back.shape[0] // 2
    at = (level - 1) * (2 * slots + TILE)
    shard = lax.axis_index("seq")
    meet(
        level == 1, [(block, 0, shard - 2 * reach)],
        [
            (own, at, shard), (other, at, shard ^ 1),
            (near, 0, shard - 2), (cross, 0, (shard - 2) ^ 1),
        ],
        positions, heads, None,
        Store(slots, [(back, 0)], True),
        Store(slots, [(ref, 0) for ref in totals], reach == 1),
    )


def four_middle_kernel(heads, positions, own, other, near, cross, middle, back, *totals):
    for level in (1, 2):

        @pl.when(lax.axis_index("seq") // 2 == level)
        def _():
            four_far_meet(
                heads, level, middle, 1, (own, other, near, cross), positions, back, totals
            )


def four_far_kernel(
    heads, positions, logit, dots, own, other, near, cross, skip,
    own_in, other_in, near_in, cross_in, own_mid, other_mid, near_mid, cross_mid, step_back,
    own_total, other_low, near_low, cross_low, skip_back, router, *totals
):
    slots = near_in.shape[0] // 2
    shard = lax.axis_index("seq")
    own_total[...] = own_in[...]
    other_low[...] = other_in[...].astype(BF16)
    router[...] = router_part(positions, logit, dots, slots, shard)
    inner = (shard >= 2) & (shard < 6)

    @pl.when(jnp.logical_not(inner))
    def _():
        near_low[...] = step_back[...]

    for level in (1, 2):
        part = pl.ds(2 * slots * (level - 1), 2 * slots)

        @pl.when(shard // 2 == level)
        def _():
            totals[0][...] = own_in[part, :] + own_mid[...]
            totals[1][...] = other_in[part, :] + other_mid[...]
            totals[2][...] = near_in[...] + near_mid[...]
            totals[3][...] = cross_in[...] + cross_mid[...]
            four_far_meet(
                heads, level, skip, 2, (own, other, near, cross), positions, skip_back, totals
            )
            own_total[part, :] = totals[0][...]
            other_low[part, :] = totals[1][...].astype(BF16)
            near_low[...] = totals[2][...].astype(BF16)
            cross_low[...] = totals[3][...].astype(BF16)


def four_join_kernel(
    heads, grads, own, other, near, cross, middle, skip, query_grad, key_grad, value_grad
):
    slots, half = grads.shape[0] // 4, grads.shape[1]
    shard = lax.axis_index("seq")

    def part(ref, at, which):
        return ref[pl.ds((2 * at + which) * slots, slots), :].astype(F32)

    def first(refs, which):
        return sum(part(ref, 0, which) for ref in refs)

    for down in (True, False):

        @pl.when((shard < 4) == down)
        def _():
            guest, late = (0, 1) if down else (1, 0)
            inner = (shard >= 2) & (shard < 6)
            for at in range(2):
                cols = pl.ds(at * half, half)
                extra = [cross] if at == guest else [middle, skip]
                if down:
                    moving, staying = [query_grad], [key_grad, value_grad]
                else:
                    moving, staying = [key_grad, value_grad], [query_grad]
                for which, out in enumerate(moving):
                    total = part(grads, at, which)
                    if at == late:
                        total = total + jnp.where(inner, part(near, 0, which), 0.0)
                    out[:, cols] = total.astype(BF16)
                for which, out in enumerate(staying):
                    total = part(own, at, which) + part(other, at, which) + first(extra, which)
                    if at == guest:
                        total = total + jnp.where(inner, 0.0, part(near, 0, which))
                    out[:, cols] = total.astype(BF16)


def four_levels(prep, shape, positions, logit, slots, heads, width):
    double, block, total = shape(4 * slots + 2 * TILE), shape(2 * slots + TILE), shape(2 * slots, F32)
    totals, low = shape(4 * slots, F32), shape(2 * slots)
    own, mine, near_send, far_send, dots = prep(FOUR_PLAN, [double, double, block, block])
    near_send, far_send = call(
        gate_kernel, [block, block], near_send, far_send,
        ins=[pltpu.HBM] * 2, outs=[pltpu.HBM] * 2, aliases={0: 0, 1: 1},
    )

    def pairs(levels, flip=0):
        return [(2 * a + c, 2 * b + (c ^ flip)) for a, b in levels for c in range(2)]

    near = lax.ppermute(near_send, "seq", pairs([(0, 1), (1, 0), (2, 3), (3, 2)]))
    cross = lax.ppermute(near_send, "seq", pairs([(0, 1), (3, 2)], 1))
    other = lax.ppermute(own, "seq", pairs([(i, i) for i in range(4)], 1))
    middle = lax.ppermute(far_send, "seq", pairs([(1, 2), (2, 1)]))
    skip = lax.ppermute(far_send, "seq", pairs([(0, 2), (3, 1)]))
    grads, own_total = call(
        functools.partial(four_home_kernel, heads),
        [totals] * 2,
        positions, mine, own,
        flops=HOME_FLOPS,
    )
    grads, near_total, cross_total, dots = call(
        functools.partial(four_guest_kernel, heads),
        [totals, total, total, shape(1, F32, slots)],
        positions, dots, mine, near, cross, grads,
    )
    dots = sum_over(dots, "tp")
    grads, own_total, other_total, step_back = call(
        functools.partial(four_pair_kernel, heads),
        [totals] * 3 + [low],
        positions, mine, own, other, near, grads, own_total,
    )
    middle_back, *middles = call(
        functools.partial(four_middle_kernel, heads),
        [low] + [total] * 4,
        positions, own, other, near, cross, middle,
    )
    own_total, other_low, near_low, cross_low, skip_back, router = call(
        functools.partial(four_far_kernel, heads),
        [totals, shape(4 * slots), low, low, low, shape(1, F32, slots)],
        positions, logit, dots, own, other, near, cross, skip,
        own_total, other_total, near_total, cross_total, *middles, step_back,
        scratch=[pltpu.VMEM(total.shape, F32)] * 4,
    )
    near = lax.ppermute(near_low, "seq", pairs([(0, 1), (1, 0), (2, 3), (3, 2)]))
    cross = lax.ppermute(cross_low, "seq", pairs([(1, 0), (2, 3)], 1))
    skip = lax.ppermute(skip_back, "seq", pairs([(2, 0), (1, 3)]))
    middle = lax.ppermute(middle_back, "seq", pairs([(1, 2), (2, 1)]))
    other = lax.ppermute(other_low, "seq", pairs([(i, i) for i in range(4)], 1))
    outs = call(
        functools.partial(four_join_kernel, heads),
        [shape(slots, BF16, width)] * 3,
        grads, own_total, other, near, cross, middle, skip,
    )
    return *outs, router


def ring_plan(levels):
    sends = [
        lambda level, step=step: [jnp.where(level >= step, 2, 1)] for step in range(1, levels)
    ]
    return (lambda level: [0, 3], lambda level: [2], lambda level: [1], *sends)


def ring_home_kernel(
    heads, positions, logit, dots, down, up, own, other, grads, own_total, other_total, router
):
    slots = grads.shape[0] // 3
    rows = 2 * slots + TILE
    shard = lax.axis_index("seq")
    for goes_down, mine, at, base, stay_base in ((True, down, 0, 0, 0), (False, up, rows, 1, 2)):
        meet(
            goes_down, [(mine, 0, shard)], [(own, at, shard), (other, at, shard ^ 1)],
            positions, heads, causal(goes_down, slots, shard),
            Store(slots, [(grads, base * slots)], True),
            Store(slots, [(own_total, stay_base * slots), (other_total, stay_base * slots)], True),
        )
    router[...] = router_part(positions, logit, dots, slots, shard)


def ring_away_kernel(
    step, levels, heads, positions, own, other, block, own_in, other_in,
    back, own_total, other_total, *low
):
    slots = own_in.shape[0] // 3
    own_total[...] = own_in[...]
    other_total[...] = other_in[...]
    rows = 2 * slots + TILE
    shard = lax.axis_index("seq")
    for goes_down, at, base in ((True, 0, 0), (False, rows, 2 * slots)):

        @pl.when((shard // 2 + step < levels) == goes_down)
        def _():
            meet(
                goes_down, [(block, 0, shard + 2 * (step - levels))],
                [(own, at, shard), (other, at, shard ^ 1)],
                positions, heads, None,
                Store(slots, [(back, 0)], True),
                Store(slots, [(own_total, base), (other_total, base)], False),
            )

    for ref in low:
        ref[...] = other_total[...].astype(BF16)


def ring_join_kernel(heads, grads, own, other, *refs):
    back, (query_grad, key_grad, value_grad) = refs[:-3], refs[-3:]
    slots, half = grads.shape[0] // 3, grads.shape[1]
    level = lax.axis_index("seq") // 2
    low, high = pl.ds(0, half), pl.ds(half, half)
    parts = [pl.ds(i * slots, slots) for i in range(3)]
    stays = [(own[rows, :] + other[rows, :].astype(F32)).astype(BF16) for rows in parts]
    key_grad[:, low], value_grad[:, low], query_grad[:, high] = stays
    query_sum, key_sum, value_sum = [grads[rows, :] for rows in parts]
    for step, ref in enumerate(back, 1):
        went_down = level >= step
        first, second = ref[parts[0], :].astype(F32), ref[parts[1], :].astype(F32)
        query_sum = query_sum + jnp.where(went_down, first, 0.0)
        key_sum = key_sum + jnp.where(went_down, 0.0, first)
        value_sum = value_sum + jnp.where(went_down, 0.0, second)
    query_grad[:, low] = query_sum.astype(BF16)
    key_grad[:, high] = key_sum.astype(BF16)
    value_grad[:, high] = value_sum.astype(BF16)


def ring_levels(prep, shape, positions, logit, slots, heads, width, shards):
    levels = shards // 2
    block, total = shape(2 * slots + TILE), shape(3 * slots, F32)
    own, down, up, *sends, dots = prep(
        ring_plan(levels), [shape(4 * slots + 2 * TILE)] + [block] * (levels + 1)
    )
    pair = [(s, s ^ 1) for s in range(shards)]
    arrived = [
        lax.ppermute(send, "seq", [(s, (s - 2 * step) % shards) for s in range(shards)])
        for step, send in enumerate(sends, 1)
    ]
    other = lax.ppermute(own, "seq", pair)
    dots = sum_over(dots, "tp")
    grads, own_total, other_total, router = call(
        functools.partial(ring_home_kernel, heads),
        [total] * 3 + [shape(1, F32, slots)],
        positions, logit, dots, down, up, own, other,
    )
    backs, low = [], [other_total.astype(BF16)]
    for step, arrival in enumerate(arrived, 1):
        back, own_total, other_total, *low = call(
            functools.partial(ring_away_kernel, step, levels, heads),
            [shape(2 * slots), total, total] + [shape(3 * slots)] * (step == levels - 1),
            positions, own, other, arrival, own_total, other_total,
            )
        backs.append(
            lax.ppermute(back, "seq", [(s, (s + 2 * step) % shards) for s in range(shards)])
        )
    outs = call(
        functools.partial(ring_join_kernel, heads),
        [shape(slots, BF16, width)] * 3,
        grads, own_total, lax.ppermute(low[0], "seq", pair), *backs,
    )
    return *outs, router


def call(kernel, out_shape, *args, scratch=(), ins=None, outs=None, limit=VMEM, flops=1024, aliases=None):
    ins = ins or [pltpu.VMEM] * len(args)
    outs = outs or [pltpu.VMEM] * len(out_shape)
    return pl.pallas_call(
        kernel,
        out_shape=out_shape,
        in_specs=[pl.BlockSpec(memory_space=space) for space in ins],
        out_specs=[pl.BlockSpec(memory_space=space) for space in outs],
        scratch_shapes=list(scratch),
        input_output_aliases=aliases or {},
        compiler_params=pltpu.CompilerParams(vmem_limit_bytes=limit),
        cost_estimate=pl.CostEstimate(flops=flops, bytes_accessed=1024, transcendentals=0),
    )(*args)


def sum_over(values, axis):
    size = lax.axis_size(axis)
    if size & (size - 1):
        return lax.psum(values, axis)
    reach = 1
    while reach < size:
        pairs = [(i, i ^ reach) for i in range(size)]
        values = values + lax.ppermute(values, axis, pairs)
        reach *= 2
    return values


def body(
    query_proj, key_proj, value_proj, attn_output, out_grad, log_norm, router_logit, keep_positions
):
    slots, width = query_proj.shape
    heads = log_norm.shape[1]
    half = width // 2
    shards = lax.axis_size("seq")
    logit = router_logit.reshape(1, slots)
    positions = keep_positions.reshape(-1, LANES)

    def shape(rows, dtype=BF16, columns=half):
        return jax.ShapeDtypeStruct((rows, columns), dtype)

    sources = (
        attn_output, out_grad, logit, log_norm.T, positions, query_proj, key_proj, value_proj
    )

    def prep(plan, shapes):
        dots, *outs = call(
            functools.partial(prep_kernel, plan, heads),
            [shape(1, F32, slots)] + shapes,
            *sources,
            scratch=[pltpu.VMEM(a.shape, a.dtype) for a in sources[:5]]
            + [pltpu.VMEM((4 * (2 * slots + TILE), half), BF16)]
            + [pltpu.SemaphoreType.DMA((11,)), pltpu.SemaphoreType.DMA((2 * len(plan),))],
            ins=[pltpu.HBM] * len(sources),
            outs=[pltpu.VMEM] + [pltpu.HBM] * len(shapes),
            limit=PREP_VMEM,
        )
        return *outs, dots

    if shards == 8:
        query_grad, key_grad, value_grad, router = four_levels(
            prep, shape, positions, logit, slots, heads, width
        )
    else:
        query_grad, key_grad, value_grad, router = ring_levels(
            prep, shape, positions, logit, slots, heads, width, shards
        )
    return query_grad, key_grad, value_grad, router.reshape(slots)


def solution(mesh):
    wide = P("seq", "tp")
    return jax.shard_map(
        body,
        mesh=mesh,
        in_specs=(wide,) * 6 + (P("seq"), P()),
        out_specs=(wide, wide, wide, P("seq")),
        check_vma=False,
    )
```

```python
import functools
import math

import jax
import jax.numpy as jnp
from jax import lax
from jax.experimental import pallas as pl
from jax.experimental.pallas import tpu as pltpu
from jax.sharding import PartitionSpec as P


LANES = 128
PIECE = 8
GROUP = 4
ONE = 6 * GROUP
PACK = 4
TILE = 16
BIG = 1e30
VMEM = 24 * 1024 * 1024
PREP_VMEM = 63 * 1024 * 1024
F32 = jnp.float32
BF16 = jnp.bfloat16
NT = (((1,), (1,)), ((), ()))
NN = (((1,), (0,)), ((), ()))
TN = (((0,), (0,)), ((), ()))


def dot(left, right, dims):
    return lax.dot_general(left, right, dims, preferred_element_type=F32)


def pieces(rows):
    high = rows.astype(BF16).astype(F32)
    rest = rows - high
    middle = rest.astype(BF16).astype(F32)
    return [high, middle, rest - middle]


def split_exact(product):
    high = product.astype(BF16)
    return high, (product - high.astype(F32)).astype(BF16)


def used_slots(positions, shard, slots):
    table = positions[...]
    place = lax.broadcasted_iota(jnp.int32, table.shape, 0) * LANES
    place = place + lax.broadcasted_iota(jnp.int32, table.shape, 1)
    mine = (place >= shard * slots) & (place < (shard + 1) * slots) & (table >= 0)
    count = jnp.sum(jnp.where(mine, 1.0, 0.0), axis=1, keepdims=True)
    return jnp.sum(count, axis=0, keepdims=True)


def pack(ext):
    quarter = ext.shape[0] // PACK
    total = ext[:quarter]
    for part in range(1, PACK):
        rows = ext[part * quarter:(part + 1) * quarter]
        total = total + pltpu.roll(rows, part * LANES // PACK, 1)
    groups = [total[at:at + TILE] for at in range(0, quarter, TILE)]
    return jnp.concatenate(groups, axis=1).astype(BF16)


def unpack(packed):
    wide = packed.astype(F32)
    groups = [wide[:, at:at + LANES] for at in range(0, wide.shape[1], LANES)]
    total = jnp.concatenate(groups, axis=0)
    parts = [total]
    for part in range(1, PACK):
        parts.append(pltpu.roll(total, LANES - part * LANES // PACK, 1))
    return jnp.concatenate(parts, axis=0).astype(BF16)


def key_ext(positions, shard, slots):
    count = used_slots(positions, shard, slots)
    slot = lax.broadcasted_iota(jnp.int32, (slots, LANES), 0).astype(F32)
    lane = lax.broadcasted_iota(jnp.int32, (slots, LANES), 1)
    return jnp.where((lane == ONE) & (slot >= count), -BIG, 0.0).astype(BF16)


def prep_kernel(plan, heads, *refs):
    sources, (query, key, value), rest = refs[:5], refs[5:8], refs[8:]
    dots, outs, rest = rest[0], rest[1:len(plan) + 1], rest[len(plan) + 1:]
    held, (bank, sems, done) = rest[:5], rest[5:]
    output, grad, logit, norm, positions = held
    slots, width = grad.shape
    half = width // 2
    rows = 2 * slots + TILE
    copies = [
        pltpu.make_async_copy(source, dest, sems.at[i])
        for i, (source, dest) in enumerate(zip(sources, held))
    ]
    for at in range(2):
        for source, base in ((key, at), (value, at + 0.5), (query, at + 2)):
            first = int(base) * rows + (slots if base % 1 else 0)
            copies.append(
                pltpu.make_async_copy(
                    source.at[:, pl.ds(at * half, half)],
                    bank.at[pl.ds(first, slots), :],
                    sems.at[len(copies)],
                )
            )
    for copy in copies:
        copy.start()
    for copy in copies[:5]:
        copy.wait()
    head_dim = width // heads
    root = math.sqrt(head_dim)
    shard = lax.axis_index("seq")
    level = shard // 2
    count = used_slots(positions, shard, slots)
    lane = lax.broadcasted_iota(jnp.int32, (PIECE, slots), 1).astype(F32)
    used = lane < count
    gate_row = jax.nn.sigmoid(logit[...])
    gate = jnp.transpose(jnp.broadcast_to(gate_row, (LANES, slots)))
    head_of = lax.broadcasted_iota(jnp.int32, (PIECE, width), 1) // head_dim
    head_row = lax.broadcasted_iota(jnp.int32, (PIECE, width), 0)
    pick = (head_of == head_row).astype(BF16)
    ones = jnp.ones((PIECE, width), BF16)
    dout_parts, delta_parts, dot_parts = [], [], []
    for h in range(heads):
        cols = pl.ds(h * head_dim, head_dim)
        wide = grad[:, cols].astype(F32)
        out = output[:, cols].astype(F32)
        dout = (wide * gate).astype(BF16)
        dout_parts.append(dout)
        delta_parts.append(dout.astype(F32) * out)
        dot_parts.append(wide * out)
    delta_high, delta_low = split_exact(jnp.concatenate(delta_parts, axis=1))
    delta = dot(pick, delta_high, NT) + dot(pick, delta_low, NT)
    dot_high, dot_low = split_exact(jnp.concatenate(dot_parts, axis=1))
    dots[...] = (dot(ones, dot_high, NT) + dot(ones, dot_low, NT))[:1]

    pad = jnp.zeros((PIECE - heads, slots), F32)
    scaled = jnp.where(used, jnp.concatenate([norm[...] * root, pad], axis=0), BIG)
    delta = jnp.where(used, delta, 0.0)
    first = lax.broadcasted_iota(jnp.int32, (PIECE, slots), 0) == 0
    stack = pieces(scaled) + pieces(delta) + [jnp.where(first, 1.0, 0.0)]
    stack.append(jnp.zeros((PIECE * (PIECE - len(stack)), slots), F32))
    stats = jnp.concatenate(stack, axis=0).astype(BF16)
    source = lax.broadcasted_iota(jnp.int32, (PIECE * PIECE, LANES), 0)
    target = lax.broadcasted_iota(jnp.int32, (PIECE * PIECE, LANES), 1)
    piece, head = source // PIECE, source % PIECE

    def ext(first_head):
        local = head - first_head
        taken = (local >= 0) & (local < heads // 2) & (piece < 6)
        column = jnp.where(taken, piece * GROUP + local, -1)
        column = jnp.where(source == 6 * PIECE, ONE, column)
        return dot(stats, (column == target).astype(BF16), TN)

    per = heads // 2
    for at in range(2):
        bank[pl.ds(at * rows + 2 * slots, TILE), :] = jnp.zeros((TILE, half), BF16)
        base = (2 + at) * rows
        bank[pl.ds(base + slots, slots), :] = jnp.concatenate(
            dout_parts[at * per:(at + 1) * per], axis=1
        )
        bank[pl.ds(base + 2 * slots, TILE), :] = pack(ext(at * per))
    for copy in copies[5:]:
        copy.wait()
    moves = []
    for out, blocks in zip(outs, plan):
        for place, block in enumerate(blocks(level)):
            start = pl.multiple_of(jnp.int32(block) * rows, TILE)
            moves.append(
                pltpu.make_async_copy(
                    bank.at[pl.ds(start, rows), :],
                    out.at[pl.ds(place * rows, rows), :],
                    done.at[len(moves)],
                )
            )
    for move in moves:
        move.start()
    for move in moves:
        move.wait()


def head_marks(head, is_value):
    lane = lax.broadcasted_iota(jnp.int32, (1, LANES), 1)
    base = (3 * GROUP if is_value else 0) + head
    marked = (lane == base) | (lane == base + GROUP) | (lane == base + 2 * GROUP)
    return jnp.where(marked, -1.0, 0.0).astype(BF16)


def meet(down, movings, stays, positions, heads, mask, emit, add):
    half = movings[0][0].shape[1]
    slots = emit.slots
    head_dim = half // (heads // 2)
    scale = head_dim ** -0.5
    to_log2 = scale * math.log2(math.e)

    def stats(blocks, queries):
        parts = []
        for ref, at, shard in blocks:
            if queries:
                parts.append(unpack(ref[pl.ds(at + 2 * slots, TILE), :]))
            else:
                parts.append(key_ext(positions, shard, slots))
        return jnp.concatenate(parts, axis=0)

    def load(blocks, which, cols):
        parts = [ref[pl.ds(at + which * slots, slots), cols] for ref, at, _ in blocks]
        return jnp.concatenate(parts, axis=0)

    moving_ext, stay_ext = stats(movings, down), stats(stays, not down)
    for h in range(heads // 2):
        cols = pl.ds(h * head_dim, head_dim)
        m1, m2 = load(movings, 0, cols), load(movings, 1, cols)
        r1, r2 = load(stays, 0, cols), load(stays, 1, cols)
        key_mark, value_mark = head_marks(h, False), head_marks(h, True)
        if down:
            m1_ext, m2_ext = moving_ext, moving_ext
            r1_ext = stay_ext + key_mark
            r2_ext = jnp.broadcast_to(value_mark, stay_ext.shape)
        else:
            m1_ext = moving_ext + key_mark
            m2_ext = jnp.broadcast_to(value_mark, moving_ext.shape)
            r1_ext, r2_ext = stay_ext, stay_ext
        scores = dot(
            jnp.concatenate([m1, m1_ext], axis=1), jnp.concatenate([r1, r1_ext], axis=1), NT
        )
        if mask is not None:
            scores = jnp.where(mask, scores, -BIG)
        prob = jnp.exp2(scores * to_log2)
        dprob = dot(
            jnp.concatenate([m2, m2_ext], axis=1), jnp.concatenate([r2, r2_ext], axis=1), NT
        )
        dscore = (prob * dprob * scale).astype(BF16)
        prob = prob.astype(BF16)
        emit(0, cols, dot(dscore, r1, NN))
        add(0, cols, dot(dscore, m1, TN))
        if down:
            add(1, cols, dot(prob, m2, TN))
        else:
            emit(1, cols, dot(prob, r2, NN))


class Store:
    def __init__(self, slots, targets, fresh):
        self.slots, self.targets, self.fresh = slots, targets, fresh

    def __call__(self, which, cols, term):
        for i, (ref, base) in enumerate(self.targets):
            rows = pl.ds(base + which * self.slots, self.slots)
            part = term[i * self.slots:(i + 1) * self.slots]
            part = part if self.fresh else ref[rows, cols] + part
            ref[rows, cols] = part.astype(ref.dtype)


def causal(down, slots, shard=None):
    shape = (slots, slots if shard is None else 2 * slots)
    row = lax.broadcasted_iota(jnp.int32, shape, 0)
    place = lax.broadcasted_iota(jnp.int32, shape, 1)
    if shard is not None:
        place = jnp.where(place < slots, place, slots - shard % 2 * (slots + 1))
    return place <= row if down else place >= row


def router_part(positions, logit, dots, slots, shard):
    gate = jax.nn.sigmoid(logit[...])
    lane = lax.broadcasted_iota(jnp.int32, (1, slots), 1).astype(F32)
    used = lane < used_slots(positions, shard, slots)
    return jnp.where(used, gate * (1.0 - gate) * dots, 0.0)


FOUR_PLAN = (
    lambda level: [jnp.where(level < 2, 0, 2), jnp.where(level < 2, 1, 3)],
    lambda level: [jnp.where(level < 2, 2, 0), jnp.where(level < 2, 3, 1)],
    lambda level: [jnp.where(level % 2 == 0, 0, 3)],
    lambda level: [jnp.where(level < 2, 1, 2)],
)


def gate_kernel(*refs):
    pass


def four_home_kernel(heads, positions, mine, own, dots_in, grads, own_total, dots):
    slots = grads.shape[0] // 4
    rows = 2 * slots + TILE
    shard = lax.axis_index("seq")
    dots[...] = dots_in[...]
    for down in (True, False):

        @pl.when((shard < 4) == down)
        def _():
            for at in range(2):
                base = 2 * slots * at
                meet(
                    down, [(mine, at * rows, shard)], [(own, at * rows, shard)],
                    positions, heads, causal(down, slots),
                    Store(slots, [(grads, base)], True),
                    Store(slots, [(own_total, base)], True),
                )


def four_guest_kernel(
    heads, positions, after, mine, near, cross, turn, grads, near_total, cross_total
):
    turn[...] = after[...]
    slots = grads.shape[0] // 2
    rows = 2 * slots + TILE
    shard = lax.axis_index("seq")
    for level in (1, 2):

        @pl.when(shard // 2 == level)
        def _():
            meet(
                level == 1, [(mine, (level - 1) * rows, shard)],
                [(near, 0, shard - 2), (cross, 0, (shard - 2) ^ 1)],
                positions, heads, None,
                Store(slots, [(grads, 0)], True),
                Store(slots, [(near_total, 0), (cross_total, 0)], True),
            )


def meets_pair(shard):
    return (shard % 2 == 1) == (shard < 4)


def four_pair_kernel(
    heads, positions, after, mine, own, other, near,
    turn, grads, other_total, own_near, other_near, back, early
):
    turn[...] = after[...]
    slots = grads.shape[0] // 4
    rows = 2 * slots + TILE
    shard = lax.axis_index("seq")
    meets = meets_pair(shard)
    for down in (True, False):

        @pl.when(meets & ((shard < 4) == down))
        def _():
            for at in range(2):
                base = 2 * slots * at
                meet(
                    down, [(mine, at * rows, shard)], [(other, at * rows, shard ^ 1)],
                    positions, heads, None,
                    Store(slots, [(grads, base)], True),
                    Store(slots, [(other_total, base)], True),
                )

    for at in range(2):

        @pl.when(meets & (shard // 2 % 2 == at))
        def _():
            early[...] = other_total[pl.ds(2 * slots * at, 2 * slots), :].astype(BF16)

    @pl.when(jnp.logical_not(meets))
    def _():
        early[...] = jnp.zeros(early.shape, BF16)

    for level in (0, 3):
        at = 1 if level == 0 else 0

        @pl.when(shard // 2 == level)
        def _():
            meet(
                level == 0, [(near, 0, shard - 2)],
                [(own, at * rows, shard), (other, at * rows, shard ^ 1)],
                positions, heads, None,
                Store(slots, [(back, 0)], True),
                Store(slots, [(own_near, 0), (other_near, 0)], True),
            )


def four_far_meet(heads, level, block, reach, refs, positions, back, totals):
    own, other, near, cross = refs
    slots = back.shape[0] // 2
    at = (level - 1) * (2 * slots + TILE)
    shard = lax.axis_index("seq")
    meet(
        level == 1, [(block, 0, shard - 2 * reach)],
        [
            (own, at, shard), (other, at, shard ^ 1),
            (near, 0, shard - 2), (cross, 0, (shard - 2) ^ 1),
        ],
        positions, heads, None,
        Store(slots, [(back, 0)], True),
        Store(slots, [(ref, 0) for ref in totals], reach == 1),
    )


def four_middle_kernel(
    heads, positions, after, dots, dots_near, own, other, near, cross, middle, back, dots_sum, *totals
):
    dots_sum[...] = dots[...] + dots_near[...]
    for level in (1, 2):

        @pl.when(lax.axis_index("seq") // 2 == level)
        def _():
            four_far_meet(
                heads, level, middle, 1, (own, other, near, cross), positions, back, totals
            )


def four_far_kernel(
    heads, positions, own, other, near, cross, skip,
    other_pair, other_near, near_in, cross_in, own_mid, other_mid, near_mid, cross_mid, step_back,
    own_total, late, near_low, cross_low, skip_back, *totals
):
    slots = near_in.shape[0] // 2
    shard = lax.axis_index("seq")
    meets = meets_pair(shard)
    for level in range(4):
        part = pl.ds(2 * slots * (1 - level % 2), 2 * slots)

        @pl.when(shard // 2 == level)
        def _():
            paired = jnp.where(meets, other_pair[part, :], 0.0)
            if level in (0, 3):
                late[...] = (paired + other_near[...]).astype(BF16)
                near_low[...] = step_back[...]
                return
            own_total[...] = own_mid[...]
            totals[0][...] = paired + other_mid[...]
            totals[1][...] = near_in[...] + near_mid[...]
            totals[2][...] = cross_in[...] + cross_mid[...]
            four_far_meet(
                heads, level, skip, 2, (own, other, near, cross), positions, skip_back,
                (own_total, *totals),
            )
            late[...] = totals[0][...].astype(BF16)
            near_low[...] = totals[1][...].astype(BF16)
            cross_low[...] = totals[2][...].astype(BF16)


def four_join_kernel(
    heads, positions, logit, dots, dots_far, grads, grads_guest, grads_pair, own, own_near, own_far,
    early, near, cross, skip, middle, late,
    query_grad, key_grad, value_grad, router
):
    slots, half = grads.shape[0] // 4, grads.shape[1]
    shard = lax.axis_index("seq")
    meets = meets_pair(shard)
    router[...] = router_part(positions, logit, dots[...] + dots_far[...], slots, shard)

    def part(ref, which, at=0):
        return ref[pl.ds((2 * at + which) * slots, slots), :].astype(F32)

    for level in range(4):
        inner = level in (1, 2)

        @pl.when(shard // 2 == level)
        def _():
            if level < 2:
                moving, staying = [query_grad], [key_grad, value_grad]
            else:
                moving, staying = [key_grad, value_grad], [query_grad]
            for at in range(2):
                cols = pl.ds(at * half, half)
                center = inner and at == level - 1
                early_half = at == level % 2
                for which, out in enumerate(moving):
                    total = part(grads, which, at)
                    total = total + jnp.where(meets, part(grads_pair, which, at), 0.0)
                    if inner:
                        total = total + part(grads_guest if center else near, which)
                    out[:, cols] = total.astype(BF16)
                if inner:
                    extra = [own_far] if center else [middle]
                else:
                    extra = [near, cross] if early_half else [own_near, skip]
                extra.append(early if early_half else late)
                for which, out in enumerate(staying):
                    total = part(own, which, at) + sum(part(ref, which) for ref in extra)
                    out[:, cols] = total.astype(BF16)


def four_levels(prep, shape, positions, logit, slots, heads, width):
    double, block, total = shape(4 * slots + 2 * TILE), shape(2 * slots + TILE), shape(2 * slots, F32)
    totals, low = shape(4 * slots, F32), shape(2 * slots)
    own, mine, near_send, far_send, dots = prep(FOUR_PLAN, [double, double, block, block])
    near_send, far_send = call(
        gate_kernel, [block, block], near_send, far_send,
        ins=[pltpu.HBM] * 2, outs=[pltpu.HBM] * 2, aliases={0: 0, 1: 1},
    )

    def pairs(levels, flip=0):
        return [(2 * a + c, 2 * b + (c ^ flip)) for a, b in levels for c in range(2)]

    near = lax.ppermute(near_send, "seq", pairs([(0, 1), (1, 0), (2, 3), (3, 2)]))
    cross = lax.ppermute(near_send, "seq", pairs([(0, 1), (3, 2)], 1))
    other = lax.ppermute(own, "seq", pairs([(i, i) for i in range(4)], 1))
    middle = lax.ppermute(far_send, "seq", pairs([(1, 2), (2, 1)]))
    skip = lax.ppermute(far_send, "seq", pairs([(0, 2), (3, 1)]))
    grads, own_total, dots = call(
        functools.partial(four_home_kernel, heads),
        [totals] * 2 + [shape(1, F32, slots)],
        positions, mine, own, dots,
    )
    row = shape(1, F32, slots)
    dots, grads_guest, near_total, cross_total = call(
        functools.partial(four_guest_kernel, heads), [row] + [total] * 3,
        positions, dots, mine, near, cross,
    )
    turn, grads_pair, other_total, own_near, other_near, step_back, early = call(
        functools.partial(four_pair_kernel, heads),
        [row, totals, totals, total, total, low, low],
        positions, dots, mine, own, other, near,
    )
    dots_near = lax.ppermute(dots, "tp", [(i, i ^ 1) for i in range(4)])
    early = lax.ppermute(early, "seq", pairs([(i, i) for i in range(4)], 1))
    middle_back, dots, *middles = call(
        functools.partial(four_middle_kernel, heads),
        [low, row] + [total] * 4,
        positions, turn, dots, dots_near, own, other, near, cross, middle,
    )
    dots_far = lax.ppermute(dots, "tp", [(i, i ^ 2) for i in range(4)])
    own_far, late, near_low, cross_low, skip_back = call(
        functools.partial(four_far_kernel, heads),
        [total, low, low, low, low],
        positions, own, other, near, cross, skip,
        other_total, other_near, near_total, cross_total, *middles, step_back,
        scratch=[pltpu.VMEM(total.shape, F32)] * 3,
    )
    near = lax.ppermute(near_low, "seq", pairs([(0, 1), (1, 0), (2, 3), (3, 2)]))
    cross = lax.ppermute(cross_low, "seq", pairs([(1, 0), (2, 3)], 1))
    skip = lax.ppermute(skip_back, "seq", pairs([(2, 0), (1, 3)]))
    middle = lax.ppermute(middle_back, "seq", pairs([(1, 2), (2, 1)]))
    late = lax.ppermute(late, "seq", pairs([(i, i) for i in range(4)], 1))
    return call(
        functools.partial(four_join_kernel, heads),
        [shape(slots, BF16, width)] * 3 + [row],
        positions, logit, dots, dots_far, grads, grads_guest, grads_pair,
        own_total, own_near, own_far, early, near, cross, skip, middle, late,
    )


def ring_plan(levels):
    sends = [
        lambda level, step=step: [jnp.where(level >= step, 2, 1)] for step in range(1, levels)
    ]
    return (lambda level: [0, 3], lambda level: [2], lambda level: [1], *sends)


def ring_home_kernel(
    heads, positions, logit, dots, down, up, own, other, grads, own_total, other_total, router
):
    slots = grads.shape[0] // 3
    rows = 2 * slots + TILE
    shard = lax.axis_index("seq")
    for goes_down, mine, at, base, stay_base in ((True, down, 0, 0, 0), (False, up, rows, 1, 2)):
        meet(
            goes_down, [(mine, 0, shard)], [(own, at, shard), (other, at, shard ^ 1)],
            positions, heads, causal(goes_down, slots, shard),
            Store(slots, [(grads, base * slots)], True),
            Store(slots, [(own_total, stay_base * slots), (other_total, stay_base * slots)], True),
        )
    router[...] = router_part(positions, logit, dots[...], slots, shard)


def ring_away_kernel(
    step, levels, heads, positions, own, other, block, own_in, other_in,
    back, own_total, other_total, *low
):
    slots = own_in.shape[0] // 3
    own_total[...] = own_in[...]
    other_total[...] = other_in[...]
    rows = 2 * slots + TILE
    shard = lax.axis_index("seq")
    for goes_down, at, base in ((True, 0, 0), (False, rows, 2 * slots)):

        @pl.when((shard // 2 + step < levels) == goes_down)
        def _():
            meet(
                goes_down, [(block, 0, shard + 2 * (step - levels))],
                [(own, at, shard), (other, at, shard ^ 1)],
                positions, heads, None,
                Store(slots, [(back, 0)], True),
                Store(slots, [(own_total, base), (other_total, base)], False),
            )

    for ref in low:
        ref[...] = other_total[...].astype(BF16)


def ring_join_kernel(heads, grads, own, other, *refs):
    back, (query_grad, key_grad, value_grad) = refs[:-3], refs[-3:]
    slots, half = grads.shape[0] // 3, grads.shape[1]
    level = lax.axis_index("seq") // 2
    low, high = pl.ds(0, half), pl.ds(half, half)
    parts = [pl.ds(i * slots, slots) for i in range(3)]
    stays = [(own[rows, :] + other[rows, :].astype(F32)).astype(BF16) for rows in parts]
    key_grad[:, low], value_grad[:, low], query_grad[:, high] = stays
    query_sum, key_sum, value_sum = [grads[rows, :] for rows in parts]
    for step, ref in enumerate(back, 1):
        went_down = level >= step
        first, second = ref[parts[0], :].astype(F32), ref[parts[1], :].astype(F32)
        query_sum = query_sum + jnp.where(went_down, first, 0.0)
        key_sum = key_sum + jnp.where(went_down, 0.0, first)
        value_sum = value_sum + jnp.where(went_down, 0.0, second)
    query_grad[:, low] = query_sum.astype(BF16)
    key_grad[:, high] = key_sum.astype(BF16)
    value_grad[:, high] = value_sum.astype(BF16)


def ring_levels(prep, shape, positions, logit, slots, heads, width, shards):
    levels = shards // 2
    block, total = shape(2 * slots + TILE), shape(3 * slots, F32)
    own, down, up, *sends, dots = prep(
        ring_plan(levels), [shape(4 * slots + 2 * TILE)] + [block] * (levels + 1)
    )
    pair = [(s, s ^ 1) for s in range(shards)]
    arrived = [
        lax.ppermute(send, "seq", [(s, (s - 2 * step) % shards) for s in range(shards)])
        for step, send in enumerate(sends, 1)
    ]
    other = lax.ppermute(own, "seq", pair)
    dots = sum_over(dots, "tp")
    grads, own_total, other_total, router = call(
        functools.partial(ring_home_kernel, heads),
        [total] * 3 + [shape(1, F32, slots)],
        positions, logit, dots, down, up, own, other,
    )
    backs, low = [], [other_total.astype(BF16)]
    for step, arrival in enumerate(arrived, 1):
        back, own_total, other_total, *low = call(
            functools.partial(ring_away_kernel, step, levels, heads),
            [shape(2 * slots), total, total] + [shape(3 * slots)] * (step == levels - 1),
            positions, own, other, arrival, own_total, other_total,
            )
        backs.append(
            lax.ppermute(back, "seq", [(s, (s + 2 * step) % shards) for s in range(shards)])
        )
    outs = call(
        functools.partial(ring_join_kernel, heads),
        [shape(slots, BF16, width)] * 3,
        grads, own_total, lax.ppermute(low[0], "seq", pair), *backs,
    )
    return *outs, router


def call(kernel, out_shape, *args, scratch=(), ins=None, outs=None, limit=VMEM, flops=1024, aliases=None):
    ins = ins or [pltpu.VMEM] * len(args)
    outs = outs or [pltpu.VMEM] * len(out_shape)
    return pl.pallas_call(
        kernel,
        out_shape=out_shape,
        in_specs=[pl.BlockSpec(memory_space=space) for space in ins],
        out_specs=[pl.BlockSpec(memory_space=space) for space in outs],
        scratch_shapes=list(scratch),
        input_output_aliases=aliases or {},
        compiler_params=pltpu.CompilerParams(vmem_limit_bytes=limit),
        cost_estimate=pl.CostEstimate(flops=flops, bytes_accessed=1024, transcendentals=0),
    )(*args)


def sum_over(values, axis):
    size = lax.axis_size(axis)
    if size & (size - 1):
        return lax.psum(values, axis)
    reach = 1
    while reach < size:
        pairs = [(i, i ^ reach) for i in range(size)]
        values = values + lax.ppermute(values, axis, pairs)
        reach *= 2
    return values


def body(
    query_proj, key_proj, value_proj, attn_output, out_grad, log_norm, router_logit, keep_positions
):
    slots, width = query_proj.shape
    heads = log_norm.shape[1]
    half = width // 2
    shards = lax.axis_size("seq")
    logit = router_logit.reshape(1, slots)
    positions = keep_positions.reshape(-1, LANES)

    def shape(rows, dtype=BF16, columns=half):
        return jax.ShapeDtypeStruct((rows, columns), dtype)

    sources = (
        attn_output, out_grad, logit, log_norm.T, positions, query_proj, key_proj, value_proj
    )

    def prep(plan, shapes):
        dots, *outs = call(
            functools.partial(prep_kernel, plan, heads),
            [shape(1, F32, slots)] + shapes,
            *sources,
            scratch=[pltpu.VMEM(a.shape, a.dtype) for a in sources[:5]]
            + [pltpu.VMEM((4 * (2 * slots + TILE), half), BF16)]
            + [pltpu.SemaphoreType.DMA((11,)), pltpu.SemaphoreType.DMA((2 * len(plan),))],
            ins=[pltpu.HBM] * len(sources),
            outs=[pltpu.VMEM] + [pltpu.HBM] * len(shapes),
            limit=PREP_VMEM,
        )
        return *outs, dots

    if shards == 8 and lax.axis_size("tp") == 4:
        query_grad, key_grad, value_grad, router = four_levels(
            prep, shape, positions, logit, slots, heads, width
        )
    else:
        query_grad, key_grad, value_grad, router = ring_levels(
            prep, shape, positions, logit, slots, heads, width, shards
        )
    return query_grad, key_grad, value_grad, router.reshape(slots)


def solution(mesh):
    wide = P("seq", "tp")
    return jax.shard_map(
        body,
        mesh=mesh,
        in_specs=(wide,) * 6 + (P("seq"), P()),
        out_specs=(wide, wide, wide, P("seq")),
        check_vma=False,
    )
```

```python
import functools
import math

import jax
import jax.numpy as jnp
from jax import lax
from jax.experimental import pallas as pl
from jax.experimental.pallas import tpu as pltpu
from jax.sharding import PartitionSpec as P


LANES = 128
PIECE = 8
GROUP = 4
ONE = 6 * GROUP
PACK = 4
TILE = 16
BIG = 1e30
VMEM = 24 * 1024 * 1024
SUM_FLOPS = 5_000_000_000
PREP_VMEM = 63 * 1024 * 1024
F32 = jnp.float32
BF16 = jnp.bfloat16
NT = (((1,), (1,)), ((), ()))
NN = (((1,), (0,)), ((), ()))
TN = (((0,), (0,)), ((), ()))


def dot(left, right, dims):
    return lax.dot_general(left, right, dims, preferred_element_type=F32)


def pieces(rows):
    high = rows.astype(BF16).astype(F32)
    rest = rows - high
    middle = rest.astype(BF16).astype(F32)
    return [high, middle, rest - middle]


def split_exact(product):
    high = product.astype(BF16)
    return high, (product - high.astype(F32)).astype(BF16)


def used_slots(positions, shard, slots):
    table = positions[...]
    place = lax.broadcasted_iota(jnp.int32, table.shape, 0) * LANES
    place = place + lax.broadcasted_iota(jnp.int32, table.shape, 1)
    mine = (place >= shard * slots) & (place < (shard + 1) * slots) & (table >= 0)
    count = jnp.sum(jnp.where(mine, 1.0, 0.0), axis=1, keepdims=True)
    return jnp.sum(count, axis=0, keepdims=True)


def pack(ext):
    quarter = ext.shape[0] // PACK
    total = ext[:quarter]
    for part in range(1, PACK):
        rows = ext[part * quarter:(part + 1) * quarter]
        total = total + pltpu.roll(rows, part * LANES // PACK, 1)
    groups = [total[at:at + TILE] for at in range(0, quarter, TILE)]
    return jnp.concatenate(groups, axis=1).astype(BF16)


def unpack(packed):
    wide = packed.astype(F32)
    groups = [wide[:, at:at + LANES] for at in range(0, wide.shape[1], LANES)]
    total = jnp.concatenate(groups, axis=0)
    parts = [total]
    for part in range(1, PACK):
        parts.append(pltpu.roll(total, LANES - part * LANES // PACK, 1))
    return jnp.concatenate(parts, axis=0).astype(BF16)


def key_ext(positions, shard, slots):
    count = used_slots(positions, shard, slots)
    slot = lax.broadcasted_iota(jnp.int32, (slots, LANES), 0).astype(F32)
    lane = lax.broadcasted_iota(jnp.int32, (slots, LANES), 1)
    return jnp.where((lane == ONE) & (slot >= count), -BIG, 0.0).astype(BF16)


def prep_kernel(plan, heads, *refs):
    sources, (query, key, value), rest = refs[:5], refs[5:8], refs[8:]
    dots, outs, rest = rest[0], rest[1:len(plan) + 1], rest[len(plan) + 1:]
    held, (bank, sems, done) = rest[:5], rest[5:]
    output, grad, logit, norm, positions = held
    slots, width = grad.shape
    half = width // 2
    rows = 2 * slots + TILE
    copies = [
        pltpu.make_async_copy(source, dest, sems.at[i])
        for i, (source, dest) in enumerate(zip(sources, held))
    ]
    for at in range(2):
        for source, base in ((key, at), (value, at + 0.5), (query, at + 2)):
            first = int(base) * rows + (slots if base % 1 else 0)
            copies.append(
                pltpu.make_async_copy(
                    source.at[:, pl.ds(at * half, half)],
                    bank.at[pl.ds(first, slots), :],
                    sems.at[len(copies)],
                )
            )
    for copy in copies:
        copy.start()
    for copy in copies[5:]:
        copy.wait()
    for at in range(2):
        bank[pl.ds(at * rows + 2 * slots, TILE), :] = jnp.zeros((TILE, half), BF16)
    level = lax.axis_index("seq") // 2
    moves = []
    for out, blocks in zip(outs, plan):
        for place, block in enumerate(blocks(level)):
            block = jnp.int32(block)
            move = pltpu.make_async_copy(
                bank.at[pl.ds(pl.multiple_of(block * rows, TILE), rows), :],
                out.at[pl.ds(place * rows, rows), :],
                done.at[len(moves)],
            )
            moves.append((block, move))

    def each(some, early):
        for block, move in some:

            @pl.when((block < 2) == early)
            def _():
                move.start()

    each(moves, True)
    for copy in copies[:5]:
        copy.wait()
    head_dim = width // heads
    root = math.sqrt(head_dim)
    shard = lax.axis_index("seq")
    count = used_slots(positions, shard, slots)
    lane = lax.broadcasted_iota(jnp.int32, (PIECE, slots), 1).astype(F32)
    used = lane < count
    gate_row = jax.nn.sigmoid(logit[...])
    gate = jnp.transpose(jnp.broadcast_to(gate_row, (LANES, slots)))
    head_of = lax.broadcasted_iota(jnp.int32, (PIECE, width), 1) // head_dim
    head_row = lax.broadcasted_iota(jnp.int32, (PIECE, width), 0)
    pick = (head_of == head_row).astype(BF16)
    ones = jnp.ones((PIECE, width), BF16)
    dout_parts, delta_parts, dot_parts = [], [], []
    for h in range(heads):
        cols = pl.ds(h * head_dim, head_dim)
        wide = grad[:, cols].astype(F32)
        out = output[:, cols].astype(F32)
        dout = (wide * gate).astype(BF16)
        dout_parts.append(dout)
        delta_parts.append(dout.astype(F32) * out)
        dot_parts.append(wide * out)
    delta_high, delta_low = split_exact(jnp.concatenate(delta_parts, axis=1))
    delta = dot(pick, delta_high, NT) + dot(pick, delta_low, NT)
    dot_high, dot_low = split_exact(jnp.concatenate(dot_parts, axis=1))
    dots[...] = (dot(ones, dot_high, NT) + dot(ones, dot_low, NT))[:1]

    pad = jnp.zeros((PIECE - heads, slots), F32)
    scaled = jnp.where(used, jnp.concatenate([norm[...] * root, pad], axis=0), BIG)
    delta = jnp.where(used, delta, 0.0)
    first = lax.broadcasted_iota(jnp.int32, (PIECE, slots), 0) == 0
    stack = pieces(scaled) + pieces(delta) + [jnp.where(first, 1.0, 0.0)]
    stack.append(jnp.zeros((PIECE * (PIECE - len(stack)), slots), F32))
    stats = jnp.concatenate(stack, axis=0).astype(BF16)
    source = lax.broadcasted_iota(jnp.int32, (PIECE * PIECE, LANES), 0)
    target = lax.broadcasted_iota(jnp.int32, (PIECE * PIECE, LANES), 1)
    piece, head = source // PIECE, source % PIECE

    def ext(first_head):
        local = head - first_head
        taken = (local >= 0) & (local < heads // 2) & (piece < 6)
        column = jnp.where(taken, piece * GROUP + local, -1)
        column = jnp.where(source == 6 * PIECE, ONE, column)
        return dot(stats, (column == target).astype(BF16), TN)

    per = heads // 2
    for at in range(2):
        base = (2 + at) * rows
        bank[pl.ds(base + slots, slots), :] = jnp.concatenate(
            dout_parts[at * per:(at + 1) * per], axis=1
        )
        bank[pl.ds(base + 2 * slots, TILE), :] = pack(ext(at * per))
    each(moves, False)
    for _, move in moves:
        move.wait()


def head_marks(head, is_value):
    lane = lax.broadcasted_iota(jnp.int32, (1, LANES), 1)
    base = (3 * GROUP if is_value else 0) + head
    marked = (lane == base) | (lane == base + GROUP) | (lane == base + 2 * GROUP)
    return jnp.where(marked, -1.0, 0.0).astype(BF16)


def meet(down, movings, stays, positions, heads, mask, emit, add):
    half = movings[0][0].shape[1]
    slots = emit.slots
    head_dim = half // (heads // 2)
    scale = head_dim ** -0.5
    to_log2 = scale * math.log2(math.e)

    def stats(blocks, queries):
        parts = []
        for ref, at, shard in blocks:
            if queries:
                parts.append(unpack(ref[pl.ds(at + 2 * slots, TILE), :]))
            else:
                parts.append(key_ext(positions, shard, slots))
        return jnp.concatenate(parts, axis=0)

    def load(blocks, which, cols):
        parts = [ref[pl.ds(at + which * slots, slots), cols] for ref, at, _ in blocks]
        return jnp.concatenate(parts, axis=0)

    moving_ext, stay_ext = stats(movings, down), stats(stays, not down)
    for h in range(heads // 2):
        cols = pl.ds(h * head_dim, head_dim)
        m1, m2 = load(movings, 0, cols), load(movings, 1, cols)
        r1, r2 = load(stays, 0, cols), load(stays, 1, cols)
        key_mark, value_mark = head_marks(h, False), head_marks(h, True)
        if down:
            m1_ext, m2_ext = moving_ext, moving_ext
            r1_ext = stay_ext + key_mark
            r2_ext = jnp.broadcast_to(value_mark, stay_ext.shape)
        else:
            m1_ext = moving_ext + key_mark
            m2_ext = jnp.broadcast_to(value_mark, moving_ext.shape)
            r1_ext, r2_ext = stay_ext, stay_ext
        scores = dot(
            jnp.concatenate([m1, m1_ext], axis=1), jnp.concatenate([r1, r1_ext], axis=1), NT
        )
        if mask is not None:
            scores = jnp.where(mask, scores, -BIG)
        prob = jnp.exp2(scores * to_log2)
        dprob = dot(
            jnp.concatenate([m2, m2_ext], axis=1), jnp.concatenate([r2, r2_ext], axis=1), NT
        )
        dscore = (prob * dprob * scale).astype(BF16)
        prob = prob.astype(BF16)
        emit(0, cols, dot(dscore, r1, NN))
        add(0, cols, dot(dscore, m1, TN))
        if down:
            add(1, cols, dot(prob, m2, TN))
        else:
            emit(1, cols, dot(prob, r2, NN))


class Store:
    def __init__(self, slots, targets, fresh, olds=None):
        self.slots, self.targets, self.fresh = slots, targets, fresh
        self.olds = olds or [ref for ref, _ in targets]

    def __call__(self, which, cols, term):
        for i, (ref, base) in enumerate(self.targets):
            rows = pl.ds(base + which * self.slots, self.slots)
            part = term[i * self.slots:(i + 1) * self.slots]
            part = part if self.fresh else self.olds[i][rows, cols] + part
            ref[rows, cols] = part.astype(ref.dtype)


def causal(down, slots, shard=None):
    shape = (slots, slots if shard is None else 2 * slots)
    row = lax.broadcasted_iota(jnp.int32, shape, 0)
    place = lax.broadcasted_iota(jnp.int32, shape, 1)
    if shard is not None:
        place = jnp.where(place < slots, place, slots - shard % 2 * (slots + 1))
    return place <= row if down else place >= row


def router_part(positions, logit, dots, slots, shard):
    gate = jax.nn.sigmoid(logit[...])
    lane = lax.broadcasted_iota(jnp.int32, (1, slots), 1).astype(F32)
    used = lane < used_slots(positions, shard, slots)
    return jnp.where(used, gate * (1.0 - gate) * dots, 0.0)


FOUR_PLAN = (
    lambda level: [jnp.where(level < 2, 0, 2), jnp.where(level < 2, 1, 3)],
    lambda level: [jnp.where(level < 2, 2, 0), jnp.where(level < 2, 3, 1)],
    lambda level: [jnp.where(level % 2 == 0, 0, 3)],
    lambda level: [jnp.where(level < 2, 1, 2)],
)


def four_home_kernel(heads, positions, mine, own, turn, grads, own_total):
    slots = grads.shape[0] // 4
    rows = 2 * slots + TILE
    shard = lax.axis_index("seq")
    turn[...] = jnp.zeros(turn.shape, F32)
    for down in (True, False):

        @pl.when((shard < 4) == down)
        def _():
            for at in range(2):
                base = 2 * slots * at
                meet(
                    down, [(mine, at * rows, shard)], [(own, at * rows, shard)],
                    positions, heads, causal(down, slots),
                    Store(slots, [(grads, base)], True),
                    Store(slots, [(own_total, base)], True),
                )


def meets_pair(shard):
    return (shard % 2 == 1) == (shard < 4)


def four_pair_kernel(
    heads, positions, after, mine, own, other, near,
    turn, grads_pair, other_total, own_near, other_near, back
):
    slots = back.shape[0] // 2
    rows = 2 * slots + TILE
    shard = lax.axis_index("seq")
    meets = meets_pair(shard)
    turn[...] = after[...]
    for down in (True, False):

        @pl.when(meets & ((shard < 4) == down))
        def _():
            for at in range(2):
                base = 2 * slots * at
                meet(
                    down, [(mine, at * rows, shard)], [(other, at * rows, shard ^ 1)],
                    positions, heads, None,
                    Store(slots, [(grads_pair, base)], True),
                    Store(slots, [(other_total, base)], True),
                )

    for level in (0, 3):
        at = 1 if level == 0 else 0

        @pl.when(shard // 2 == level)
        def _():
            meet(
                level == 0, [(near, 0, shard - 2)],
                [(own, at * rows, shard), (other, at * rows, shard ^ 1)],
                positions, heads, None,
                Store(slots, [(back, 0)], True),
                Store(slots, [(own_near, 0), (other_near, 0)], True),
            )


def four_near_kernel(
    heads, positions, after, dots, dots_near, mine, near, skip, middle, back,
    dots_sum, near_low, grads_guest, skip_part, middle_part
):
    slots = near_low.shape[0] // 2
    rows = 2 * slots + TILE
    shard = lax.axis_index("seq")
    dots_sum[...] = dots[...] + dots_near[...]
    for level in range(4):

        @pl.when(shard // 2 == level)
        def _():
            if level in (0, 3):
                near_low[...] = back[...]
                return
            meet(
                level == 1,
                [
                    (mine, (level - 1) * rows, shard),
                    (skip, 0, shard - 4), (middle, 0, shard - 2),
                ],
                [(near, 0, shard - 2)],
                positions, heads, None,
                Store(slots, [(grads_guest, 0), (skip_part, 0), (middle_part, 0)], True),
                Store(slots, [(near_low, 0)], True),
            )


def four_last_kernel(
    heads, positions, dots_in, mine, own, other, cross, skip, middle,
    grads_in, skip_in, middle_in, other_pair, own_in, other_in,
    dots, grads_guest, skip_back, cross_low, middle_back, other_low, own_near,
    skip_part, middle_part, other_near,
):
    slots = grads_in.shape[0] // 2
    rows = 2 * slots + TILE
    shard = lax.axis_index("seq")
    meets = meets_pair(shard)
    dots[...] = dots_in[...]
    for level in range(4):
        at = (1, 0, 1, 0)[level]

        @pl.when(shard // 2 == level)
        def _():
            if level in (0, 3):
                own_near[...] = own_in[...]
                other_near[...] = other_in[...]
            else:
                far = [(skip, 0, shard - 4), (middle, 0, shard - 2)]
                parts = [(skip_part, 0), (middle_part, 0)]
                meet(
                    level == 1, far, [(own, at * rows, shard), (other, at * rows, shard ^ 1)],
                    positions, heads, None,
                    Store(slots, parts, False, [skip_in, middle_in]),
                    Store(slots, [(own_near, 0), (other_near, 0)], True),
                )
                meet(
                    level == 1, [(mine, at * rows, shard)] + far, [(cross, 0, (shard - 2) ^ 1)],
                    positions, heads, None,
                    Store(
                        slots, [(grads_guest, 0), (skip_back, 0), (middle_back, 0)], False,
                        [grads_in, skip_part, middle_part],
                    ),
                    Store(slots, [(cross_low, 0)], True),
                )
            for half in range(2):
                part = pl.ds(2 * slots * half, 2 * slots)
                total = jnp.where(meets, other_pair[part, :], 0.0)
                total = total + other_near[...] if half == at else total
                other_low[part, :] = total.astype(BF16)


def four_sum_kernel(heads, grads, grads_pair, own, near, moving_sum, staying_sum):
    slots = grads.shape[0] // 4
    shard = lax.axis_index("seq")
    meets = meets_pair(shard)
    for level in range(4):

        @pl.when(shard // 2 == level)
        def _():
            for at in range(2):
                part = pl.ds(2 * slots * at, 2 * slots)
                moving = grads[part, :] + jnp.where(meets, grads_pair[part, :], 0.0)
                staying = own[part, :]
                if at != (1, 0, 1, 0)[level]:
                    if level in (1, 2):
                        moving = moving + near[...].astype(F32)
                    else:
                        staying = staying + near[...].astype(F32)
                moving_sum[part, :] = moving
                staying_sum[part, :] = staying


def four_join_kernel(
    heads, positions, logit, dots, dots_far, moving_sum, staying_sum, grads_guest, own_near,
    other, middle, skip, cross, query_grad, key_grad, value_grad, router
):
    slots, half = moving_sum.shape[0] // 4, moving_sum.shape[1]
    shard = lax.axis_index("seq")
    router[...] = router_part(positions, logit, dots[...] + dots_far[...], slots, shard)
    for level in range(4):
        inner = level in (1, 2)

        @pl.when(shard // 2 == level)
        def _():
            if level < 2:
                moving, staying = [query_grad], [key_grad, value_grad]
            else:
                moving, staying = [key_grad, value_grad], [query_grad]
            for at in range(2):
                cols = pl.ds(at * half, half)
                met = at == (1, 0, 1, 0)[level]
                plus = [grads_guest] if inner and met else []
                if inner:
                    extra = [own_near] if met else [middle]
                else:
                    extra = [own_near, skip] if met else [cross]
                for outs, base, more in ((moving, moving_sum, plus), (staying, staying_sum, extra)):
                    for which, out in enumerate(outs):
                        rows = pl.ds((2 * at + which) * slots, slots)
                        total = base[rows, :]
                        for ref in more:
                            total = total + ref[pl.ds(which * slots, slots), :].astype(F32)
                        if outs is staying:
                            total = total + other[rows, :].astype(F32)
                        out[:, cols] = total.astype(BF16)


def four_levels(prep, shape, positions, logit, slots, heads, width):
    double, block, total = shape(4 * slots + 2 * TILE), shape(2 * slots + TILE), shape(2 * slots, F32)
    totals, totals_low, low = shape(4 * slots, F32), shape(4 * slots), shape(2 * slots)
    own, mine, near_send, far_send, dots = prep(FOUR_PLAN, [double, double, block, block])
    def pairs(levels, flip=0):
        return [(2 * a + c, 2 * b + (c ^ flip)) for a, b in levels for c in range(2)]

    near = lax.ppermute(near_send, "seq", pairs([(0, 1), (1, 0), (2, 3), (3, 2)]))
    cross = lax.ppermute(near, "seq", pairs([(1, 1), (2, 2)], 1))
    other = lax.ppermute(own, "seq", pairs([(i, i) for i in range(4)], 1))
    skip = lax.ppermute(far_send, "seq", pairs([(0, 2), (3, 1)]))
    middle = lax.ppermute(far_send, "seq", pairs([(1, 2), (2, 1)]))
    row = shape(1, F32, slots)
    turn, grads, own_total = call(
        functools.partial(four_home_kernel, heads),
        [row] + [totals] * 2,
        positions, mine, own,
    )
    turn, grads_pair, other_total, own_near, other_near, step_back = call(
        functools.partial(four_pair_kernel, heads),
        [row, totals, totals, total, total, low],
        positions, turn, mine, own, other, near,
    )
    dots_near = lax.ppermute(dots, "tp", [(i, i ^ 1) for i in range(4)])
    dots, near_low, grads_guest, skip_part, middle_part = call(
        functools.partial(four_near_kernel, heads),
        [row, low, total, total, total],
        positions, turn, dots, dots_near, mine, near, skip, middle, step_back,
    )
    near = lax.ppermute(near_low, "seq", pairs([(0, 1), (1, 0), (2, 3), (3, 2)]))
    dots, grads_guest, skip_back, cross_low, middle_back, other_low, own_near = call(
        functools.partial(four_last_kernel, heads),
        [row, total, low, low, low, totals_low, total],
        positions, dots, mine, own, other, cross, skip, middle,
        grads_guest, skip_part, middle_part, other_total, own_near, other_near,
        scratch=[pltpu.VMEM(total.shape, F32)] * 3,
    )
    dots_far = lax.ppermute(dots, "tp", [(i, i ^ 2) for i in range(4)])
    skip = lax.ppermute(skip_back, "seq", pairs([(2, 0), (1, 3)]))
    cross = lax.ppermute(cross_low, "seq", pairs([(1, 0), (2, 3)], 1))
    middle = lax.ppermute(middle_back, "seq", pairs([(1, 2), (2, 1)]))
    other = lax.ppermute(other_low, "seq", pairs([(i, i) for i in range(4)], 1))
    moving_sum, staying_sum = call(
        functools.partial(four_sum_kernel, heads),
        [totals] * 2,
        grads, grads_pair, own_total, near,
        flops=SUM_FLOPS,
    )
    return call(
        functools.partial(four_join_kernel, heads),
        [shape(slots, BF16, width)] * 3 + [row],
        positions, logit, dots, dots_far, moving_sum, staying_sum, grads_guest, own_near,
        other, middle, skip, cross,
    )


def ring_plan(levels):
    sends = [
        lambda level, step=step: [jnp.where(level >= step, 2, 1)] for step in range(1, levels)
    ]
    return (lambda level: [0, 3], lambda level: [2], lambda level: [1], *sends)


def ring_home_kernel(
    heads, positions, logit, dots, down, up, own, other, grads, own_total, other_total, router
):
    slots = grads.shape[0] // 3
    rows = 2 * slots + TILE
    shard = lax.axis_index("seq")
    for goes_down, mine, at, base, stay_base in ((True, down, 0, 0, 0), (False, up, rows, 1, 2)):
        meet(
            goes_down, [(mine, 0, shard)], [(own, at, shard), (other, at, shard ^ 1)],
            positions, heads, causal(goes_down, slots, shard),
            Store(slots, [(grads, base * slots)], True),
            Store(slots, [(own_total, stay_base * slots), (other_total, stay_base * slots)], True),
        )
    router[...] = router_part(positions, logit, dots[...], slots, shard)


def ring_away_kernel(
    step, levels, heads, positions, own, other, block, own_in, other_in,
    back, own_total, other_total, *low
):
    slots = own_in.shape[0] // 3
    own_total[...] = own_in[...]
    other_total[...] = other_in[...]
    rows = 2 * slots + TILE
    shard = lax.axis_index("seq")
    for goes_down, at, base in ((True, 0, 0), (False, rows, 2 * slots)):

        @pl.when((shard // 2 + step < levels) == goes_down)
        def _():
            meet(
                goes_down, [(block, 0, shard + 2 * (step - levels))],
                [(own, at, shard), (other, at, shard ^ 1)],
                positions, heads, None,
                Store(slots, [(back, 0)], True),
                Store(slots, [(own_total, base), (other_total, base)], False),
            )

    for ref in low:
        ref[...] = other_total[...].astype(BF16)


def ring_join_kernel(heads, grads, own, other, *refs):
    back, (query_grad, key_grad, value_grad) = refs[:-3], refs[-3:]
    slots, half = grads.shape[0] // 3, grads.shape[1]
    level = lax.axis_index("seq") // 2
    low, high = pl.ds(0, half), pl.ds(half, half)
    parts = [pl.ds(i * slots, slots) for i in range(3)]
    stays = [(own[rows, :] + other[rows, :].astype(F32)).astype(BF16) for rows in parts]
    key_grad[:, low], value_grad[:, low], query_grad[:, high] = stays
    query_sum, key_sum, value_sum = [grads[rows, :] for rows in parts]
    for step, ref in enumerate(back, 1):
        went_down = level >= step
        first, second = ref[parts[0], :].astype(F32), ref[parts[1], :].astype(F32)
        query_sum = query_sum + jnp.where(went_down, first, 0.0)
        key_sum = key_sum + jnp.where(went_down, 0.0, first)
        value_sum = value_sum + jnp.where(went_down, 0.0, second)
    query_grad[:, low] = query_sum.astype(BF16)
    key_grad[:, high] = key_sum.astype(BF16)
    value_grad[:, high] = value_sum.astype(BF16)


def ring_levels(prep, shape, positions, logit, slots, heads, width, shards):
    levels = shards // 2
    block, total = shape(2 * slots + TILE), shape(3 * slots, F32)
    own, down, up, *sends, dots = prep(
        ring_plan(levels), [shape(4 * slots + 2 * TILE)] + [block] * (levels + 1)
    )
    pair = [(s, s ^ 1) for s in range(shards)]
    arrived = [
        lax.ppermute(send, "seq", [(s, (s - 2 * step) % shards) for s in range(shards)])
        for step, send in enumerate(sends, 1)
    ]
    other = lax.ppermute(own, "seq", pair)
    dots = sum_over(dots, "tp")
    grads, own_total, other_total, router = call(
        functools.partial(ring_home_kernel, heads),
        [total] * 3 + [shape(1, F32, slots)],
        positions, logit, dots, down, up, own, other,
    )
    backs, low = [], [other_total.astype(BF16)]
    for step, arrival in enumerate(arrived, 1):
        back, own_total, other_total, *low = call(
            functools.partial(ring_away_kernel, step, levels, heads),
            [shape(2 * slots), total, total] + [shape(3 * slots)] * (step == levels - 1),
            positions, own, other, arrival, own_total, other_total,
            )
        backs.append(
            lax.ppermute(back, "seq", [(s, (s + 2 * step) % shards) for s in range(shards)])
        )
    outs = call(
        functools.partial(ring_join_kernel, heads),
        [shape(slots, BF16, width)] * 3,
        grads, own_total, lax.ppermute(low[0], "seq", pair), *backs,
    )
    return *outs, router


def call(kernel, out_shape, *args, scratch=(), ins=None, outs=None, limit=VMEM, flops=1024, aliases=None):
    ins = ins or [pltpu.VMEM] * len(args)
    outs = outs or [pltpu.VMEM] * len(out_shape)
    return pl.pallas_call(
        kernel,
        out_shape=out_shape,
        in_specs=[pl.BlockSpec(memory_space=space) for space in ins],
        out_specs=[pl.BlockSpec(memory_space=space) for space in outs],
        scratch_shapes=list(scratch),
        input_output_aliases=aliases or {},
        compiler_params=pltpu.CompilerParams(vmem_limit_bytes=limit),
        cost_estimate=pl.CostEstimate(flops=flops, bytes_accessed=1024, transcendentals=0),
    )(*args)


def sum_over(values, axis):
    size = lax.axis_size(axis)
    if size & (size - 1):
        return lax.psum(values, axis)
    reach = 1
    while reach < size:
        pairs = [(i, i ^ reach) for i in range(size)]
        values = values + lax.ppermute(values, axis, pairs)
        reach *= 2
    return values


def body(
    query_proj, key_proj, value_proj, attn_output, out_grad, log_norm, router_logit, keep_positions
):
    slots, width = query_proj.shape
    heads = log_norm.shape[1]
    half = width // 2
    shards = lax.axis_size("seq")
    logit = router_logit.reshape(1, slots)
    positions = keep_positions.reshape(-1, LANES)

    def shape(rows, dtype=BF16, columns=half):
        return jax.ShapeDtypeStruct((rows, columns), dtype)

    sources = (
        attn_output, out_grad, logit, log_norm.T, positions, query_proj, key_proj, value_proj
    )

    def prep(plan, shapes):
        dots, *outs = call(
            functools.partial(prep_kernel, plan, heads),
            [shape(1, F32, slots)] + shapes,
            *sources,
            scratch=[pltpu.VMEM(a.shape, a.dtype) for a in sources[:5]]
            + [pltpu.VMEM((4 * (2 * slots + TILE), half), BF16)]
            + [pltpu.SemaphoreType.DMA((11,)), pltpu.SemaphoreType.DMA((2 * len(plan),))],
            ins=[pltpu.HBM] * len(sources),
            outs=[pltpu.VMEM] + [pltpu.HBM] * len(shapes),
            limit=PREP_VMEM,
        )
        return *outs, dots

    if shards == 8 and lax.axis_size("tp") == 4:
        query_grad, key_grad, value_grad, router = four_levels(
            prep, shape, positions, logit, slots, heads, width
        )
    else:
        query_grad, key_grad, value_grad, router = ring_levels(
            prep, shape, positions, logit, slots, heads, width, shards
        )
    return query_grad, key_grad, value_grad, router.reshape(slots)


def solution(mesh):
    wide = P("seq", "tp")
    return jax.shard_map(
        body,
        mesh=mesh,
        in_specs=(wide,) * 6 + (P("seq"), P()),
        out_specs=(wide, wide, wide, P("seq")),
        check_vma=False,
    )
```

```python
import functools
import math

import jax
import jax.numpy as jnp
from jax import lax
from jax.experimental import pallas as pl
from jax.experimental.pallas import tpu as pltpu
from jax.sharding import PartitionSpec as P


LANES = 128
PIECE = 8
GROUP = 4
ONE = 6 * GROUP
PACK = 4
TILE = 16
BIG = 1e30
VMEM = 24 * 1024 * 1024
SUM_FLOPS = 5_000_000_000
PREP_VMEM = 63 * 1024 * 1024
F32 = jnp.float32
BF16 = jnp.bfloat16
NT = (((1,), (1,)), ((), ()))
NN = (((1,), (0,)), ((), ()))
TN = (((0,), (0,)), ((), ()))


def dot(left, right, dims):
    return lax.dot_general(left, right, dims, preferred_element_type=F32)


def pieces(rows):
    high = rows.astype(BF16).astype(F32)
    rest = rows - high
    middle = rest.astype(BF16).astype(F32)
    return [high, middle, rest - middle]


def split_exact(product):
    high = product.astype(BF16)
    return high, (product - high.astype(F32)).astype(BF16)


def used_slots(positions, shard, slots):
    table = positions[...]
    place = lax.broadcasted_iota(jnp.int32, table.shape, 0) * LANES
    place = place + lax.broadcasted_iota(jnp.int32, table.shape, 1)
    mine = (place >= shard * slots) & (place < (shard + 1) * slots) & (table >= 0)
    count = jnp.sum(jnp.where(mine, 1.0, 0.0), axis=1, keepdims=True)
    return jnp.sum(count, axis=0, keepdims=True)


def pack(ext):
    quarter = ext.shape[0] // PACK
    total = ext[:quarter]
    for part in range(1, PACK):
        rows = ext[part * quarter:(part + 1) * quarter]
        total = total + pltpu.roll(rows, part * LANES // PACK, 1)
    groups = [total[at:at + TILE] for at in range(0, quarter, TILE)]
    return jnp.concatenate(groups, axis=1).astype(BF16)


def unpack(packed):
    wide = packed.astype(F32)
    groups = [wide[:, at:at + LANES] for at in range(0, wide.shape[1], LANES)]
    total = jnp.concatenate(groups, axis=0)
    parts = [total]
    for part in range(1, PACK):
        parts.append(pltpu.roll(total, LANES - part * LANES // PACK, 1))
    return jnp.concatenate(parts, axis=0).astype(BF16)


def key_ext(positions, shard, slots):
    count = used_slots(positions, shard, slots)
    slot = lax.broadcasted_iota(jnp.int32, (slots, LANES), 0).astype(F32)
    lane = lax.broadcasted_iota(jnp.int32, (slots, LANES), 1)
    return jnp.where((lane == ONE) & (slot >= count), -BIG, 0.0).astype(BF16)


def prep_kernel(plan, heads, *refs):
    sources, (query, key, value), rest = refs[:5], refs[5:8], refs[8:]
    dots, outs, rest = rest[0], rest[1:len(plan) + 1], rest[len(plan) + 1:]
    held, (bank, sems, done) = rest[:5], rest[5:]
    output, grad, logit, norm, positions = held
    slots, width = grad.shape
    half = width // 2
    rows = 2 * slots + TILE
    copies = [
        pltpu.make_async_copy(source, dest, sems.at[i])
        for i, (source, dest) in enumerate(zip(sources, held))
    ]
    for at in range(2):
        for source, base in ((key, at), (value, at + 0.5), (query, at + 2)):
            first = int(base) * rows + (slots if base % 1 else 0)
            copies.append(
                pltpu.make_async_copy(
                    source.at[:, pl.ds(at * half, half)],
                    bank.at[pl.ds(first, slots), :],
                    sems.at[len(copies)],
                )
            )
    for copy in copies:
        copy.start()
    for copy in copies[5:]:
        copy.wait()
    for at in range(2):
        bank[pl.ds(at * rows + 2 * slots, TILE), :] = jnp.zeros((TILE, half), BF16)
    level = lax.axis_index("seq") // 2
    moves = []
    for out, blocks in zip(outs, plan):
        for place, block in enumerate(blocks(level)):
            block = jnp.int32(block)
            move = pltpu.make_async_copy(
                bank.at[pl.ds(pl.multiple_of(block * rows, TILE), rows), :],
                out.at[pl.ds(place * rows, rows), :],
                done.at[len(moves)],
            )
            moves.append((block, move))

    def each(some, early):
        for block, move in some:

            @pl.when((block < 2) == early)
            def _():
                move.start()

    each(moves, True)
    for copy in copies[:5]:
        copy.wait()
    head_dim = width // heads
    root = math.sqrt(head_dim)
    shard = lax.axis_index("seq")
    count = used_slots(positions, shard, slots)
    lane = lax.broadcasted_iota(jnp.int32, (PIECE, slots), 1).astype(F32)
    used = lane < count
    gate_row = jax.nn.sigmoid(logit[...])
    gate = jnp.transpose(jnp.broadcast_to(gate_row, (LANES, slots)))
    head_of = lax.broadcasted_iota(jnp.int32, (PIECE, width), 1) // head_dim
    head_row = lax.broadcasted_iota(jnp.int32, (PIECE, width), 0)
    pick = (head_of == head_row).astype(BF16)
    ones = jnp.ones((PIECE, width), BF16)
    dout_parts, delta_parts, dot_parts = [], [], []
    for h in range(heads):
        cols = pl.ds(h * head_dim, head_dim)
        wide = grad[:, cols].astype(F32)
        out = output[:, cols].astype(F32)
        dout = (wide * gate).astype(BF16)
        dout_parts.append(dout)
        delta_parts.append(dout.astype(F32) * out)
        dot_parts.append(wide * out)
    delta_high, delta_low = split_exact(jnp.concatenate(delta_parts, axis=1))
    delta = dot(pick, delta_high, NT) + dot(pick, delta_low, NT)
    dot_high, dot_low = split_exact(jnp.concatenate(dot_parts, axis=1))
    dots[...] = (dot(ones, dot_high, NT) + dot(ones, dot_low, NT))[:1]

    pad = jnp.zeros((PIECE - heads, slots), F32)
    scaled = jnp.where(used, jnp.concatenate([norm[...] * root, pad], axis=0), BIG)
    delta = jnp.where(used, delta, 0.0)
    first = lax.broadcasted_iota(jnp.int32, (PIECE, slots), 0) == 0
    stack = pieces(scaled) + pieces(delta) + [jnp.where(first, 1.0, 0.0)]
    stack.append(jnp.zeros((PIECE * (PIECE - len(stack)), slots), F32))
    stats = jnp.concatenate(stack, axis=0).astype(BF16)
    source = lax.broadcasted_iota(jnp.int32, (PIECE * PIECE, LANES), 0)
    target = lax.broadcasted_iota(jnp.int32, (PIECE * PIECE, LANES), 1)
    piece, head = source // PIECE, source % PIECE

    def ext(first_head):
        local = head - first_head
        taken = (local >= 0) & (local < heads // 2) & (piece < 6)
        column = jnp.where(taken, piece * GROUP + local, -1)
        column = jnp.where(source == 6 * PIECE, ONE, column)
        return dot(stats, (column == target).astype(BF16), TN)

    per = heads // 2
    for at in range(2):
        base = (2 + at) * rows
        bank[pl.ds(base + slots, slots), :] = jnp.concatenate(
            dout_parts[at * per:(at + 1) * per], axis=1
        )
        bank[pl.ds(base + 2 * slots, TILE), :] = pack(ext(at * per))
    each(moves, False)
    for _, move in moves:
        move.wait()


def head_marks(head, is_value):
    lane = lax.broadcasted_iota(jnp.int32, (1, LANES), 1)
    base = (3 * GROUP if is_value else 0) + head
    marked = (lane == base) | (lane == base + GROUP) | (lane == base + 2 * GROUP)
    return jnp.where(marked, -1.0, 0.0).astype(BF16)


def meet(down, movings, stays, positions, heads, mask, emit, add):
    half = movings[0][0].shape[1]
    slots = emit.slots
    head_dim = half // (heads // 2)
    scale = head_dim ** -0.5
    to_log2 = scale * math.log2(math.e)

    def stats(blocks, queries):
        parts = []
        for ref, at, shard in blocks:
            if queries:
                parts.append(unpack(ref[pl.ds(at + 2 * slots, TILE), :]))
            else:
                parts.append(key_ext(positions, shard, slots))
        return jnp.concatenate(parts, axis=0)

    def load(blocks, which, cols):
        parts = [ref[pl.ds(at + which * slots, slots), cols] for ref, at, _ in blocks]
        return jnp.concatenate(parts, axis=0)

    moving_ext, stay_ext = stats(movings, down), stats(stays, not down)
    for h in range(heads // 2):
        cols = pl.ds(h * head_dim, head_dim)
        m1, m2 = load(movings, 0, cols), load(movings, 1, cols)
        r1, r2 = load(stays, 0, cols), load(stays, 1, cols)
        key_mark, value_mark = head_marks(h, False), head_marks(h, True)
        if down:
            m1_ext, m2_ext = moving_ext, moving_ext
            r1_ext = stay_ext + key_mark
            r2_ext = jnp.broadcast_to(value_mark, stay_ext.shape)
        else:
            m1_ext = moving_ext + key_mark
            m2_ext = jnp.broadcast_to(value_mark, moving_ext.shape)
            r1_ext, r2_ext = stay_ext, stay_ext
        scores = dot(
            jnp.concatenate([m1, m1_ext], axis=1), jnp.concatenate([r1, r1_ext], axis=1), NT
        )
        if mask is not None:
            scores = jnp.where(mask, scores, -BIG)
        prob = jnp.exp2(scores * to_log2)
        dprob = dot(
            jnp.concatenate([m2, m2_ext], axis=1), jnp.concatenate([r2, r2_ext], axis=1), NT
        )
        dscore = (prob * dprob * scale).astype(BF16)
        prob = prob.astype(BF16)
        emit(0, cols, dot(dscore, r1, NN))
        add(0, cols, dot(dscore, m1, TN))
        if down:
            add(1, cols, dot(prob, m2, TN))
        else:
            emit(1, cols, dot(prob, r2, NN))


class Store:
    def __init__(self, slots, targets, fresh, olds=None):
        self.slots, self.targets, self.fresh = slots, targets, fresh
        self.olds = olds or [ref for ref, _ in targets]

    def __call__(self, which, cols, term):
        for i, (ref, base) in enumerate(self.targets):
            rows = pl.ds(base + which * self.slots, self.slots)
            part = term[i * self.slots:(i + 1) * self.slots]
            part = part if self.fresh else self.olds[i][rows, cols] + part
            ref[rows, cols] = part.astype(ref.dtype)


def causal(down, slots, shard=None):
    shape = (slots, slots if shard is None else 2 * slots)
    row = lax.broadcasted_iota(jnp.int32, shape, 0)
    place = lax.broadcasted_iota(jnp.int32, shape, 1)
    if shard is not None:
        place = jnp.where(place < slots, place, slots - shard % 2 * (slots + 1))
    return place <= row if down else place >= row


def router_part(positions, logit, dots, slots, shard):
    gate = jax.nn.sigmoid(logit[...])
    lane = lax.broadcasted_iota(jnp.int32, (1, slots), 1).astype(F32)
    used = lane < used_slots(positions, shard, slots)
    return jnp.where(used, gate * (1.0 - gate) * dots, 0.0)


FOUR_PLAN = (
    lambda level: [jnp.where(level < 2, 0, 2), jnp.where(level < 2, 1, 3)],
    lambda level: [jnp.where(level < 2, 2, 0), jnp.where(level < 2, 3, 1)],
    lambda level: [jnp.where(level % 2 == 0, 0, 3)],
    lambda level: [jnp.where(level < 2, 1, 2)],
)


def four_home_kernel(heads, positions, mine, own, turn, grads, own_total):
    slots = grads.shape[0] // 4
    rows = 2 * slots + TILE
    shard = lax.axis_index("seq")
    turn[...] = jnp.zeros(turn.shape, F32)
    for down in (True, False):

        @pl.when((shard < 4) == down)
        def _():
            for at in range(2):
                base = 2 * slots * at
                meet(
                    down, [(mine, at * rows, shard)], [(own, at * rows, shard)],
                    positions, heads, causal(down, slots),
                    Store(slots, [(grads, base)], True),
                    Store(slots, [(own_total, base)], True),
                )


def meets_pair(shard):
    return (shard % 2 == 1) == (shard < 4)


def follow_kernel(block, after, out):
    pass


def four_pair_kernel(
    heads, positions, after, mine, other, turn, grads_pair, met_total, early, early_total
):
    slots = early.shape[0] // 2
    rows = 2 * slots + TILE
    shard = lax.axis_index("seq")
    meets = meets_pair(shard)
    turn[...] = after[...]
    for level in range(4):

        @pl.when(meets & (shard // 2 == level))
        def _():
            for at in range(2):
                met = at == (1, 0, 1, 0)[level]
                meet(
                    level < 2, [(mine, at * rows, shard)], [(other, at * rows, shard ^ 1)],
                    positions, heads, None,
                    Store(slots, [(grads_pair, 2 * slots * at)], True),
                    Store(slots, [(met_total if met else early_total, 0)], True),
                )
            early[...] = early_total[...].astype(BF16)

    @pl.when(jnp.logical_not(meets))
    def _():
        early[...] = jnp.zeros(early.shape, BF16)


def four_skip_kernel(
    heads, positions, after, mine, own, other, near, skip,
    turn, own_near, other_near, back, near_total, grads_guest, skip_part
):
    slots = back.shape[0] // 2
    rows = 2 * slots + TILE
    shard = lax.axis_index("seq")
    turn[...] = after[...]
    for level in range(4):
        at = (1, 0, 1, 0)[level]

        @pl.when(shard // 2 == level)
        def _():
            pair = [(own, at * rows, shard), (other, at * rows, shard ^ 1)]
            totals = Store(slots, [(own_near, 0), (other_near, 0)], True)
            guest = [(near, 0, shard - 2)]
            if level in (0, 3):
                meet(
                    level == 0, guest, pair, positions, heads, None,
                    Store(slots, [(back, 0)], True), totals,
                )
                return
            far = [(skip, 0, shard - 4)]
            meet(
                level == 1, [(mine, at * rows, shard)] + far, guest, positions, heads, None,
                Store(slots, [(grads_guest, 0), (skip_part, 0)], True),
                Store(slots, [(near_total, 0)], True),
            )
            meet(
                level == 1, far, pair, positions, heads, None,
                Store(slots, [(skip_part, 0)], False), totals,
            )


def four_near_kernel(
    heads, positions, after, dots, dots_near, near, middle, back, near_total,
    dots_sum, near_low, middle_part
):
    slots = near_low.shape[0] // 2
    shard = lax.axis_index("seq")
    dots_sum[...] = dots[...] + dots_near[...]
    for level in range(4):

        @pl.when(shard // 2 == level)
        def _():
            if level in (0, 3):
                near_low[...] = back[...]
                return
            meet(
                level == 1, [(middle, 0, shard - 2)], [(near, 0, shard - 2)],
                positions, heads, None,
                Store(slots, [(middle_part, 0)], True),
                Store(slots, [(near_low, 0)], False, [near_total]),
            )


def four_last_kernel(
    heads, positions, dots_in, mine, own, other, cross, skip, middle,
    grads_in, skip_in, middle_in, met_pair, own_in, other_in,
    dots, grads_guest, skip_back, cross_low, middle_back, late, own_near,
    middle_part, other_near,
):
    slots = grads_in.shape[0] // 2
    rows = 2 * slots + TILE
    shard = lax.axis_index("seq")
    meets = meets_pair(shard)
    dots[...] = dots_in[...]
    for level in range(4):
        at = (1, 0, 1, 0)[level]

        @pl.when(shard // 2 == level)
        def _():
            if level in (0, 3):
                own_near[...] = own_in[...]
                other_near[...] = other_in[...]
            else:
                far = [(skip, 0, shard - 4), (middle, 0, shard - 2)]
                meet(
                    level == 1, far[1:], [(own, at * rows, shard), (other, at * rows, shard ^ 1)],
                    positions, heads, None,
                    Store(slots, [(middle_part, 0)], False, [middle_in]),
                    Store(slots, [(own_near, 0), (other_near, 0)], False, [own_in, other_in]),
                )
                meet(
                    level == 1, [(mine, at * rows, shard)] + far, [(cross, 0, (shard - 2) ^ 1)],
                    positions, heads, None,
                    Store(
                        slots, [(grads_guest, 0), (skip_back, 0), (middle_back, 0)], False,
                        [grads_in, skip_in, middle_part],
                    ),
                    Store(slots, [(cross_low, 0)], True),
                )

    late[...] = (other_near[...] + jnp.where(meets, met_pair[...], 0.0)).astype(BF16)


def four_sum_kernel(heads, grads, grads_pair, own, near, early, moving_sum, staying_sum):
    slots = grads.shape[0] // 4
    shard = lax.axis_index("seq")
    meets = meets_pair(shard)
    for level in range(4):

        @pl.when(shard // 2 == level)
        def _():
            for at in range(2):
                part = pl.ds(2 * slots * at, 2 * slots)
                moving = grads[part, :] + jnp.where(meets, grads_pair[part, :], 0.0)
                staying = own[part, :]
                if at != (1, 0, 1, 0)[level]:
                    staying = staying + early[...].astype(F32)
                    if level in (1, 2):
                        moving = moving + near[...].astype(F32)
                    else:
                        staying = staying + near[...].astype(F32)
                moving_sum[part, :] = moving
                staying_sum[part, :] = staying


def four_join_kernel(
    heads, positions, logit, dots, dots_far, moving_sum, staying_sum, grads_guest, own_near,
    late, skip, cross, middle, query_grad, key_grad, value_grad, router
):
    slots, half = moving_sum.shape[0] // 4, moving_sum.shape[1]
    shard = lax.axis_index("seq")
    router[...] = router_part(positions, logit, dots[...] + dots_far[...], slots, shard)
    for level in range(4):
        inner = level in (1, 2)

        @pl.when(shard // 2 == level)
        def _():
            if level < 2:
                moving, staying = [query_grad], [key_grad, value_grad]
            else:
                moving, staying = [key_grad, value_grad], [query_grad]
            for at in range(2):
                cols = pl.ds(at * half, half)
                met = at == (1, 0, 1, 0)[level]
                plus = [grads_guest] if inner and met else []
                if inner:
                    extra = [own_near, late] if met else [middle]
                else:
                    extra = [own_near, skip, late] if met else [cross]
                for outs, base, more in ((moving, moving_sum, plus), (staying, staying_sum, extra)):
                    for which, out in enumerate(outs):
                        rows = pl.ds((2 * at + which) * slots, slots)
                        total = base[rows, :]
                        for ref in more:
                            total = total + ref[pl.ds(which * slots, slots), :].astype(F32)
                        out[:, cols] = total.astype(BF16)


def four_levels(prep, shape, positions, logit, slots, heads, width):
    double, block, total = shape(4 * slots + 2 * TILE), shape(2 * slots + TILE), shape(2 * slots, F32)
    totals, low = shape(4 * slots, F32), shape(2 * slots)
    own, mine, near_send, far_send, dots = prep(FOUR_PLAN, [double, double, block, block])
    def pairs(levels, flip=0):
        return [(2 * a + c, 2 * b + (c ^ flip)) for a, b in levels for c in range(2)]

    near = lax.ppermute(near_send, "seq", pairs([(0, 1), (1, 0), (2, 3), (3, 2)]))
    other = lax.ppermute(own, "seq", pairs([(i, i) for i in range(4)], 1))
    skip = lax.ppermute(far_send, "seq", pairs([(0, 2), (3, 1)]))
    middle = lax.ppermute(far_send, "seq", pairs([(1, 2), (2, 1)]))
    row = shape(1, F32, slots)
    turn, grads, own_total = call(
        functools.partial(four_home_kernel, heads),
        [row] + [totals] * 2,
        positions, mine, own,
    )
    (near,) = call(
        follow_kernel, [block], near, turn, ins=[pl.ANY, pltpu.VMEM], outs=[pl.ANY], aliases={0: 0}
    )
    cross = lax.ppermute(near, "seq", pairs([(1, 1), (2, 2)], 1))
    turn, grads_pair, met_pair, early = call(
        functools.partial(four_pair_kernel, heads),
        [row, totals, total, low],
        positions, turn, mine, other,
        scratch=[pltpu.VMEM(total.shape, F32)],
    )
    early = lax.ppermute(early, "seq", pairs([(i, i) for i in range(4)], 1))
    turn, own_near, other_near, step_back, near_total, grads_guest, skip_part = call(
        functools.partial(four_skip_kernel, heads),
        [row, total, total, low, total, total, total],
        positions, turn, mine, own, other, near, skip,
    )
    dots_near = lax.ppermute(dots, "tp", [(i, i ^ 1) for i in range(4)])
    dots, near_low, middle_part = call(
        functools.partial(four_near_kernel, heads),
        [row, low, total],
        positions, turn, dots, dots_near, near, middle, step_back, near_total,
    )
    near = lax.ppermute(near_low, "seq", pairs([(0, 1), (1, 0), (2, 3), (3, 2)]))
    dots, grads_guest, skip_back, cross_low, middle_back, late, own_near = call(
        functools.partial(four_last_kernel, heads),
        [row, total, low, low, low, low, total],
        positions, dots, mine, own, other, cross, skip, middle,
        grads_guest, skip_part, middle_part, met_pair, own_near, other_near,
        scratch=[pltpu.VMEM(total.shape, F32)] * 2,
    )
    dots_far = lax.ppermute(dots, "tp", [(i, i ^ 2) for i in range(4)])
    skip = lax.ppermute(skip_back, "seq", pairs([(2, 0), (1, 3)]))
    cross = lax.ppermute(cross_low, "seq", pairs([(1, 0), (2, 3)], 1))
    middle = lax.ppermute(middle_back, "seq", pairs([(1, 2), (2, 1)]))
    late = lax.ppermute(late, "seq", pairs([(i, i) for i in range(4)], 1))
    moving_sum, staying_sum = call(
        functools.partial(four_sum_kernel, heads),
        [totals] * 2,
        grads, grads_pair, own_total, near, early,
        flops=SUM_FLOPS,
    )
    return call(
        functools.partial(four_join_kernel, heads),
        [shape(slots, BF16, width)] * 3 + [row],
        positions, logit, dots, dots_far, moving_sum, staying_sum, grads_guest, own_near,
        late, skip, cross, middle,
    )


def ring_plan(levels):
    sends = [
        lambda level, step=step: [jnp.where(level >= step, 2, 1)] for step in range(1, levels)
    ]
    return (lambda level: [0, 3], lambda level: [2], lambda level: [1], *sends)


def ring_home_kernel(
    heads, positions, logit, dots, down, up, own, other, grads, own_total, other_total, router
):
    slots = grads.shape[0] // 3
    rows = 2 * slots + TILE
    shard = lax.axis_index("seq")
    for goes_down, mine, at, base, stay_base in ((True, down, 0, 0, 0), (False, up, rows, 1, 2)):
        meet(
            goes_down, [(mine, 0, shard)], [(own, at, shard), (other, at, shard ^ 1)],
            positions, heads, causal(goes_down, slots, shard),
            Store(slots, [(grads, base * slots)], True),
            Store(slots, [(own_total, stay_base * slots), (other_total, stay_base * slots)], True),
        )
    router[...] = router_part(positions, logit, dots[...], slots, shard)


def ring_away_kernel(
    step, levels, heads, positions, own, other, block, own_in, other_in,
    back, own_total, other_total, *low
):
    slots = own_in.shape[0] // 3
    own_total[...] = own_in[...]
    other_total[...] = other_in[...]
    rows = 2 * slots + TILE
    shard = lax.axis_index("seq")
    for goes_down, at, base in ((True, 0, 0), (False, rows, 2 * slots)):

        @pl.when((shard // 2 + step < levels) == goes_down)
        def _():
            meet(
                goes_down, [(block, 0, shard + 2 * (step - levels))],
                [(own, at, shard), (other, at, shard ^ 1)],
                positions, heads, None,
                Store(slots, [(back, 0)], True),
                Store(slots, [(own_total, base), (other_total, base)], False),
            )

    for ref in low:
        ref[...] = other_total[...].astype(BF16)


def ring_join_kernel(heads, grads, own, other, *refs):
    back, (query_grad, key_grad, value_grad) = refs[:-3], refs[-3:]
    slots, half = grads.shape[0] // 3, grads.shape[1]
    level = lax.axis_index("seq") // 2
    low, high = pl.ds(0, half), pl.ds(half, half)
    parts = [pl.ds(i * slots, slots) for i in range(3)]
    stays = [(own[rows, :] + other[rows, :].astype(F32)).astype(BF16) for rows in parts]
    key_grad[:, low], value_grad[:, low], query_grad[:, high] = stays
    query_sum, key_sum, value_sum = [grads[rows, :] for rows in parts]
    for step, ref in enumerate(back, 1):
        went_down = level >= step
        first, second = ref[parts[0], :].astype(F32), ref[parts[1], :].astype(F32)
        query_sum = query_sum + jnp.where(went_down, first, 0.0)
        key_sum = key_sum + jnp.where(went_down, 0.0, first)
        value_sum = value_sum + jnp.where(went_down, 0.0, second)
    query_grad[:, low] = query_sum.astype(BF16)
    key_grad[:, high] = key_sum.astype(BF16)
    value_grad[:, high] = value_sum.astype(BF16)


def ring_levels(prep, shape, positions, logit, slots, heads, width, shards):
    levels = shards // 2
    block, total = shape(2 * slots + TILE), shape(3 * slots, F32)
    own, down, up, *sends, dots = prep(
        ring_plan(levels), [shape(4 * slots + 2 * TILE)] + [block] * (levels + 1)
    )
    pair = [(s, s ^ 1) for s in range(shards)]
    arrived = [
        lax.ppermute(send, "seq", [(s, (s - 2 * step) % shards) for s in range(shards)])
        for step, send in enumerate(sends, 1)
    ]
    other = lax.ppermute(own, "seq", pair)
    dots = sum_over(dots, "tp")
    grads, own_total, other_total, router = call(
        functools.partial(ring_home_kernel, heads),
        [total] * 3 + [shape(1, F32, slots)],
        positions, logit, dots, down, up, own, other,
    )
    backs, low = [], [other_total.astype(BF16)]
    for step, arrival in enumerate(arrived, 1):
        back, own_total, other_total, *low = call(
            functools.partial(ring_away_kernel, step, levels, heads),
            [shape(2 * slots), total, total] + [shape(3 * slots)] * (step == levels - 1),
            positions, own, other, arrival, own_total, other_total,
            )
        backs.append(
            lax.ppermute(back, "seq", [(s, (s + 2 * step) % shards) for s in range(shards)])
        )
    outs = call(
        functools.partial(ring_join_kernel, heads),
        [shape(slots, BF16, width)] * 3,
        grads, own_total, lax.ppermute(low[0], "seq", pair), *backs,
    )
    return *outs, router


def call(kernel, out_shape, *args, scratch=(), ins=None, outs=None, limit=VMEM, flops=1024, aliases=None):
    ins = ins or [pltpu.VMEM] * len(args)
    outs = outs or [pltpu.VMEM] * len(out_shape)
    return pl.pallas_call(
        kernel,
        out_shape=out_shape,
        in_specs=[pl.BlockSpec(memory_space=space) for space in ins],
        out_specs=[pl.BlockSpec(memory_space=space) for space in outs],
        scratch_shapes=list(scratch),
        input_output_aliases=aliases or {},
        compiler_params=pltpu.CompilerParams(vmem_limit_bytes=limit),
        cost_estimate=pl.CostEstimate(flops=flops, bytes_accessed=1024, transcendentals=0),
    )(*args)


def sum_over(values, axis):
    size = lax.axis_size(axis)
    if size & (size - 1):
        return lax.psum(values, axis)
    reach = 1
    while reach < size:
        pairs = [(i, i ^ reach) for i in range(size)]
        values = values + lax.ppermute(values, axis, pairs)
        reach *= 2
    return values


def body(
    query_proj, key_proj, value_proj, attn_output, out_grad, log_norm, router_logit, keep_positions
):
    slots, width = query_proj.shape
    heads = log_norm.shape[1]
    half = width // 2
    shards = lax.axis_size("seq")
    logit = router_logit.reshape(1, slots)
    positions = keep_positions.reshape(-1, LANES)

    def shape(rows, dtype=BF16, columns=half):
        return jax.ShapeDtypeStruct((rows, columns), dtype)

    sources = (
        attn_output, out_grad, logit, log_norm.T, positions, query_proj, key_proj, value_proj
    )

    def prep(plan, shapes):
        dots, *outs = call(
            functools.partial(prep_kernel, plan, heads),
            [shape(1, F32, slots)] + shapes,
            *sources,
            scratch=[pltpu.VMEM(a.shape, a.dtype) for a in sources[:5]]
            + [pltpu.VMEM((4 * (2 * slots + TILE), half), BF16)]
            + [pltpu.SemaphoreType.DMA((11,)), pltpu.SemaphoreType.DMA((2 * len(plan),))],
            ins=[pltpu.HBM] * len(sources),
            outs=[pltpu.VMEM] + [pltpu.HBM] * len(shapes),
            limit=PREP_VMEM,
        )
        return *outs, dots

    if shards == 8 and lax.axis_size("tp") == 4:
        query_grad, key_grad, value_grad, router = four_levels(
            prep, shape, positions, logit, slots, heads, width
        )
    else:
        query_grad, key_grad, value_grad, router = ring_levels(
            prep, shape, positions, logit, slots, heads, width, shards
        )
    return query_grad, key_grad, value_grad, router.reshape(slots)


def solution(mesh):
    wide = P("seq", "tp")
    return jax.shard_map(
        body,
        mesh=mesh,
        in_specs=(wide,) * 6 + (P("seq"), P()),
        out_specs=(wide, wide, wide, P("seq")),
        check_vma=False,
    )
```

```python
import functools
import math

import jax
import jax.numpy as jnp
from jax import lax
from jax.experimental import pallas as pl
from jax.experimental.pallas import tpu as pltpu
from jax.sharding import PartitionSpec as P


LANES = 128
PIECE = 8
GROUP = 4
ONE = 6 * GROUP
PACK = 4
TILE = 16
BIG = 1e30
VMEM = 24 * 1024 * 1024
SUM_FLOPS = 5_000_000_000
PREP_VMEM = 63 * 1024 * 1024
F32 = jnp.float32
BF16 = jnp.bfloat16
NT = (((1,), (1,)), ((), ()))
NN = (((1,), (0,)), ((), ()))
TN = (((0,), (0,)), ((), ()))


def dot(left, right, dims):
    return lax.dot_general(left, right, dims, preferred_element_type=F32)


def pieces(rows):
    high = rows.astype(BF16).astype(F32)
    rest = rows - high
    middle = rest.astype(BF16).astype(F32)
    return [high, middle, rest - middle]


def split_exact(product):
    high = product.astype(BF16)
    return high, (product - high.astype(F32)).astype(BF16)


def used_slots(positions, shard, slots):
    table = positions[...]
    place = lax.broadcasted_iota(jnp.int32, table.shape, 0) * LANES
    place = place + lax.broadcasted_iota(jnp.int32, table.shape, 1)
    mine = (place >= shard * slots) & (place < (shard + 1) * slots) & (table >= 0)
    count = jnp.sum(jnp.where(mine, 1.0, 0.0), axis=1, keepdims=True)
    return jnp.sum(count, axis=0, keepdims=True)


def pack(ext):
    quarter = ext.shape[0] // PACK
    total = ext[:quarter]
    for part in range(1, PACK):
        rows = ext[part * quarter:(part + 1) * quarter]
        total = total + pltpu.roll(rows, part * LANES // PACK, 1)
    groups = [total[at:at + TILE] for at in range(0, quarter, TILE)]
    return jnp.concatenate(groups, axis=1).astype(BF16)


def unpack(packed):
    wide = packed.astype(F32)
    groups = [wide[:, at:at + LANES] for at in range(0, wide.shape[1], LANES)]
    total = jnp.concatenate(groups, axis=0)
    parts = [total]
    for part in range(1, PACK):
        parts.append(pltpu.roll(total, LANES - part * LANES // PACK, 1))
    return jnp.concatenate(parts, axis=0).astype(BF16)


def key_ext(positions, shard, slots):
    count = used_slots(positions, shard, slots)
    slot = lax.broadcasted_iota(jnp.int32, (slots, LANES), 0).astype(F32)
    lane = lax.broadcasted_iota(jnp.int32, (slots, LANES), 1)
    return jnp.where((lane == ONE) & (slot >= count), -BIG, 0.0).astype(BF16)


def prep_kernel(plan, heads, *refs):
    sources, (query, key, value), rest = refs[:5], refs[5:8], refs[8:]
    dots, outs, rest = rest[0], rest[1:len(plan) + 1], rest[len(plan) + 1:]
    held, (bank, sems, done) = rest[:5], rest[5:]
    output, grad, logit, norm, positions = held
    slots, width = grad.shape
    half = width // 2
    rows = 2 * slots + TILE
    copies = [
        pltpu.make_async_copy(source, dest, sems.at[i])
        for i, (source, dest) in enumerate(zip(sources, held))
    ]
    for at in range(2):
        for source, base in ((key, at), (value, at + 0.5), (query, at + 2)):
            first = int(base) * rows + (slots if base % 1 else 0)
            copies.append(
                pltpu.make_async_copy(
                    source.at[:, pl.ds(at * half, half)],
                    bank.at[pl.ds(first, slots), :],
                    sems.at[len(copies)],
                )
            )
    for copy in copies:
        copy.start()
    for copy in copies[5:]:
        copy.wait()
    for at in range(2):
        bank[pl.ds(at * rows + 2 * slots, TILE), :] = jnp.zeros((TILE, half), BF16)
    level = lax.axis_index("seq") // 2
    moves = []
    for out, blocks in zip(outs, plan):
        for place, block in enumerate(blocks(level)):
            block = jnp.int32(block)
            move = pltpu.make_async_copy(
                bank.at[pl.ds(pl.multiple_of(block * rows, TILE), rows), :],
                out.at[pl.ds(place * rows, rows), :],
                done.at[len(moves)],
            )
            moves.append((block, move))

    def each(some, early):
        for block, move in some:

            @pl.when((block < 2) == early)
            def _():
                move.start()

    each(moves, True)
    for copy in copies[:5]:
        copy.wait()
    head_dim = width // heads
    root = math.sqrt(head_dim)
    shard = lax.axis_index("seq")
    count = used_slots(positions, shard, slots)
    lane = lax.broadcasted_iota(jnp.int32, (PIECE, slots), 1).astype(F32)
    used = lane < count
    gate_row = jax.nn.sigmoid(logit[...])
    gate = jnp.transpose(jnp.broadcast_to(gate_row, (LANES, slots)))
    head_of = lax.broadcasted_iota(jnp.int32, (PIECE, width), 1) // head_dim
    head_row = lax.broadcasted_iota(jnp.int32, (PIECE, width), 0)
    pick = (head_of == head_row).astype(BF16)
    ones = jnp.ones((PIECE, width), BF16)
    dout_parts, delta_parts, dot_parts = [], [], []
    for h in range(heads):
        cols = pl.ds(h * head_dim, head_dim)
        wide = grad[:, cols].astype(F32)
        out = output[:, cols].astype(F32)
        dout = (wide * gate).astype(BF16)
        dout_parts.append(dout)
        delta_parts.append(dout.astype(F32) * out)
        dot_parts.append(wide * out)
    delta_high, delta_low = split_exact(jnp.concatenate(delta_parts, axis=1))
    delta = dot(pick, delta_high, NT) + dot(pick, delta_low, NT)
    dot_high, dot_low = split_exact(jnp.concatenate(dot_parts, axis=1))
    dots[...] = (dot(ones, dot_high, NT) + dot(ones, dot_low, NT))[:1]

    pad = jnp.zeros((PIECE - heads, slots), F32)
    scaled = jnp.where(used, jnp.concatenate([norm[...] * root, pad], axis=0), BIG)
    delta = jnp.where(used, delta, 0.0)
    first = lax.broadcasted_iota(jnp.int32, (PIECE, slots), 0) == 0
    stack = pieces(scaled) + pieces(delta) + [jnp.where(first, 1.0, 0.0)]
    stack.append(jnp.zeros((PIECE * (PIECE - len(stack)), slots), F32))
    stats = jnp.concatenate(stack, axis=0).astype(BF16)
    source = lax.broadcasted_iota(jnp.int32, (PIECE * PIECE, LANES), 0)
    target = lax.broadcasted_iota(jnp.int32, (PIECE * PIECE, LANES), 1)
    piece, head = source // PIECE, source % PIECE

    def ext(first_head):
        local = head - first_head
        taken = (local >= 0) & (local < heads // 2) & (piece < 6)
        column = jnp.where(taken, piece * GROUP + local, -1)
        column = jnp.where(source == 6 * PIECE, ONE, column)
        return dot(stats, (column == target).astype(BF16), TN)

    per = heads // 2
    for at in range(2):
        base = (2 + at) * rows
        bank[pl.ds(base + slots, slots), :] = jnp.concatenate(
            dout_parts[at * per:(at + 1) * per], axis=1
        )
        bank[pl.ds(base + 2 * slots, TILE), :] = pack(ext(at * per))
    each(moves, False)
    for _, move in moves:
        move.wait()


def head_marks(head, is_value):
    lane = lax.broadcasted_iota(jnp.int32, (1, LANES), 1)
    base = (3 * GROUP if is_value else 0) + head
    marked = (lane == base) | (lane == base + GROUP) | (lane == base + 2 * GROUP)
    return jnp.where(marked, -1.0, 0.0).astype(BF16)


def meet(down, movings, stays, positions, heads, mask, emit, add):
    half = movings[0][0].shape[1]
    slots = emit.slots
    head_dim = half // (heads // 2)
    scale = head_dim ** -0.5
    to_log2 = scale * math.log2(math.e)

    def stats(blocks, queries):
        parts = []
        for ref, at, shard in blocks:
            if queries:
                parts.append(unpack(ref[pl.ds(at + 2 * slots, TILE), :]))
            else:
                parts.append(key_ext(positions, shard, slots))
        return jnp.concatenate(parts, axis=0)

    def load(blocks, which, cols):
        parts = [ref[pl.ds(at + which * slots, slots), cols] for ref, at, _ in blocks]
        return jnp.concatenate(parts, axis=0)

    moving_ext, stay_ext = stats(movings, down), stats(stays, not down)
    for h in range(heads // 2):
        cols = pl.ds(h * head_dim, head_dim)
        m1, m2 = load(movings, 0, cols), load(movings, 1, cols)
        r1, r2 = load(stays, 0, cols), load(stays, 1, cols)
        key_mark, value_mark = head_marks(h, False), head_marks(h, True)
        if down:
            m1_ext, m2_ext = moving_ext, moving_ext
            r1_ext = stay_ext + key_mark
            r2_ext = jnp.broadcast_to(value_mark, stay_ext.shape)
        else:
            m1_ext = moving_ext + key_mark
            m2_ext = jnp.broadcast_to(value_mark, moving_ext.shape)
            r1_ext, r2_ext = stay_ext, stay_ext
        scores = dot(
            jnp.concatenate([m1, m1_ext], axis=1), jnp.concatenate([r1, r1_ext], axis=1), NT
        )
        if mask is not None:
            scores = jnp.where(mask, scores, -BIG)
        prob = jnp.exp2(scores * to_log2)
        dprob = dot(
            jnp.concatenate([m2, m2_ext], axis=1), jnp.concatenate([r2, r2_ext], axis=1), NT
        )
        dscore = (prob * dprob * scale).astype(BF16)
        prob = prob.astype(BF16)
        emit(0, cols, dot(dscore, r1, NN))
        add(0, cols, dot(dscore, m1, TN))
        if down:
            add(1, cols, dot(prob, m2, TN))
        else:
            emit(1, cols, dot(prob, r2, NN))


class Store:
    def __init__(self, slots, targets, fresh, olds=None):
        self.slots, self.targets, self.fresh = slots, targets, fresh
        self.olds = olds or [ref for ref, _ in targets]

    def __call__(self, which, cols, term):
        for i, (ref, base) in enumerate(self.targets):
            rows = pl.ds(base + which * self.slots, self.slots)
            part = term[i * self.slots:(i + 1) * self.slots]
            part = part if self.fresh else self.olds[i][rows, cols] + part
            ref[rows, cols] = part.astype(ref.dtype)


def causal(down, slots, shard=None):
    shape = (slots, slots if shard is None else 2 * slots)
    row = lax.broadcasted_iota(jnp.int32, shape, 0)
    place = lax.broadcasted_iota(jnp.int32, shape, 1)
    if shard is not None:
        place = jnp.where(place < slots, place, slots - shard % 2 * (slots + 1))
    return place <= row if down else place >= row


def router_part(positions, logit, dots, slots, shard):
    gate = jax.nn.sigmoid(logit[...])
    lane = lax.broadcasted_iota(jnp.int32, (1, slots), 1).astype(F32)
    used = lane < used_slots(positions, shard, slots)
    return jnp.where(used, gate * (1.0 - gate) * dots, 0.0)


FOUR_PLAN = (
    lambda level: [jnp.where(level < 2, 0, 2), jnp.where(level < 2, 1, 3)],
    lambda level: [jnp.where(level < 2, 2, 0), jnp.where(level < 2, 3, 1)],
    lambda level: [jnp.where(level % 2 == 0, 0, 3)],
    lambda level: [jnp.where(level < 2, 1, 2)],
)


def four_home_kernel(heads, positions, mine, own, turn, grads, own_total):
    slots = grads.shape[0] // 4
    rows = 2 * slots + TILE
    shard = lax.axis_index("seq")
    turn[...] = jnp.zeros(turn.shape, F32)
    for down in (True, False):

        @pl.when((shard < 4) == down)
        def _():
            for at in range(2):
                base = 2 * slots * at
                meet(
                    down, [(mine, at * rows, shard)], [(own, at * rows, shard)],
                    positions, heads, causal(down, slots),
                    Store(slots, [(grads, base)], True),
                    Store(slots, [(own_total, base)], True),
                )


def meets_pair(shard):
    return (shard % 2 == 1) == (shard < 4)


def follow_kernel(block, after, out):
    pass


def four_pair_kernel(
    heads, positions, after, mine, other, turn, grads_pair, met_total, early, early_total
):
    slots = early.shape[0] // 2
    rows = 2 * slots + TILE
    shard = lax.axis_index("seq")
    meets = meets_pair(shard)
    turn[...] = after[...]
    for level in range(4):

        @pl.when(meets & (shard // 2 == level))
        def _():
            for at in range(2):
                met = at == (1, 0, 1, 0)[level]
                meet(
                    level < 2, [(mine, at * rows, shard)], [(other, at * rows, shard ^ 1)],
                    positions, heads, None,
                    Store(slots, [(grads_pair, 2 * slots * at)], True),
                    Store(slots, [(met_total if met else early_total, 0)], True),
                )
            early[...] = early_total[...].astype(BF16)

    @pl.when(jnp.logical_not(meets))
    def _():
        early[...] = jnp.zeros(early.shape, BF16)


def four_skip_kernel(
    heads, positions, after, mine, own, other, near, skip,
    turn, own_near, other_near, back, near_total, grads_guest, skip_part
):
    slots = back.shape[0] // 2
    rows = 2 * slots + TILE
    shard = lax.axis_index("seq")
    turn[...] = after[...]
    for level in range(4):
        at = (1, 0, 1, 0)[level]

        @pl.when(shard // 2 == level)
        def _():
            pair = [(own, at * rows, shard), (other, at * rows, shard ^ 1)]
            totals = Store(slots, [(own_near, 0), (other_near, 0)], True)
            guest = [(near, 0, shard - 2)]
            if level in (0, 3):
                meet(
                    level == 0, guest, pair, positions, heads, None,
                    Store(slots, [(back, 0)], True), totals,
                )
                return
            far = [(skip, 0, shard - 4)]
            meet(
                level == 1, [(mine, at * rows, shard)] + far, guest, positions, heads, None,
                Store(slots, [(grads_guest, 0), (skip_part, 0)], True),
                Store(slots, [(near_total, 0)], True),
            )
            meet(
                level == 1, far, pair, positions, heads, None,
                Store(slots, [(skip_part, 0)], False), totals,
            )


def four_near_kernel(
    heads, positions, after, dots, dots_near, near, middle, back, near_total,
    dots_sum, near_low, middle_part
):
    slots = near_low.shape[0] // 2
    shard = lax.axis_index("seq")
    dots_sum[...] = dots[...] + dots_near[...]
    for level in range(4):

        @pl.when(shard // 2 == level)
        def _():
            if level in (0, 3):
                near_low[...] = back[...]
                return
            meet(
                level == 1, [(middle, 0, shard - 2)], [(near, 0, shard - 2)],
                positions, heads, None,
                Store(slots, [(middle_part, 0)], True),
                Store(slots, [(near_low, 0)], False, [near_total]),
            )


def four_last_kernel(
    heads, positions, dots_in, mine, own, other, cross, skip, middle,
    grads_in, skip_in, middle_in, met_pair, own_in, other_in,
    dots, grads_guest, skip_back, cross_low, middle_back, late, own_near,
    middle_part, other_near,
):
    slots = grads_in.shape[0] // 2
    rows = 2 * slots + TILE
    shard = lax.axis_index("seq")
    meets = meets_pair(shard)
    dots[...] = dots_in[...]
    for level in range(4):
        at = (1, 0, 1, 0)[level]

        @pl.when(shard // 2 == level)
        def _():
            if level in (0, 3):
                own_near[...] = own_in[...]
                other_near[...] = other_in[...]
            else:
                far = [(skip, 0, shard - 4), (middle, 0, shard - 2)]
                meet(
                    level == 1, far[1:], [(own, at * rows, shard), (other, at * rows, shard ^ 1)],
                    positions, heads, None,
                    Store(slots, [(middle_part, 0)], False, [middle_in]),
                    Store(slots, [(own_near, 0), (other_near, 0)], False, [own_in, other_in]),
                )
                meet(
                    level == 1, [(mine, at * rows, shard)] + far, [(cross, 0, (shard - 2) ^ 1)],
                    positions, heads, None,
                    Store(
                        slots, [(grads_guest, 0), (skip_back, 0), (middle_back, 0)], False,
                        [grads_in, skip_in, middle_part],
                    ),
                    Store(slots, [(cross_low, 0)], True),
                )

    late[...] = (other_near[...] + jnp.where(meets, met_pair[...], 0.0)).astype(BF16)


def four_sum_kernel(heads, grads, grads_pair, own, near, early, moving_sum, staying_sum):
    slots = grads.shape[0] // 4
    shard = lax.axis_index("seq")
    meets = meets_pair(shard)
    for level in range(4):

        @pl.when(shard // 2 == level)
        def _():
            for at in range(2):
                part = pl.ds(2 * slots * at, 2 * slots)
                moving = grads[part, :] + jnp.where(meets, grads_pair[part, :], 0.0)
                staying = own[part, :]
                if at != (1, 0, 1, 0)[level]:
                    staying = staying + early[...].astype(F32)
                    if level in (1, 2):
                        moving = moving + near[...].astype(F32)
                    else:
                        staying = staying + near[...].astype(F32)
                moving_sum[part, :] = moving
                staying_sum[part, :] = staying


def four_join_kernel(
    heads, positions, logit, dots, dots_far, moving_sum, staying_sum, grads_guest, own_near,
    middle, skip, cross, late, query_grad, key_grad, value_grad, router
):
    slots, half = moving_sum.shape[0] // 4, moving_sum.shape[1]
    shard = lax.axis_index("seq")
    router[...] = router_part(positions, logit, dots[...] + dots_far[...], slots, shard)
    for level in range(4):
        inner = level in (1, 2)

        @pl.when(shard // 2 == level)
        def _():
            if level < 2:
                moving, staying = [query_grad], [key_grad, value_grad]
            else:
                moving, staying = [key_grad, value_grad], [query_grad]
            for at in range(2):
                cols = pl.ds(at * half, half)
                met = at == (1, 0, 1, 0)[level]
                plus = [grads_guest] if inner and met else []
                if inner:
                    extra = [own_near, late] if met else [middle]
                else:
                    extra = [own_near, skip, late] if met else [cross]
                for outs, base, more in ((moving, moving_sum, plus), (staying, staying_sum, extra)):
                    for which, out in enumerate(outs):
                        rows = pl.ds((2 * at + which) * slots, slots)
                        total = base[rows, :]
                        for ref in more:
                            total = total + ref[pl.ds(which * slots, slots), :].astype(F32)
                        out[:, cols] = total.astype(BF16)


def four_levels(prep, shape, positions, logit, slots, heads, width):
    double, block, total = shape(4 * slots + 2 * TILE), shape(2 * slots + TILE), shape(2 * slots, F32)
    totals, low = shape(4 * slots, F32), shape(2 * slots)
    own, mine, near_send, far_send, dots = prep(FOUR_PLAN, [double, double, block, block])
    def pairs(levels, flip=0):
        return [(2 * a + c, 2 * b + (c ^ flip)) for a, b in levels for c in range(2)]

    near = lax.ppermute(near_send, "seq", pairs([(0, 1), (1, 0), (2, 3), (3, 2)]))
    other = lax.ppermute(own, "seq", pairs([(i, i) for i in range(4)], 1))
    skip = lax.ppermute(far_send, "seq", pairs([(0, 2), (3, 1)]))
    middle = lax.ppermute(far_send, "seq", pairs([(1, 2), (2, 1)]))
    row = shape(1, F32, slots)
    turn, grads, own_total = call(
        functools.partial(four_home_kernel, heads),
        [row] + [totals] * 2,
        positions, mine, own,
    )
    (near,) = call(
        follow_kernel, [block], near, turn, ins=[pl.ANY, pltpu.VMEM], outs=[pl.ANY], aliases={0: 0}
    )
    cross = lax.ppermute(near, "seq", pairs([(1, 1), (2, 2)], 1))
    turn, grads_pair, met_pair, early = call(
        functools.partial(four_pair_kernel, heads),
        [row, totals, total, low],
        positions, turn, mine, other,
        scratch=[pltpu.VMEM(total.shape, F32)],
    )
    early = lax.ppermute(early, "seq", pairs([(i, i) for i in range(4)], 1))
    turn, own_near, other_near, step_back, near_total, grads_guest, skip_part = call(
        functools.partial(four_skip_kernel, heads),
        [row, total, total, low, total, total, total],
        positions, turn, mine, own, other, near, skip,
    )
    dots_near = lax.ppermute(dots, "tp", [(i, i ^ 1) for i in range(4)])
    dots, near_low, middle_part = call(
        functools.partial(four_near_kernel, heads),
        [row, low, total],
        positions, turn, dots, dots_near, near, middle, step_back, near_total,
    )
    near = lax.ppermute(near_low, "seq", pairs([(0, 1), (1, 0), (2, 3), (3, 2)]))
    dots, grads_guest, skip_back, cross_low, middle_back, late, own_near = call(
        functools.partial(four_last_kernel, heads),
        [row, total, low, low, low, low, total],
        positions, dots, mine, own, other, cross, skip, middle,
        grads_guest, skip_part, middle_part, met_pair, own_near, other_near,
        scratch=[pltpu.VMEM(total.shape, F32)] * 2,
    )
    dots_far = lax.ppermute(dots, "tp", [(i, i ^ 2) for i in range(4)])
    skip = lax.ppermute(skip_back, "seq", pairs([(2, 0), (1, 3)]))
    cross = lax.ppermute(cross_low, "seq", pairs([(1, 0), (2, 3)], 1))
    middle = lax.ppermute(middle_back, "seq", pairs([(1, 2), (2, 1)]))
    late = lax.ppermute(late, "seq", pairs([(i, i) for i in range(4)], 1))
    moving_sum, staying_sum = call(
        functools.partial(four_sum_kernel, heads),
        [totals] * 2,
        grads, grads_pair, own_total, near, early,
        flops=SUM_FLOPS,
    )
    return call(
        functools.partial(four_join_kernel, heads),
        [shape(slots, BF16, width)] * 3 + [row],
        positions, logit, dots, dots_far, moving_sum, staying_sum, grads_guest, own_near,
        middle, skip, cross, late,
    )


def ring_plan(levels):
    sends = [
        lambda level, step=step: [jnp.where(level >= step, 2, 1)] for step in range(1, levels)
    ]
    return (lambda level: [0, 3], lambda level: [2], lambda level: [1], *sends)


def ring_home_kernel(
    heads, positions, logit, dots, down, up, own, other, grads, own_total, other_total, router
):
    slots = grads.shape[0] // 3
    rows = 2 * slots + TILE
    shard = lax.axis_index("seq")
    for goes_down, mine, at, base, stay_base in ((True, down, 0, 0, 0), (False, up, rows, 1, 2)):
        meet(
            goes_down, [(mine, 0, shard)], [(own, at, shard), (other, at, shard ^ 1)],
            positions, heads, causal(goes_down, slots, shard),
            Store(slots, [(grads, base * slots)], True),
            Store(slots, [(own_total, stay_base * slots), (other_total, stay_base * slots)], True),
        )
    router[...] = router_part(positions, logit, dots[...], slots, shard)


def ring_away_kernel(
    step, levels, heads, positions, own, other, block, own_in, other_in,
    back, own_total, other_total, *low
):
    slots = own_in.shape[0] // 3
    own_total[...] = own_in[...]
    other_total[...] = other_in[...]
    rows = 2 * slots + TILE
    shard = lax.axis_index("seq")
    for goes_down, at, base in ((True, 0, 0), (False, rows, 2 * slots)):

        @pl.when((shard // 2 + step < levels) == goes_down)
        def _():
            meet(
                goes_down, [(block, 0, shard + 2 * (step - levels))],
                [(own, at, shard), (other, at, shard ^ 1)],
                positions, heads, None,
                Store(slots, [(back, 0)], True),
                Store(slots, [(own_total, base), (other_total, base)], False),
            )

    for ref in low:
        ref[...] = other_total[...].astype(BF16)


def ring_join_kernel(heads, grads, own, other, *refs):
    back, (query_grad, key_grad, value_grad) = refs[:-3], refs[-3:]
    slots, half = grads.shape[0] // 3, grads.shape[1]
    level = lax.axis_index("seq") // 2
    low, high = pl.ds(0, half), pl.ds(half, half)
    parts = [pl.ds(i * slots, slots) for i in range(3)]
    stays = [(own[rows, :] + other[rows, :].astype(F32)).astype(BF16) for rows in parts]
    key_grad[:, low], value_grad[:, low], query_grad[:, high] = stays
    query_sum, key_sum, value_sum = [grads[rows, :] for rows in parts]
    for step, ref in enumerate(back, 1):
        went_down = level >= step
        first, second = ref[parts[0], :].astype(F32), ref[parts[1], :].astype(F32)
        query_sum = query_sum + jnp.where(went_down, first, 0.0)
        key_sum = key_sum + jnp.where(went_down, 0.0, first)
        value_sum = value_sum + jnp.where(went_down, 0.0, second)
    query_grad[:, low] = query_sum.astype(BF16)
    key_grad[:, high] = key_sum.astype(BF16)
    value_grad[:, high] = value_sum.astype(BF16)


def ring_levels(prep, shape, positions, logit, slots, heads, width, shards):
    levels = shards // 2
    block, total = shape(2 * slots + TILE), shape(3 * slots, F32)
    own, down, up, *sends, dots = prep(
        ring_plan(levels), [shape(4 * slots + 2 * TILE)] + [block] * (levels + 1)
    )
    pair = [(s, s ^ 1) for s in range(shards)]
    arrived = [
        lax.ppermute(send, "seq", [(s, (s - 2 * step) % shards) for s in range(shards)])
        for step, send in enumerate(sends, 1)
    ]
    other = lax.ppermute(own, "seq", pair)
    dots = sum_over(dots, "tp")
    grads, own_total, other_total, router = call(
        functools.partial(ring_home_kernel, heads),
        [total] * 3 + [shape(1, F32, slots)],
        positions, logit, dots, down, up, own, other,
    )
    backs, low = [], [other_total.astype(BF16)]
    for step, arrival in enumerate(arrived, 1):
        back, own_total, other_total, *low = call(
            functools.partial(ring_away_kernel, step, levels, heads),
            [shape(2 * slots), total, total] + [shape(3 * slots)] * (step == levels - 1),
            positions, own, other, arrival, own_total, other_total,
            )
        backs.append(
            lax.ppermute(back, "seq", [(s, (s + 2 * step) % shards) for s in range(shards)])
        )
    outs = call(
        functools.partial(ring_join_kernel, heads),
        [shape(slots, BF16, width)] * 3,
        grads, own_total, lax.ppermute(low[0], "seq", pair), *backs,
    )
    return *outs, router


def call(kernel, out_shape, *args, scratch=(), ins=None, outs=None, limit=VMEM, flops=1024, aliases=None):
    ins = ins or [pltpu.VMEM] * len(args)
    outs = outs or [pltpu.VMEM] * len(out_shape)
    return pl.pallas_call(
        kernel,
        out_shape=out_shape,
        in_specs=[pl.BlockSpec(memory_space=space) for space in ins],
        out_specs=[pl.BlockSpec(memory_space=space) for space in outs],
        scratch_shapes=list(scratch),
        input_output_aliases=aliases or {},
        compiler_params=pltpu.CompilerParams(vmem_limit_bytes=limit),
        cost_estimate=pl.CostEstimate(flops=flops, bytes_accessed=1024, transcendentals=0),
    )(*args)


def sum_over(values, axis):
    size = lax.axis_size(axis)
    if size & (size - 1):
        return lax.psum(values, axis)
    reach = 1
    while reach < size:
        pairs = [(i, i ^ reach) for i in range(size)]
        values = values + lax.ppermute(values, axis, pairs)
        reach *= 2
    return values


def body(
    query_proj, key_proj, value_proj, attn_output, out_grad, log_norm, router_logit, keep_positions
):
    slots, width = query_proj.shape
    heads = log_norm.shape[1]
    half = width // 2
    shards = lax.axis_size("seq")
    logit = router_logit.reshape(1, slots)
    positions = keep_positions.reshape(-1, LANES)

    def shape(rows, dtype=BF16, columns=half):
        return jax.ShapeDtypeStruct((rows, columns), dtype)

    sources = (
        attn_output, out_grad, logit, log_norm.T, positions, query_proj, key_proj, value_proj
    )

    def prep(plan, shapes):
        dots, *outs = call(
            functools.partial(prep_kernel, plan, heads),
            [shape(1, F32, slots)] + shapes,
            *sources,
            scratch=[pltpu.VMEM(a.shape, a.dtype) for a in sources[:5]]
            + [pltpu.VMEM((4 * (2 * slots + TILE), half), BF16)]
            + [pltpu.SemaphoreType.DMA((11,)), pltpu.SemaphoreType.DMA((2 * len(plan),))],
            ins=[pltpu.HBM] * len(sources),
            outs=[pltpu.VMEM] + [pltpu.HBM] * len(shapes),
            limit=PREP_VMEM,
        )
        return *outs, dots

    if shards == 8 and lax.axis_size("tp") == 4:
        query_grad, key_grad, value_grad, router = four_levels(
            prep, shape, positions, logit, slots, heads, width
        )
    else:
        query_grad, key_grad, value_grad, router = ring_levels(
            prep, shape, positions, logit, slots, heads, width, shards
        )
    return query_grad, key_grad, value_grad, router.reshape(slots)


def solution(mesh):
    wide = P("seq", "tp")
    return jax.shard_map(
        body,
        mesh=mesh,
        in_specs=(wide,) * 6 + (P("seq"), P()),
        out_specs=(wide, wide, wide, P("seq")),
        check_vma=False,
    )
```

```python
import functools
import math

import jax
import jax.numpy as jnp
from jax import lax
from jax.experimental import pallas as pl
from jax.experimental.pallas import tpu as pltpu
from jax.sharding import PartitionSpec as P


LANES = 128
PIECE = 8
GROUP = 4
ONE = 6 * GROUP
PACK = 4
TILE = 16
BIG = 1e30
VMEM = 24 * 1024 * 1024
SUM_FLOPS = 5_000_000_000
PREP_VMEM = 63 * 1024 * 1024
F32 = jnp.float32
BF16 = jnp.bfloat16
NT = (((1,), (1,)), ((), ()))
NN = (((1,), (0,)), ((), ()))
TN = (((0,), (0,)), ((), ()))


def dot(left, right, dims):
    return lax.dot_general(left, right, dims, preferred_element_type=F32)


def pieces(rows):
    high = rows.astype(BF16).astype(F32)
    rest = rows - high
    middle = rest.astype(BF16).astype(F32)
    return [high, middle, rest - middle]


def split_exact(product):
    high = product.astype(BF16)
    return high, (product - high.astype(F32)).astype(BF16)


def used_slots(positions, shard, slots):
    table = positions[...]
    place = lax.broadcasted_iota(jnp.int32, table.shape, 0) * LANES
    place = place + lax.broadcasted_iota(jnp.int32, table.shape, 1)
    mine = (place >= shard * slots) & (place < (shard + 1) * slots) & (table >= 0)
    count = jnp.sum(jnp.where(mine, 1.0, 0.0), axis=1, keepdims=True)
    return jnp.sum(count, axis=0, keepdims=True)


def pack(ext):
    quarter = ext.shape[0] // PACK
    total = ext[:quarter]
    for part in range(1, PACK):
        rows = ext[part * quarter:(part + 1) * quarter]
        total = total + pltpu.roll(rows, part * LANES // PACK, 1)
    groups = [total[at:at + TILE] for at in range(0, quarter, TILE)]
    return jnp.concatenate(groups, axis=1).astype(BF16)


def unpack(packed):
    wide = packed.astype(F32)
    groups = [wide[:, at:at + LANES] for at in range(0, wide.shape[1], LANES)]
    total = jnp.concatenate(groups, axis=0)
    parts = [total]
    for part in range(1, PACK):
        parts.append(pltpu.roll(total, LANES - part * LANES // PACK, 1))
    return jnp.concatenate(parts, axis=0).astype(BF16)


def key_ext(positions, shard, slots):
    count = used_slots(positions, shard, slots)
    slot = lax.broadcasted_iota(jnp.int32, (slots, LANES), 0).astype(F32)
    lane = lax.broadcasted_iota(jnp.int32, (slots, LANES), 1)
    return jnp.where((lane == ONE) & (slot >= count), -BIG, 0.0).astype(BF16)


def prep_kernel(plan, heads, *refs):
    sources, (query, key, value), rest = refs[:5], refs[5:8], refs[8:]
    dots, outs, rest = rest[0], rest[1:len(plan) + 1], rest[len(plan) + 1:]
    held, (bank, sems, done) = rest[:5], rest[5:]
    output, grad, logit, norm, positions = held
    slots, width = grad.shape
    half = width // 2
    rows = 2 * slots + TILE
    copies = [
        pltpu.make_async_copy(source, dest, sems.at[i])
        for i, (source, dest) in enumerate(zip(sources, held))
    ]
    for at in range(2):
        for source, base in ((key, at), (value, at + 0.5), (query, at + 2)):
            first = int(base) * rows + (slots if base % 1 else 0)
            copies.append(
                pltpu.make_async_copy(
                    source.at[:, pl.ds(at * half, half)],
                    bank.at[pl.ds(first, slots), :],
                    sems.at[len(copies)],
                )
            )
    for copy in copies:
        copy.start()
    for copy in copies[:5]:
        copy.wait()
    head_dim = width // heads
    root = math.sqrt(head_dim)
    shard = lax.axis_index("seq")
    count = used_slots(positions, shard, slots)
    lane = lax.broadcasted_iota(jnp.int32, (PIECE, slots), 1).astype(F32)
    used = lane < count
    gate_row = jax.nn.sigmoid(logit[...])
    gate = jnp.transpose(jnp.broadcast_to(gate_row, (LANES, slots)))
    head_of = lax.broadcasted_iota(jnp.int32, (PIECE, width), 1) // head_dim
    head_row = lax.broadcasted_iota(jnp.int32, (PIECE, width), 0)
    pick = (head_of == head_row).astype(BF16)
    ones = jnp.ones((PIECE, width), BF16)
    dout_parts, delta_parts, dot_parts = [], [], []
    for h in range(heads):
        cols = pl.ds(h * head_dim, head_dim)
        wide = grad[:, cols].astype(F32)
        out = output[:, cols].astype(F32)
        dout = (wide * gate).astype(BF16)
        dout_parts.append(dout)
        delta_parts.append(dout.astype(F32) * out)
        dot_parts.append(wide * out)
    for copy in copies[5:]:
        copy.wait()
    for at in range(2):
        bank[pl.ds(at * rows + 2 * slots, TILE), :] = jnp.zeros((TILE, half), BF16)
    level = lax.axis_index("seq") // 2
    moves = []
    for out, blocks in zip(outs, plan):
        for place, block in enumerate(blocks(level)):
            block = jnp.int32(block)
            move = pltpu.make_async_copy(
                bank.at[pl.ds(pl.multiple_of(block * rows, TILE), rows), :],
                out.at[pl.ds(place * rows, rows), :],
                done.at[len(moves)],
            )
            moves.append((block, move))

    def each(some, early):
        for block, move in some:

            @pl.when((block < 2) == early)
            def _():
                move.start()

    each(moves, True)
    delta_high, delta_low = split_exact(jnp.concatenate(delta_parts, axis=1))
    delta = dot(pick, delta_high, NT) + dot(pick, delta_low, NT)
    dot_high, dot_low = split_exact(jnp.concatenate(dot_parts, axis=1))
    dots[...] = (dot(ones, dot_high, NT) + dot(ones, dot_low, NT))[:1]

    pad = jnp.zeros((PIECE - heads, slots), F32)
    scaled = jnp.where(used, jnp.concatenate([norm[...] * root, pad], axis=0), BIG)
    delta = jnp.where(used, delta, 0.0)
    first = lax.broadcasted_iota(jnp.int32, (PIECE, slots), 0) == 0
    stack = pieces(scaled) + pieces(delta) + [jnp.where(first, 1.0, 0.0)]
    stack.append(jnp.zeros((PIECE * (PIECE - len(stack)), slots), F32))
    stats = jnp.concatenate(stack, axis=0).astype(BF16)
    source = lax.broadcasted_iota(jnp.int32, (PIECE * PIECE, LANES), 0)
    target = lax.broadcasted_iota(jnp.int32, (PIECE * PIECE, LANES), 1)
    piece, head = source // PIECE, source % PIECE

    def ext(first_head):
        local = head - first_head
        taken = (local >= 0) & (local < heads // 2) & (piece < 6)
        column = jnp.where(taken, piece * GROUP + local, -1)
        column = jnp.where(source == 6 * PIECE, ONE, column)
        return dot(stats, (column == target).astype(BF16), TN)

    per = heads // 2
    for at in range(2):
        base = (2 + at) * rows
        bank[pl.ds(base + slots, slots), :] = jnp.concatenate(
            dout_parts[at * per:(at + 1) * per], axis=1
        )
        bank[pl.ds(base + 2 * slots, TILE), :] = pack(ext(at * per))
    each(moves, False)
    for _, move in moves:
        move.wait()


def head_marks(head, is_value):
    lane = lax.broadcasted_iota(jnp.int32, (1, LANES), 1)
    base = (3 * GROUP if is_value else 0) + head
    marked = (lane == base) | (lane == base + GROUP) | (lane == base + 2 * GROUP)
    return jnp.where(marked, -1.0, 0.0).astype(BF16)


def meet(down, movings, stays, positions, heads, mask, emit, add):
    half = movings[0][0].shape[1]
    slots = emit.slots
    head_dim = half // (heads // 2)
    scale = head_dim ** -0.5
    to_log2 = scale * math.log2(math.e)

    def stats(blocks, queries):
        parts = []
        for ref, at, shard in blocks:
            if queries:
                parts.append(unpack(ref[pl.ds(at + 2 * slots, TILE), :]))
            else:
                parts.append(key_ext(positions, shard, slots))
        return jnp.concatenate(parts, axis=0)

    def load(blocks, which, cols):
        parts = [ref[pl.ds(at + which * slots, slots), cols] for ref, at, _ in blocks]
        return jnp.concatenate(parts, axis=0)

    moving_ext, stay_ext = stats(movings, down), stats(stays, not down)
    for h in range(heads // 2):
        cols = pl.ds(h * head_dim, head_dim)
        m1, m2 = load(movings, 0, cols), load(movings, 1, cols)
        r1, r2 = load(stays, 0, cols), load(stays, 1, cols)
        key_mark, value_mark = head_marks(h, False), head_marks(h, True)
        if down:
            m1_ext, m2_ext = moving_ext, moving_ext
            r1_ext = stay_ext + key_mark
            r2_ext = jnp.broadcast_to(value_mark, stay_ext.shape)
        else:
            m1_ext = moving_ext + key_mark
            m2_ext = jnp.broadcast_to(value_mark, moving_ext.shape)
            r1_ext, r2_ext = stay_ext, stay_ext
        scores = dot(
            jnp.concatenate([m1, m1_ext], axis=1), jnp.concatenate([r1, r1_ext], axis=1), NT
        )
        if mask is not None:
            scores = jnp.where(mask, scores, -BIG)
        prob = jnp.exp2(scores * to_log2)
        dprob = dot(
            jnp.concatenate([m2, m2_ext], axis=1), jnp.concatenate([r2, r2_ext], axis=1), NT
        )
        dscore = (prob * dprob * scale).astype(BF16)
        prob = prob.astype(BF16)
        emit(0, cols, dot(dscore, r1, NN))
        add(0, cols, dot(dscore, m1, TN))
        if down:
            add(1, cols, dot(prob, m2, TN))
        else:
            emit(1, cols, dot(prob, r2, NN))


class Store:
    def __init__(self, slots, targets, fresh, olds=None):
        self.slots, self.targets, self.fresh = slots, targets, fresh
        self.olds = olds or [ref for ref, _ in targets]

    def __call__(self, which, cols, term):
        for i, (ref, base) in enumerate(self.targets):
            rows = pl.ds(base + which * self.slots, self.slots)
            part = term[i * self.slots:(i + 1) * self.slots]
            part = part if self.fresh else self.olds[i][rows, cols] + part
            ref[rows, cols] = part.astype(ref.dtype)


def causal(down, slots, shard=None):
    shape = (slots, slots if shard is None else 2 * slots)
    row = lax.broadcasted_iota(jnp.int32, shape, 0)
    place = lax.broadcasted_iota(jnp.int32, shape, 1)
    if shard is not None:
        place = jnp.where(place < slots, place, slots - shard % 2 * (slots + 1))
    return place <= row if down else place >= row


def router_part(positions, logit, dots, slots, shard):
    gate = jax.nn.sigmoid(logit[...])
    lane = lax.broadcasted_iota(jnp.int32, (1, slots), 1).astype(F32)
    used = lane < used_slots(positions, shard, slots)
    return jnp.where(used, gate * (1.0 - gate) * dots, 0.0)


FOUR_PLAN = (
    lambda level: [jnp.where(level < 2, 0, 2), jnp.where(level < 2, 1, 3)],
    lambda level: [jnp.where(level < 2, 2, 0), jnp.where(level < 2, 3, 1)],
    lambda level: [jnp.where(level % 2 == 0, 0, 3)],
    lambda level: [jnp.where(level < 2, 1, 2)],
)


def four_home_kernel(heads, positions, mine, own, turn, grads, own_total):
    slots = grads.shape[0] // 4
    rows = 2 * slots + TILE
    shard = lax.axis_index("seq")
    turn[...] = jnp.zeros(turn.shape, F32)
    for down in (True, False):

        @pl.when((shard < 4) == down)
        def _():
            for at in range(2):
                base = 2 * slots * at
                meet(
                    down, [(mine, at * rows, shard)], [(own, at * rows, shard)],
                    positions, heads, causal(down, slots),
                    Store(slots, [(grads, base)], True),
                    Store(slots, [(own_total, base)], True),
                )


def meets_pair(shard):
    return (shard % 2 == 1) == (shard < 4)


def follow_kernel(block, after, out):
    pass


def four_pair_kernel(
    heads, positions, after, mine, other, turn, grads_pair, met_total, early, early_total
):
    slots = early.shape[0] // 2
    rows = 2 * slots + TILE
    shard = lax.axis_index("seq")
    meets = meets_pair(shard)
    turn[...] = after[...]
    for level in range(4):

        @pl.when(meets & (shard // 2 == level))
        def _():
            for at in range(2):
                met = at == (1, 0, 1, 0)[level]
                meet(
                    level < 2, [(mine, at * rows, shard)], [(other, at * rows, shard ^ 1)],
                    positions, heads, None,
                    Store(slots, [(grads_pair, 2 * slots * at)], True),
                    Store(slots, [(met_total if met else early_total, 0)], True),
                )
            early[...] = early_total[...].astype(BF16)

    @pl.when(jnp.logical_not(meets))
    def _():
        early[...] = jnp.zeros(early.shape, BF16)


def four_skip_kernel(
    heads, positions, after, mine, own, other, near, skip,
    turn, own_near, other_near, back, near_total, grads_guest, skip_part
):
    slots = back.shape[0] // 2
    rows = 2 * slots + TILE
    shard = lax.axis_index("seq")
    turn[...] = after[...]
    for level in range(4):
        at = (1, 0, 1, 0)[level]

        @pl.when(shard // 2 == level)
        def _():
            pair = [(own, at * rows, shard), (other, at * rows, shard ^ 1)]
            totals = Store(slots, [(own_near, 0), (other_near, 0)], True)
            guest = [(near, 0, shard - 2)]
            if level in (0, 3):
                meet(
                    level == 0, guest, pair, positions, heads, None,
                    Store(slots, [(back, 0)], True), totals,
                )
                return
            far = [(skip, 0, shard - 4)]
            meet(
                level == 1, [(mine, at * rows, shard)] + far, guest, positions, heads, None,
                Store(slots, [(grads_guest, 0), (skip_part, 0)], True),
                Store(slots, [(near_total, 0)], True),
            )
            meet(
                level == 1, far, pair, positions, heads, None,
                Store(slots, [(skip_part, 0)], False), totals,
            )


def four_near_kernel(
    heads, positions, after, dots, dots_near, near, middle, back, near_total,
    dots_sum, near_low, middle_part
):
    slots = near_low.shape[0] // 2
    shard = lax.axis_index("seq")
    dots_sum[...] = dots[...] + dots_near[...]
    for level in range(4):

        @pl.when(shard // 2 == level)
        def _():
            if level in (0, 3):
                near_low[...] = back[...]
                return
            meet(
                level == 1, [(middle, 0, shard - 2)], [(near, 0, shard - 2)],
                positions, heads, None,
                Store(slots, [(middle_part, 0)], True),
                Store(slots, [(near_low, 0)], False, [near_total]),
            )


def four_last_kernel(
    heads, positions, dots_in, mine, own, other, cross, skip, middle,
    grads_in, skip_in, middle_in, met_pair, own_in, other_in,
    dots, grads_guest, skip_back, cross_low, middle_back, late, own_near,
    middle_part, other_near,
):
    slots = grads_in.shape[0] // 2
    rows = 2 * slots + TILE
    shard = lax.axis_index("seq")
    meets = meets_pair(shard)
    dots[...] = dots_in[...]
    for level in range(4):
        at = (1, 0, 1, 0)[level]

        @pl.when(shard // 2 == level)
        def _():
            if level in (0, 3):
                own_near[...] = own_in[...]
                other_near[...] = other_in[...]
            else:
                far = [(skip, 0, shard - 4), (middle, 0, shard - 2)]
                meet(
                    level == 1, far[1:], [(own, at * rows, shard), (other, at * rows, shard ^ 1)],
                    positions, heads, None,
                    Store(slots, [(middle_part, 0)], False, [middle_in]),
                    Store(slots, [(own_near, 0), (other_near, 0)], False, [own_in, other_in]),
                )
                meet(
                    level == 1, [(mine, at * rows, shard)] + far, [(cross, 0, (shard - 2) ^ 1)],
                    positions, heads, None,
                    Store(
                        slots, [(grads_guest, 0), (skip_back, 0), (middle_back, 0)], False,
                        [grads_in, skip_in, middle_part],
                    ),
                    Store(slots, [(cross_low, 0)], True),
                )

    late[...] = (other_near[...] + jnp.where(meets, met_pair[...], 0.0)).astype(BF16)


def four_sum_kernel(heads, grads, grads_pair, own, near, early, moving_sum, staying_sum):
    slots = grads.shape[0] // 4
    shard = lax.axis_index("seq")
    meets = meets_pair(shard)
    for level in range(4):

        @pl.when(shard // 2 == level)
        def _():
            for at in range(2):
                part = pl.ds(2 * slots * at, 2 * slots)
                moving = grads[part, :] + jnp.where(meets, grads_pair[part, :], 0.0)
                staying = own[part, :]
                if at != (1, 0, 1, 0)[level]:
                    staying = staying + early[...].astype(F32)
                    if level in (1, 2):
                        moving = moving + near[...].astype(F32)
                    else:
                        staying = staying + near[...].astype(F32)
                moving_sum[part, :] = moving
                staying_sum[part, :] = staying


def four_join_kernel(
    heads, positions, logit, dots, dots_far, moving_sum, staying_sum, grads_guest, own_near,
    middle, skip, cross, late, query_grad, key_grad, value_grad, router
):
    slots, half = moving_sum.shape[0] // 4, moving_sum.shape[1]
    shard = lax.axis_index("seq")
    router[...] = router_part(positions, logit, dots[...] + dots_far[...], slots, shard)
    for level in range(4):
        inner = level in (1, 2)

        @pl.when(shard // 2 == level)
        def _():
            if level < 2:
                moving, staying = [query_grad], [key_grad, value_grad]
            else:
                moving, staying = [key_grad, value_grad], [query_grad]
            for at in range(2):
                cols = pl.ds(at * half, half)
                met = at == (1, 0, 1, 0)[level]
                plus = [grads_guest] if inner and met else []
                if inner:
                    extra = [own_near, late] if met else [middle]
                else:
                    extra = [own_near, skip, late] if met else [cross]
                for outs, base, more in ((moving, moving_sum, plus), (staying, staying_sum, extra)):
                    for which, out in enumerate(outs):
                        rows = pl.ds((2 * at + which) * slots, slots)
                        total = base[rows, :]
                        for ref in more:
                            total = total + ref[pl.ds(which * slots, slots), :].astype(F32)
                        out[:, cols] = total.astype(BF16)


def four_levels(prep, shape, positions, logit, slots, heads, width):
    double, block, total = shape(4 * slots + 2 * TILE), shape(2 * slots + TILE), shape(2 * slots, F32)
    totals, low = shape(4 * slots, F32), shape(2 * slots)
    own, mine, near_send, far_send, dots = prep(FOUR_PLAN, [double, double, block, block])
    def pairs(levels, flip=0):
        return [(2 * a + c, 2 * b + (c ^ flip)) for a, b in levels for c in range(2)]

    near = lax.ppermute(near_send, "seq", pairs([(0, 1), (1, 0), (2, 3), (3, 2)]))
    other = lax.ppermute(own, "seq", pairs([(i, i) for i in range(4)], 1))
    skip = lax.ppermute(far_send, "seq", pairs([(0, 2), (3, 1)]))
    middle = lax.ppermute(far_send, "seq", pairs([(1, 2), (2, 1)]))
    row = shape(1, F32, slots)
    turn, grads, own_total = call(
        functools.partial(four_home_kernel, heads),
        [row] + [totals] * 2,
        positions, mine, own,
    )
    (near,) = call(
        follow_kernel, [block], near, turn, ins=[pl.ANY, pltpu.VMEM], outs=[pl.ANY], aliases={0: 0}
    )
    cross = lax.ppermute(near, "seq", pairs([(1, 1), (2, 2)], 1))
    turn, grads_pair, met_pair, early = call(
        functools.partial(four_pair_kernel, heads),
        [row, totals, total, low],
        positions, turn, mine, other,
        scratch=[pltpu.VMEM(total.shape, F32)],
    )
    early = lax.ppermute(early, "seq", pairs([(i, i) for i in range(4)], 1))
    turn, own_near, other_near, step_back, near_total, grads_guest, skip_part = call(
        functools.partial(four_skip_kernel, heads),
        [row, total, total, low, total, total, total],
        positions, turn, mine, own, other, near, skip,
    )
    dots_near = lax.ppermute(dots, "tp", [(i, i ^ 1) for i in range(4)])
    dots, near_low, middle_part = call(
        functools.partial(four_near_kernel, heads),
        [row, low, total],
        positions, turn, dots, dots_near, near, middle, step_back, near_total,
    )
    near = lax.ppermute(near_low, "seq", pairs([(0, 1), (1, 0), (2, 3), (3, 2)]))
    dots, grads_guest, skip_back, cross_low, middle_back, late, own_near = call(
        functools.partial(four_last_kernel, heads),
        [row, total, low, low, low, low, total],
        positions, dots, mine, own, other, cross, skip, middle,
        grads_guest, skip_part, middle_part, met_pair, own_near, other_near,
        scratch=[pltpu.VMEM(total.shape, F32)] * 2,
    )
    dots_far = lax.ppermute(dots, "tp", [(i, i ^ 2) for i in range(4)])
    skip = lax.ppermute(skip_back, "seq", pairs([(2, 0), (1, 3)]))
    cross = lax.ppermute(cross_low, "seq", pairs([(1, 0), (2, 3)], 1))
    middle = lax.ppermute(middle_back, "seq", pairs([(1, 2), (2, 1)]))
    late = lax.ppermute(late, "seq", pairs([(i, i) for i in range(4)], 1))
    moving_sum, staying_sum = call(
        functools.partial(four_sum_kernel, heads),
        [totals] * 2,
        grads, grads_pair, own_total, near, early,
        flops=SUM_FLOPS,
    )
    return call(
        functools.partial(four_join_kernel, heads),
        [shape(slots, BF16, width)] * 3 + [row],
        positions, logit, dots, dots_far, moving_sum, staying_sum, grads_guest, own_near,
        middle, skip, cross, late,
    )


def ring_plan(levels):
    sends = [
        lambda level, step=step: [jnp.where(level >= step, 2, 1)] for step in range(1, levels)
    ]
    return (lambda level: [0, 3], lambda level: [2], lambda level: [1], *sends)


def ring_home_kernel(
    heads, positions, logit, dots, down, up, own, other, grads, own_total, other_total, router
):
    slots = grads.shape[0] // 3
    rows = 2 * slots + TILE
    shard = lax.axis_index("seq")
    for goes_down, mine, at, base, stay_base in ((True, down, 0, 0, 0), (False, up, rows, 1, 2)):
        meet(
            goes_down, [(mine, 0, shard)], [(own, at, shard), (other, at, shard ^ 1)],
            positions, heads, causal(goes_down, slots, shard),
            Store(slots, [(grads, base * slots)], True),
            Store(slots, [(own_total, stay_base * slots), (other_total, stay_base * slots)], True),
        )
    router[...] = router_part(positions, logit, dots[...], slots, shard)


def ring_away_kernel(
    step, levels, heads, positions, own, other, block, own_in, other_in,
    back, own_total, other_total, *low
):
    slots = own_in.shape[0] // 3
    own_total[...] = own_in[...]
    other_total[...] = other_in[...]
    rows = 2 * slots + TILE
    shard = lax.axis_index("seq")
    for goes_down, at, base in ((True, 0, 0), (False, rows, 2 * slots)):

        @pl.when((shard // 2 + step < levels) == goes_down)
        def _():
            meet(
                goes_down, [(block, 0, shard + 2 * (step - levels))],
                [(own, at, shard), (other, at, shard ^ 1)],
                positions, heads, None,
                Store(slots, [(back, 0)], True),
                Store(slots, [(own_total, base), (other_total, base)], False),
            )

    for ref in low:
        ref[...] = other_total[...].astype(BF16)


def ring_join_kernel(heads, grads, own, other, *refs):
    back, (query_grad, key_grad, value_grad) = refs[:-3], refs[-3:]
    slots, half = grads.shape[0] // 3, grads.shape[1]
    level = lax.axis_index("seq") // 2
    low, high = pl.ds(0, half), pl.ds(half, half)
    parts = [pl.ds(i * slots, slots) for i in range(3)]
    stays = [(own[rows, :] + other[rows, :].astype(F32)).astype(BF16) for rows in parts]
    key_grad[:, low], value_grad[:, low], query_grad[:, high] = stays
    query_sum, key_sum, value_sum = [grads[rows, :] for rows in parts]
    for step, ref in enumerate(back, 1):
        went_down = level >= step
        first, second = ref[parts[0], :].astype(F32), ref[parts[1], :].astype(F32)
        query_sum = query_sum + jnp.where(went_down, first, 0.0)
        key_sum = key_sum + jnp.where(went_down, 0.0, first)
        value_sum = value_sum + jnp.where(went_down, 0.0, second)
    query_grad[:, low] = query_sum.astype(BF16)
    key_grad[:, high] = key_sum.astype(BF16)
    value_grad[:, high] = value_sum.astype(BF16)


def ring_levels(prep, shape, positions, logit, slots, heads, width, shards):
    levels = shards // 2
    block, total = shape(2 * slots + TILE), shape(3 * slots, F32)
    own, down, up, *sends, dots = prep(
        ring_plan(levels), [shape(4 * slots + 2 * TILE)] + [block] * (levels + 1)
    )
    pair = [(s, s ^ 1) for s in range(shards)]
    arrived = [
        lax.ppermute(send, "seq", [(s, (s - 2 * step) % shards) for s in range(shards)])
        for step, send in enumerate(sends, 1)
    ]
    other = lax.ppermute(own, "seq", pair)
    dots = sum_over(dots, "tp")
    grads, own_total, other_total, router = call(
        functools.partial(ring_home_kernel, heads),
        [total] * 3 + [shape(1, F32, slots)],
        positions, logit, dots, down, up, own, other,
    )
    backs, low = [], [other_total.astype(BF16)]
    for step, arrival in enumerate(arrived, 1):
        back, own_total, other_total, *low = call(
            functools.partial(ring_away_kernel, step, levels, heads),
            [shape(2 * slots), total, total] + [shape(3 * slots)] * (step == levels - 1),
            positions, own, other, arrival, own_total, other_total,
            )
        backs.append(
            lax.ppermute(back, "seq", [(s, (s + 2 * step) % shards) for s in range(shards)])
        )
    outs = call(
        functools.partial(ring_join_kernel, heads),
        [shape(slots, BF16, width)] * 3,
        grads, own_total, lax.ppermute(low[0], "seq", pair), *backs,
    )
    return *outs, router


def call(kernel, out_shape, *args, scratch=(), ins=None, outs=None, limit=VMEM, flops=1024, aliases=None):
    ins = ins or [pltpu.VMEM] * len(args)
    outs = outs or [pltpu.VMEM] * len(out_shape)
    return pl.pallas_call(
        kernel,
        out_shape=out_shape,
        in_specs=[pl.BlockSpec(memory_space=space) for space in ins],
        out_specs=[pl.BlockSpec(memory_space=space) for space in outs],
        scratch_shapes=list(scratch),
        input_output_aliases=aliases or {},
        compiler_params=pltpu.CompilerParams(vmem_limit_bytes=limit),
        cost_estimate=pl.CostEstimate(flops=flops, bytes_accessed=1024, transcendentals=0),
    )(*args)


def sum_over(values, axis):
    size = lax.axis_size(axis)
    if size & (size - 1):
        return lax.psum(values, axis)
    reach = 1
    while reach < size:
        pairs = [(i, i ^ reach) for i in range(size)]
        values = values + lax.ppermute(values, axis, pairs)
        reach *= 2
    return values


def body(
    query_proj, key_proj, value_proj, attn_output, out_grad, log_norm, router_logit, keep_positions
):
    slots, width = query_proj.shape
    heads = log_norm.shape[1]
    half = width // 2
    shards = lax.axis_size("seq")
    logit = router_logit.reshape(1, slots)
    positions = keep_positions.reshape(-1, LANES)

    def shape(rows, dtype=BF16, columns=half):
        return jax.ShapeDtypeStruct((rows, columns), dtype)

    sources = (
        attn_output, out_grad, logit, log_norm.T, positions, query_proj, key_proj, value_proj
    )

    def prep(plan, shapes):
        dots, *outs = call(
            functools.partial(prep_kernel, plan, heads),
            [shape(1, F32, slots)] + shapes,
            *sources,
            scratch=[pltpu.VMEM(a.shape, a.dtype) for a in sources[:5]]
            + [pltpu.VMEM((4 * (2 * slots + TILE), half), BF16)]
            + [pltpu.SemaphoreType.DMA((11,)), pltpu.SemaphoreType.DMA((2 * len(plan),))],
            ins=[pltpu.HBM] * len(sources),
            outs=[pltpu.VMEM] + [pltpu.HBM] * len(shapes),
            limit=PREP_VMEM,
        )
        return *outs, dots

    if shards == 8 and lax.axis_size("tp") == 4:
        query_grad, key_grad, value_grad, router = four_levels(
            prep, shape, positions, logit, slots, heads, width
        )
    else:
        query_grad, key_grad, value_grad, router = ring_levels(
            prep, shape, positions, logit, slots, heads, width, shards
        )
    return query_grad, key_grad, value_grad, router.reshape(slots)


def solution(mesh):
    wide = P("seq", "tp")
    return jax.shard_map(
        body,
        mesh=mesh,
        in_specs=(wide,) * 6 + (P("seq"), P()),
        out_specs=(wide, wide, wide, P("seq")),
        check_vma=False,
    )
```

```python
import functools
import math

import jax
import jax.numpy as jnp
from jax import lax
from jax.experimental import pallas as pl
from jax.experimental.pallas import tpu as pltpu
from jax.sharding import PartitionSpec as P


LANES = 128
PIECE = 8
GROUP = 4
ONE = 6 * GROUP
PACK = 4
TILE = 16
BIG = 1e30
VMEM = 24 * 1024 * 1024
SUM_FLOPS = 5_000_000_000
PREP_VMEM = 63 * 1024 * 1024
F32 = jnp.float32
BF16 = jnp.bfloat16
NT = (((1,), (1,)), ((), ()))
NN = (((1,), (0,)), ((), ()))
TN = (((0,), (0,)), ((), ()))


def dot(left, right, dims):
    return lax.dot_general(left, right, dims, preferred_element_type=F32)


def pieces(rows):
    high = rows.astype(BF16).astype(F32)
    rest = rows - high
    middle = rest.astype(BF16).astype(F32)
    return [high, middle, rest - middle]


def split_exact(product):
    high = product.astype(BF16)
    return high, (product - high.astype(F32)).astype(BF16)


def used_slots(positions, shard, slots):
    table = positions[...]
    place = lax.broadcasted_iota(jnp.int32, table.shape, 0) * LANES
    place = place + lax.broadcasted_iota(jnp.int32, table.shape, 1)
    mine = (place >= shard * slots) & (place < (shard + 1) * slots) & (table >= 0)
    count = jnp.sum(jnp.where(mine, 1.0, 0.0), axis=1, keepdims=True)
    return jnp.sum(count, axis=0, keepdims=True)


def pack(ext):
    quarter = ext.shape[0] // PACK
    total = ext[:quarter]
    for part in range(1, PACK):
        rows = ext[part * quarter:(part + 1) * quarter]
        total = total + pltpu.roll(rows, part * LANES // PACK, 1)
    groups = [total[at:at + TILE] for at in range(0, quarter, TILE)]
    return jnp.concatenate(groups, axis=1).astype(BF16)


def unpack(packed):
    wide = packed.astype(F32)
    groups = [wide[:, at:at + LANES] for at in range(0, wide.shape[1], LANES)]
    total = jnp.concatenate(groups, axis=0)
    parts = [total]
    for part in range(1, PACK):
        parts.append(pltpu.roll(total, LANES - part * LANES // PACK, 1))
    return jnp.concatenate(parts, axis=0).astype(BF16)


def key_ext(positions, shard, slots):
    count = used_slots(positions, shard, slots)
    slot = lax.broadcasted_iota(jnp.int32, (slots, LANES), 0).astype(F32)
    lane = lax.broadcasted_iota(jnp.int32, (slots, LANES), 1)
    return jnp.where((lane == ONE) & (slot >= count), -BIG, 0.0).astype(BF16)


def prep_kernel(plan, heads, *refs):
    sources, (query, key, value), rest = refs[:5], refs[5:8], refs[8:]
    dots, outs, rest = rest[0], rest[1:len(plan) + 1], rest[len(plan) + 1:]
    held, (bank, sems, done) = rest[:5], rest[5:]
    output, grad, logit, norm, positions = held
    slots, width = grad.shape
    half = width // 2
    rows = 2 * slots + TILE
    copies = [
        pltpu.make_async_copy(source, dest, sems.at[i])
        for i, (source, dest) in enumerate(zip(sources, held))
    ]
    for at in range(2):
        for source, base in ((key, at), (value, at + 0.5), (query, at + 2)):
            first = int(base) * rows + (slots if base % 1 else 0)
            copies.append(
                pltpu.make_async_copy(
                    source.at[:, pl.ds(at * half, half)],
                    bank.at[pl.ds(first, slots), :],
                    sems.at[len(copies)],
                )
            )
    for copy in copies:
        copy.start()
    for copy in copies[:5]:
        copy.wait()
    head_dim = width // heads
    root = math.sqrt(head_dim)
    shard = lax.axis_index("seq")
    count = used_slots(positions, shard, slots)
    lane = lax.broadcasted_iota(jnp.int32, (PIECE, slots), 1).astype(F32)
    used = lane < count
    gate_row = jax.nn.sigmoid(logit[...])
    gate = jnp.transpose(jnp.broadcast_to(gate_row, (LANES, slots)))
    head_of = lax.broadcasted_iota(jnp.int32, (PIECE, width), 1) // head_dim
    head_row = lax.broadcasted_iota(jnp.int32, (PIECE, width), 0)
    pick = (head_of == head_row).astype(BF16)
    ones = jnp.ones((PIECE, width), BF16)
    dout_parts, delta_parts, dot_parts = [], [], []
    for h in range(heads):
        cols = pl.ds(h * head_dim, head_dim)
        wide = grad[:, cols].astype(F32)
        out = output[:, cols].astype(F32)
        dout = (wide * gate).astype(BF16)
        dout_parts.append(dout)
        delta_parts.append(dout.astype(F32) * out)
        dot_parts.append(wide * out)
    for copy in copies[5:]:
        copy.wait()
    for at in range(2):
        bank[pl.ds(at * rows + 2 * slots, TILE), :] = jnp.zeros((TILE, half), BF16)
    level = lax.axis_index("seq") // 2
    moves = []
    for out, blocks in zip(outs, plan):
        for place, block in enumerate(blocks(level)):
            block = jnp.int32(block)
            move = pltpu.make_async_copy(
                bank.at[pl.ds(pl.multiple_of(block * rows, TILE), rows), :],
                out.at[pl.ds(place * rows, rows), :],
                done.at[len(moves)],
            )
            moves.append((block, move))

    def each(some, early):
        for block, move in some:

            @pl.when((block < 2) == early)
            def _():
                move.start()

    each(moves, True)
    delta_high, delta_low = split_exact(jnp.concatenate(delta_parts, axis=1))
    delta = dot(pick, delta_high, NT) + dot(pick, delta_low, NT)
    dot_high, dot_low = split_exact(jnp.concatenate(dot_parts, axis=1))
    dots[...] = (dot(ones, dot_high, NT) + dot(ones, dot_low, NT))[:1]

    pad = jnp.zeros((PIECE - heads, slots), F32)
    scaled = jnp.where(used, jnp.concatenate([norm[...] * root, pad], axis=0), BIG)
    delta = jnp.where(used, delta, 0.0)
    first = lax.broadcasted_iota(jnp.int32, (PIECE, slots), 0) == 0
    stack = pieces(scaled) + pieces(delta) + [jnp.where(first, 1.0, 0.0)]
    stack.append(jnp.zeros((PIECE * (PIECE - len(stack)), slots), F32))
    stats = jnp.concatenate(stack, axis=0).astype(BF16)
    source = lax.broadcasted_iota(jnp.int32, (PIECE * PIECE, LANES), 0)
    target = lax.broadcasted_iota(jnp.int32, (PIECE * PIECE, LANES), 1)
    piece, head = source // PIECE, source % PIECE

    def ext(first_head):
        local = head - first_head
        taken = (local >= 0) & (local < heads // 2) & (piece < 6)
        column = jnp.where(taken, piece * GROUP + local, -1)
        column = jnp.where(source == 6 * PIECE, ONE, column)
        return dot(stats, (column == target).astype(BF16), TN)

    per = heads // 2
    for at in range(2):
        base = (2 + at) * rows
        bank[pl.ds(base + slots, slots), :] = jnp.concatenate(
            dout_parts[at * per:(at + 1) * per], axis=1
        )
        bank[pl.ds(base + 2 * slots, TILE), :] = pack(ext(at * per))
    each(moves, False)
    for _, move in moves:
        move.wait()


def head_marks(head, is_value):
    lane = lax.broadcasted_iota(jnp.int32, (1, LANES), 1)
    base = (3 * GROUP if is_value else 0) + head
    marked = (lane == base) | (lane == base + GROUP) | (lane == base + 2 * GROUP)
    return jnp.where(marked, -1.0, 0.0).astype(BF16)


def meet(down, movings, stays, positions, heads, mask, emit, add):
    half = movings[0][0].shape[1]
    slots = emit.slots
    head_dim = half // (heads // 2)
    scale = head_dim ** -0.5
    to_log2 = scale * math.log2(math.e)

    def stats(blocks, queries):
        parts = []
        for ref, at, shard in blocks:
            if queries:
                parts.append(unpack(ref[pl.ds(at + 2 * slots, TILE), :]))
            else:
                parts.append(key_ext(positions, shard, slots))
        return jnp.concatenate(parts, axis=0)

    def load(blocks, which, cols):
        parts = [ref[pl.ds(at + which * slots, slots), cols] for ref, at, _ in blocks]
        return jnp.concatenate(parts, axis=0)

    moving_ext, stay_ext = stats(movings, down), stats(stays, not down)
    for h in range(heads // 2):
        cols = pl.ds(h * head_dim, head_dim)
        m1, m2 = load(movings, 0, cols), load(movings, 1, cols)
        r1, r2 = load(stays, 0, cols), load(stays, 1, cols)
        key_mark, value_mark = head_marks(h, False), head_marks(h, True)
        if down:
            m1_ext, m2_ext = moving_ext, moving_ext
            r1_ext = stay_ext + key_mark
            r2_ext = jnp.broadcast_to(value_mark, stay_ext.shape)
        else:
            m1_ext = moving_ext + key_mark
            m2_ext = jnp.broadcast_to(value_mark, moving_ext.shape)
            r1_ext, r2_ext = stay_ext, stay_ext
        scores = dot(
            jnp.concatenate([m1, m1_ext], axis=1), jnp.concatenate([r1, r1_ext], axis=1), NT
        )
        if mask is not None:
            scores = jnp.where(mask, scores, -BIG)
        prob = jnp.exp2(scores * to_log2)
        dprob = dot(
            jnp.concatenate([m2, m2_ext], axis=1), jnp.concatenate([r2, r2_ext], axis=1), NT
        )
        dscore = (prob * dprob * scale).astype(BF16)
        prob = prob.astype(BF16)
        emit(0, cols, dot(dscore, r1, NN))
        add(0, cols, dot(dscore, m1, TN))
        if down:
            add(1, cols, dot(prob, m2, TN))
        else:
            emit(1, cols, dot(prob, r2, NN))


class Store:
    def __init__(self, slots, targets, fresh, olds=None):
        self.slots, self.targets, self.fresh = slots, targets, fresh
        self.olds = olds or [ref for ref, _ in targets]

    def __call__(self, which, cols, term):
        for i, (ref, base) in enumerate(self.targets):
            rows = pl.ds(base + which * self.slots, self.slots)
            part = term[i * self.slots:(i + 1) * self.slots]
            part = part if self.fresh else self.olds[i][rows, cols] + part
            ref[rows, cols] = part.astype(ref.dtype)


def causal(down, slots, shard=None):
    shape = (slots, slots if shard is None else 2 * slots)
    row = lax.broadcasted_iota(jnp.int32, shape, 0)
    place = lax.broadcasted_iota(jnp.int32, shape, 1)
    if shard is not None:
        place = jnp.where(place < slots, place, slots - shard % 2 * (slots + 1))
    return place <= row if down else place >= row


def router_part(positions, logit, dots, slots, shard):
    gate = jax.nn.sigmoid(logit[...])
    lane = lax.broadcasted_iota(jnp.int32, (1, slots), 1).astype(F32)
    used = lane < used_slots(positions, shard, slots)
    return jnp.where(used, gate * (1.0 - gate) * dots, 0.0)


FOUR_PLAN = (
    lambda level: [jnp.where(level < 2, 0, 2), jnp.where(level < 2, 1, 3)],
    lambda level: [jnp.where(level < 2, 2, 0), jnp.where(level < 2, 3, 1)],
    lambda level: [jnp.where(level % 2 == 0, 0, 3)],
    lambda level: [jnp.where(level < 2, 1, 2)],
)


def four_home_kernel(heads, positions, mine, own, turn, grads, own_total):
    slots = grads.shape[0] // 4
    rows = 2 * slots + TILE
    shard = lax.axis_index("seq")
    turn[...] = jnp.zeros(turn.shape, F32)
    for down in (True, False):

        @pl.when((shard < 4) == down)
        def _():
            for at in range(2):
                base = 2 * slots * at
                meet(
                    down, [(mine, at * rows, shard)], [(own, at * rows, shard)],
                    positions, heads, causal(down, slots),
                    Store(slots, [(grads, base)], True),
                    Store(slots, [(own_total, base)], True),
                )


def meets_pair(shard):
    return (shard % 2 == 1) == (shard < 4)


def follow_kernel(block, after, out):
    pass


def four_pair_kernel(
    heads, positions, after, mine, other, turn, grads_pair, met_total, early, early_total
):
    slots = early.shape[0] // 2
    rows = 2 * slots + TILE
    shard = lax.axis_index("seq")
    meets = meets_pair(shard)
    turn[...] = after[...]
    for level in range(4):

        @pl.when(meets & (shard // 2 == level))
        def _():
            for at in range(2):
                met = at == (1, 0, 1, 0)[level]
                meet(
                    level < 2, [(mine, at * rows, shard)], [(other, at * rows, shard ^ 1)],
                    positions, heads, None,
                    Store(slots, [(grads_pair, 2 * slots * at)], True),
                    Store(slots, [(met_total if met else early_total, 0)], True),
                )
            early[...] = early_total[...].astype(BF16)

    @pl.when(jnp.logical_not(meets))
    def _():
        early[...] = jnp.zeros(early.shape, BF16)


def four_skip_kernel(
    heads, positions, after, mine, own, other, near, skip,
    turn, own_near, other_near, back, near_total, grads_guest, skip_part
):
    slots = back.shape[0] // 2
    rows = 2 * slots + TILE
    shard = lax.axis_index("seq")
    turn[...] = after[...]
    for level in range(4):
        at = (1, 0, 1, 0)[level]

        @pl.when(shard // 2 == level)
        def _():
            pair = [(own, at * rows, shard), (other, at * rows, shard ^ 1)]
            totals = Store(slots, [(own_near, 0), (other_near, 0)], True)
            guest = [(near, 0, shard - 2)]
            if level in (0, 3):
                meet(
                    level == 0, guest, pair, positions, heads, None,
                    Store(slots, [(back, 0)], True), totals,
                )
                return
            far = [(skip, 0, shard - 4)]
            meet(
                level == 1, [(mine, at * rows, shard)] + far, guest, positions, heads, None,
                Store(slots, [(grads_guest, 0), (skip_part, 0)], True),
                Store(slots, [(near_total, 0)], True),
            )
            meet(
                level == 1, far, pair, positions, heads, None,
                Store(slots, [(skip_part, 0)], False), totals,
            )


def four_near_kernel(
    heads, positions, after, dots, dots_near, near, middle, back, near_total,
    dots_sum, near_low, middle_part
):
    slots = near_low.shape[0] // 2
    shard = lax.axis_index("seq")
    dots_sum[...] = dots[...] + dots_near[...]
    for level in range(4):

        @pl.when(shard // 2 == level)
        def _():
            if level in (0, 3):
                near_low[...] = back[...]
                return
            meet(
                level == 1, [(middle, 0, shard - 2)], [(near, 0, shard - 2)],
                positions, heads, None,
                Store(slots, [(middle_part, 0)], True),
                Store(slots, [(near_low, 0)], False, [near_total]),
            )


def four_last_kernel(
    heads, positions, dots_in, mine, own, other, cross, skip, middle,
    grads_in, skip_in, middle_in, met_pair, own_in, other_in,
    dots, grads_guest, skip_back, cross_low, middle_back, late, own_near,
    middle_part, other_near,
):
    slots = grads_in.shape[0] // 2
    rows = 2 * slots + TILE
    shard = lax.axis_index("seq")
    meets = meets_pair(shard)
    dots[...] = dots_in[...]
    for level in range(4):
        at = (1, 0, 1, 0)[level]

        @pl.when(shard // 2 == level)
        def _():
            if level in (0, 3):
                own_near[...] = own_in[...]
                other_near[...] = other_in[...]
            else:
                far = [(skip, 0, shard - 4), (middle, 0, shard - 2)]
                meet(
                    level == 1, far[1:], [(own, at * rows, shard), (other, at * rows, shard ^ 1)],
                    positions, heads, None,
                    Store(slots, [(middle_part, 0)], False, [middle_in]),
                    Store(slots, [(own_near, 0), (other_near, 0)], False, [own_in, other_in]),
                )
                meet(
                    level == 1, [(mine, at * rows, shard)] + far, [(cross, 0, (shard - 2) ^ 1)],
                    positions, heads, None,
                    Store(
                        slots, [(grads_guest, 0), (skip_back, 0), (middle_back, 0)], False,
                        [grads_in, skip_in, middle_part],
                    ),
                    Store(slots, [(cross_low, 0)], True),
                )

    late[...] = (other_near[...] + jnp.where(meets, met_pair[...], 0.0)).astype(BF16)


def four_sum_kernel(heads, grads, grads_pair, own, near, early, moving_sum, staying_sum):
    slots = grads.shape[0] // 4
    shard = lax.axis_index("seq")
    meets = meets_pair(shard)
    for level in range(4):

        @pl.when(shard // 2 == level)
        def _():
            for at in range(2):
                part = pl.ds(2 * slots * at, 2 * slots)
                moving = grads[part, :] + jnp.where(meets, grads_pair[part, :], 0.0)
                staying = own[part, :]
                if at != (1, 0, 1, 0)[level]:
                    staying = staying + early[...].astype(F32)
                    if level in (1, 2):
                        moving = moving + near[...].astype(F32)
                    else:
                        staying = staying + near[...].astype(F32)
                moving_sum[part, :] = moving
                staying_sum[part, :] = staying


def four_join_kernel(
    heads, positions, logit, dots, dots_far, moving_sum, staying_sum, grads_guest, own_near,
    middle, cross, skip, late, query_grad, key_grad, value_grad, router
):
    slots, half = moving_sum.shape[0] // 4, moving_sum.shape[1]
    shard = lax.axis_index("seq")
    router[...] = router_part(positions, logit, dots[...] + dots_far[...], slots, shard)
    for level in range(4):
        inner = level in (1, 2)

        @pl.when(shard // 2 == level)
        def _():
            if level < 2:
                moving, staying = [query_grad], [key_grad, value_grad]
            else:
                moving, staying = [key_grad, value_grad], [query_grad]
            for at in range(2):
                cols = pl.ds(at * half, half)
                met = at == (1, 0, 1, 0)[level]
                plus = [grads_guest] if inner and met else []
                if inner:
                    extra = [own_near, late] if met else [middle]
                else:
                    extra = [own_near, skip, late] if met else [cross]
                for outs, base, more in ((moving, moving_sum, plus), (staying, staying_sum, extra)):
                    for which, out in enumerate(outs):
                        rows = pl.ds((2 * at + which) * slots, slots)
                        total = base[rows, :]
                        for ref in more:
                            total = total + ref[pl.ds(which * slots, slots), :].astype(F32)
                        out[:, cols] = total.astype(BF16)


def four_levels(prep, shape, positions, logit, slots, heads, width):
    double, block, total = shape(4 * slots + 2 * TILE), shape(2 * slots + TILE), shape(2 * slots, F32)
    totals, low = shape(4 * slots, F32), shape(2 * slots)
    own, mine, near_send, far_send, dots = prep(FOUR_PLAN, [double, double, block, block])
    def pairs(levels, flip=0):
        return [(2 * a + c, 2 * b + (c ^ flip)) for a, b in levels for c in range(2)]

    near = lax.ppermute(near_send, "seq", pairs([(0, 1), (1, 0), (2, 3), (3, 2)]))
    other = lax.ppermute(own, "seq", pairs([(i, i) for i in range(4)], 1))
    skip = lax.ppermute(far_send, "seq", pairs([(0, 2), (3, 1)]))
    middle = lax.ppermute(far_send, "seq", pairs([(1, 2), (2, 1)]))
    row = shape(1, F32, slots)
    turn, grads, own_total = call(
        functools.partial(four_home_kernel, heads),
        [row] + [totals] * 2,
        positions, mine, own,
    )
    (near,) = call(
        follow_kernel, [block], near, turn, ins=[pl.ANY, pltpu.VMEM], outs=[pl.ANY], aliases={0: 0}
    )
    cross = lax.ppermute(near, "seq", pairs([(1, 1), (2, 2)], 1))
    turn, grads_pair, met_pair, early = call(
        functools.partial(four_pair_kernel, heads),
        [row, totals, total, low],
        positions, turn, mine, other,
        scratch=[pltpu.VMEM(total.shape, F32)],
    )
    early = lax.ppermute(early, "seq", pairs([(i, i) for i in range(4)], 1))
    (early,) = call(
        follow_kernel, [low], early, turn, ins=[pl.ANY, pltpu.VMEM], outs=[pl.ANY],
        aliases={0: 0}, flops=SUM_FLOPS,
    )
    turn, own_near, other_near, step_back, near_total, grads_guest, skip_part = call(
        functools.partial(four_skip_kernel, heads),
        [row, total, total, low, total, total, total],
        positions, turn, mine, own, other, near, skip,
    )
    dots_near = lax.ppermute(dots, "tp", [(i, i ^ 1) for i in range(4)])
    dots, near_low, middle_part = call(
        functools.partial(four_near_kernel, heads),
        [row, low, total],
        positions, turn, dots, dots_near, near, middle, step_back, near_total,
    )
    near = lax.ppermute(near_low, "seq", pairs([(0, 1), (1, 0), (2, 3), (3, 2)]))
    dots, grads_guest, skip_back, cross_low, middle_back, late, own_near = call(
        functools.partial(four_last_kernel, heads),
        [row, total, low, low, low, low, total],
        positions, dots, mine, own, other, cross, skip, middle,
        grads_guest, skip_part, middle_part, met_pair, own_near, other_near,
        scratch=[pltpu.VMEM(total.shape, F32)] * 2,
    )
    dots_far = lax.ppermute(dots, "tp", [(i, i ^ 2) for i in range(4)])
    skip = lax.ppermute(skip_back, "seq", pairs([(2, 0), (1, 3)]))
    cross = lax.ppermute(cross_low, "seq", pairs([(1, 0), (2, 3)], 1))
    middle = lax.ppermute(middle_back, "seq", pairs([(1, 2), (2, 1)]))
    late = lax.ppermute(late, "seq", pairs([(i, i) for i in range(4)], 1))
    moving_sum, staying_sum = call(
        functools.partial(four_sum_kernel, heads),
        [totals] * 2,
        grads, grads_pair, own_total, near, early,
        flops=SUM_FLOPS,
    )
    return call(
        functools.partial(four_join_kernel, heads),
        [shape(slots, BF16, width)] * 3 + [row],
        positions, logit, dots, dots_far, moving_sum, staying_sum, grads_guest, own_near,
        middle, cross, skip, late,
    )


def ring_plan(levels):
    sends = [
        lambda level, step=step: [jnp.where(level >= step, 2, 1)] for step in range(1, levels)
    ]
    return (lambda level: [0, 3], lambda level: [2], lambda level: [1], *sends)


def ring_home_kernel(
    heads, positions, logit, dots, down, up, own, other, grads, own_total, other_total, router
):
    slots = grads.shape[0] // 3
    rows = 2 * slots + TILE
    shard = lax.axis_index("seq")
    for goes_down, mine, at, base, stay_base in ((True, down, 0, 0, 0), (False, up, rows, 1, 2)):
        meet(
            goes_down, [(mine, 0, shard)], [(own, at, shard), (other, at, shard ^ 1)],
            positions, heads, causal(goes_down, slots, shard),
            Store(slots, [(grads, base * slots)], True),
            Store(slots, [(own_total, stay_base * slots), (other_total, stay_base * slots)], True),
        )
    router[...] = router_part(positions, logit, dots[...], slots, shard)


def ring_away_kernel(
    step, levels, heads, positions, own, other, block, own_in, other_in,
    back, own_total, other_total, *low
):
    slots = own_in.shape[0] // 3
    own_total[...] = own_in[...]
    other_total[...] = other_in[...]
    rows = 2 * slots + TILE
    shard = lax.axis_index("seq")
    for goes_down, at, base in ((True, 0, 0), (False, rows, 2 * slots)):

        @pl.when((shard // 2 + step < levels) == goes_down)
        def _():
            meet(
                goes_down, [(block, 0, shard + 2 * (step - levels))],
                [(own, at, shard), (other, at, shard ^ 1)],
                positions, heads, None,
                Store(slots, [(back, 0)], True),
                Store(slots, [(own_total, base), (other_total, base)], False),
            )

    for ref in low:
        ref[...] = other_total[...].astype(BF16)


def ring_join_kernel(heads, grads, own, other, *refs):
    back, (query_grad, key_grad, value_grad) = refs[:-3], refs[-3:]
    slots, half = grads.shape[0] // 3, grads.shape[1]
    level = lax.axis_index("seq") // 2
    low, high = pl.ds(0, half), pl.ds(half, half)
    parts = [pl.ds(i * slots, slots) for i in range(3)]
    stays = [(own[rows, :] + other[rows, :].astype(F32)).astype(BF16) for rows in parts]
    key_grad[:, low], value_grad[:, low], query_grad[:, high] = stays
    query_sum, key_sum, value_sum = [grads[rows, :] for rows in parts]
    for step, ref in enumerate(back, 1):
        went_down = level >= step
        first, second = ref[parts[0], :].astype(F32), ref[parts[1], :].astype(F32)
        query_sum = query_sum + jnp.where(went_down, first, 0.0)
        key_sum = key_sum + jnp.where(went_down, 0.0, first)
        value_sum = value_sum + jnp.where(went_down, 0.0, second)
    query_grad[:, low] = query_sum.astype(BF16)
    key_grad[:, high] = key_sum.astype(BF16)
    value_grad[:, high] = value_sum.astype(BF16)


def ring_levels(prep, shape, positions, logit, slots, heads, width, shards):
    levels = shards // 2
    block, total = shape(2 * slots + TILE), shape(3 * slots, F32)
    own, down, up, *sends, dots = prep(
        ring_plan(levels), [shape(4 * slots + 2 * TILE)] + [block] * (levels + 1)
    )
    pair = [(s, s ^ 1) for s in range(shards)]
    arrived = [
        lax.ppermute(send, "seq", [(s, (s - 2 * step) % shards) for s in range(shards)])
        for step, send in enumerate(sends, 1)
    ]
    other = lax.ppermute(own, "seq", pair)
    dots = sum_over(dots, "tp")
    grads, own_total, other_total, router = call(
        functools.partial(ring_home_kernel, heads),
        [total] * 3 + [shape(1, F32, slots)],
        positions, logit, dots, down, up, own, other,
    )
    backs, low = [], [other_total.astype(BF16)]
    for step, arrival in enumerate(arrived, 1):
        back, own_total, other_total, *low = call(
            functools.partial(ring_away_kernel, step, levels, heads),
            [shape(2 * slots), total, total] + [shape(3 * slots)] * (step == levels - 1),
            positions, own, other, arrival, own_total, other_total,
            )
        backs.append(
            lax.ppermute(back, "seq", [(s, (s + 2 * step) % shards) for s in range(shards)])
        )
    outs = call(
        functools.partial(ring_join_kernel, heads),
        [shape(slots, BF16, width)] * 3,
        grads, own_total, lax.ppermute(low[0], "seq", pair), *backs,
    )
    return *outs, router


def call(kernel, out_shape, *args, scratch=(), ins=None, outs=None, limit=VMEM, flops=1024, aliases=None):
    ins = ins or [pltpu.VMEM] * len(args)
    outs = outs or [pltpu.VMEM] * len(out_shape)
    return pl.pallas_call(
        kernel,
        out_shape=out_shape,
        in_specs=[pl.BlockSpec(memory_space=space) for space in ins],
        out_specs=[pl.BlockSpec(memory_space=space) for space in outs],
        scratch_shapes=list(scratch),
        input_output_aliases=aliases or {},
        compiler_params=pltpu.CompilerParams(vmem_limit_bytes=limit),
        cost_estimate=pl.CostEstimate(flops=flops, bytes_accessed=1024, transcendentals=0),
    )(*args)


def sum_over(values, axis):
    size = lax.axis_size(axis)
    if size & (size - 1):
        return lax.psum(values, axis)
    reach = 1
    while reach < size:
        pairs = [(i, i ^ reach) for i in range(size)]
        values = values + lax.ppermute(values, axis, pairs)
        reach *= 2
    return values


def body(
    query_proj, key_proj, value_proj, attn_output, out_grad, log_norm, router_logit, keep_positions
):
    slots, width = query_proj.shape
    heads = log_norm.shape[1]
    half = width // 2
    shards = lax.axis_size("seq")
    logit = router_logit.reshape(1, slots)
    positions = keep_positions.reshape(-1, LANES)

    def shape(rows, dtype=BF16, columns=half):
        return jax.ShapeDtypeStruct((rows, columns), dtype)

    sources = (
        attn_output, out_grad, logit, log_norm.T, positions, query_proj, key_proj, value_proj
    )

    def prep(plan, shapes):
        dots, *outs = call(
            functools.partial(prep_kernel, plan, heads),
            [shape(1, F32, slots)] + shapes,
            *sources,
            scratch=[pltpu.VMEM(a.shape, a.dtype) for a in sources[:5]]
            + [pltpu.VMEM((4 * (2 * slots + TILE), half), BF16)]
            + [pltpu.SemaphoreType.DMA((11,)), pltpu.SemaphoreType.DMA((2 * len(plan),))],
            ins=[pltpu.HBM] * len(sources),
            outs=[pltpu.VMEM] + [pltpu.HBM] * len(shapes),
            limit=PREP_VMEM,
        )
        return *outs, dots

    if shards == 8 and lax.axis_size("tp") == 4:
        query_grad, key_grad, value_grad, router = four_levels(
            prep, shape, positions, logit, slots, heads, width
        )
    else:
        query_grad, key_grad, value_grad, router = ring_levels(
            prep, shape, positions, logit, slots, heads, width, shards
        )
    return query_grad, key_grad, value_grad, router.reshape(slots)


def solution(mesh):
    wide = P("seq", "tp")
    return jax.shard_map(
        body,
        mesh=mesh,
        in_specs=(wide,) * 6 + (P("seq"), P()),
        out_specs=(wide, wide, wide, P("seq")),
        check_vma=False,
    )
```

```python
import functools
import math

import jax
import jax.numpy as jnp
from jax import lax
from jax.experimental import pallas as pl
from jax.experimental.pallas import tpu as pltpu
from jax.sharding import PartitionSpec as P


LANES = 128
PIECE = 8
GROUP = 4
ONE = 6 * GROUP
PACK = 4
TILE = 16
BIG = 1e30
VMEM = 24 * 1024 * 1024
SUM_FLOPS = 5_000_000_000
PREP_VMEM = 63 * 1024 * 1024
F32 = jnp.float32
BF16 = jnp.bfloat16
NT = (((1,), (1,)), ((), ()))
NN = (((1,), (0,)), ((), ()))
TN = (((0,), (0,)), ((), ()))


def dot(left, right, dims):
    return lax.dot_general(left, right, dims, preferred_element_type=F32)


def pieces(rows):
    high = rows.astype(BF16).astype(F32)
    rest = rows - high
    middle = rest.astype(BF16).astype(F32)
    return [high, middle, rest - middle]


def split_exact(product):
    high = product.astype(BF16)
    return high, (product - high.astype(F32)).astype(BF16)


def used_slots(positions, shard, slots):
    table = positions[...]
    place = lax.broadcasted_iota(jnp.int32, table.shape, 0) * LANES
    place = place + lax.broadcasted_iota(jnp.int32, table.shape, 1)
    mine = (place >= shard * slots) & (place < (shard + 1) * slots) & (table >= 0)
    count = jnp.sum(jnp.where(mine, 1.0, 0.0), axis=1, keepdims=True)
    return jnp.sum(count, axis=0, keepdims=True)


def pack(ext):
    quarter = ext.shape[0] // PACK
    total = ext[:quarter]
    for part in range(1, PACK):
        rows = ext[part * quarter:(part + 1) * quarter]
        total = total + pltpu.roll(rows, part * LANES // PACK, 1)
    groups = [total[at:at + TILE] for at in range(0, quarter, TILE)]
    return jnp.concatenate(groups, axis=1).astype(BF16)


def unpack(packed):
    wide = packed.astype(F32)
    groups = [wide[:, at:at + LANES] for at in range(0, wide.shape[1], LANES)]
    total = jnp.concatenate(groups, axis=0)
    parts = [total]
    for part in range(1, PACK):
        parts.append(pltpu.roll(total, LANES - part * LANES // PACK, 1))
    return jnp.concatenate(parts, axis=0).astype(BF16)


def key_ext(positions, shard, slots):
    count = used_slots(positions, shard, slots)
    slot = lax.broadcasted_iota(jnp.int32, (slots, LANES), 0).astype(F32)
    lane = lax.broadcasted_iota(jnp.int32, (slots, LANES), 1)
    return jnp.where((lane == ONE) & (slot >= count), -BIG, 0.0).astype(BF16)


def prep_kernel(plan, heads, *refs):
    sources, (query, key, value), rest = refs[:5], refs[5:8], refs[8:]
    dots, outs, rest = rest[0], rest[1:len(plan) + 1], rest[len(plan) + 1:]
    held, (bank, sems, done) = rest[:5], rest[5:]
    output, grad, logit, norm, positions = held
    slots, width = grad.shape
    half = width // 2
    rows = 2 * slots + TILE
    copies = [
        pltpu.make_async_copy(source, dest, sems.at[i])
        for i, (source, dest) in enumerate(zip(sources, held))
    ]
    for at in range(2):
        for source, base in ((key, at), (value, at + 0.5), (query, at + 2)):
            first = int(base) * rows + (slots if base % 1 else 0)
            copies.append(
                pltpu.make_async_copy(
                    source.at[:, pl.ds(at * half, half)],
                    bank.at[pl.ds(first, slots), :],
                    sems.at[len(copies)],
                )
            )
    for copy in copies:
        copy.start()
    for copy in copies[:5]:
        copy.wait()
    head_dim = width // heads
    root = math.sqrt(head_dim)
    shard = lax.axis_index("seq")
    count = used_slots(positions, shard, slots)
    lane = lax.broadcasted_iota(jnp.int32, (PIECE, slots), 1).astype(F32)
    used = lane < count
    gate_row = jax.nn.sigmoid(logit[...])
    gate = jnp.transpose(jnp.broadcast_to(gate_row, (LANES, slots)))
    head_of = lax.broadcasted_iota(jnp.int32, (PIECE, width), 1) // head_dim
    head_row = lax.broadcasted_iota(jnp.int32, (PIECE, width), 0)
    pick = (head_of == head_row).astype(BF16)
    ones = jnp.ones((PIECE, width), BF16)
    dout_parts, delta_parts, dot_parts = [], [], []
    for h in range(heads):
        cols = pl.ds(h * head_dim, head_dim)
        wide = grad[:, cols].astype(F32)
        out = output[:, cols].astype(F32)
        dout = (wide * gate).astype(BF16)
        dout_parts.append(dout)
        delta_parts.append(dout.astype(F32) * out)
        dot_parts.append(wide * out)
    for copy in copies[5:]:
        copy.wait()
    for at in range(2):
        bank[pl.ds(at * rows + 2 * slots, TILE), :] = jnp.zeros((TILE, half), BF16)
    level = lax.axis_index("seq") // 2
    moves = []
    for out, blocks in zip(outs, plan):
        for place, block in enumerate(blocks(level)):
            block = jnp.int32(block)
            move = pltpu.make_async_copy(
                bank.at[pl.ds(pl.multiple_of(block * rows, TILE), rows), :],
                out.at[pl.ds(place * rows, rows), :],
                done.at[len(moves)],
            )
            moves.append((block, move))

    def each(some, early):
        for block, move in some:

            @pl.when((block < 2) == early)
            def _():
                move.start()

    each(moves, True)
    delta_high, delta_low = split_exact(jnp.concatenate(delta_parts, axis=1))
    delta = dot(pick, delta_high, NT) + dot(pick, delta_low, NT)
    dot_high, dot_low = split_exact(jnp.concatenate(dot_parts, axis=1))
    dots[...] = (dot(ones, dot_high, NT) + dot(ones, dot_low, NT))[:1]

    pad = jnp.zeros((PIECE - heads, slots), F32)
    scaled = jnp.where(used, jnp.concatenate([norm[...] * root, pad], axis=0), BIG)
    delta = jnp.where(used, delta, 0.0)
    first = lax.broadcasted_iota(jnp.int32, (PIECE, slots), 0) == 0
    stack = pieces(scaled) + pieces(delta) + [jnp.where(first, 1.0, 0.0)]
    stack.append(jnp.zeros((PIECE * (PIECE - len(stack)), slots), F32))
    stats = jnp.concatenate(stack, axis=0).astype(BF16)
    source = lax.broadcasted_iota(jnp.int32, (PIECE * PIECE, LANES), 0)
    target = lax.broadcasted_iota(jnp.int32, (PIECE * PIECE, LANES), 1)
    piece, head = source // PIECE, source % PIECE

    def ext(first_head):
        local = head - first_head
        taken = (local >= 0) & (local < heads // 2) & (piece < 6)
        column = jnp.where(taken, piece * GROUP + local, -1)
        column = jnp.where(source == 6 * PIECE, ONE, column)
        return dot(stats, (column == target).astype(BF16), TN)

    per = heads // 2
    for at in range(2):
        base = (2 + at) * rows
        bank[pl.ds(base + slots, slots), :] = jnp.concatenate(
            dout_parts[at * per:(at + 1) * per], axis=1
        )
        bank[pl.ds(base + 2 * slots, TILE), :] = pack(ext(at * per))
    each(moves, False)
    for _, move in moves:
        move.wait()


def head_marks(head, is_value):
    lane = lax.broadcasted_iota(jnp.int32, (1, LANES), 1)
    base = (3 * GROUP if is_value else 0) + head
    marked = (lane == base) | (lane == base + GROUP) | (lane == base + 2 * GROUP)
    return jnp.where(marked, -1.0, 0.0).astype(BF16)


def meet(down, movings, stays, positions, heads, mask, emit, add):
    half = movings[0][0].shape[1]
    slots = emit.slots
    head_dim = half // (heads // 2)
    scale = head_dim ** -0.5
    to_log2 = scale * math.log2(math.e)

    def stats(blocks, queries):
        parts = []
        for ref, at, shard in blocks:
            if queries:
                parts.append(unpack(ref[pl.ds(at + 2 * slots, TILE), :]))
            else:
                parts.append(key_ext(positions, shard, slots))
        return jnp.concatenate(parts, axis=0)

    def load(blocks, which, cols):
        parts = [ref[pl.ds(at + which * slots, slots), cols] for ref, at, _ in blocks]
        return jnp.concatenate(parts, axis=0)

    moving_ext, stay_ext = stats(movings, down), stats(stays, not down)
    for h in range(heads // 2):
        cols = pl.ds(h * head_dim, head_dim)
        m1, m2 = load(movings, 0, cols), load(movings, 1, cols)
        r1, r2 = load(stays, 0, cols), load(stays, 1, cols)
        key_mark, value_mark = head_marks(h, False), head_marks(h, True)
        if down:
            m1_ext, m2_ext = moving_ext, moving_ext
            r1_ext = stay_ext + key_mark
            r2_ext = jnp.broadcast_to(value_mark, stay_ext.shape)
        else:
            m1_ext = moving_ext + key_mark
            m2_ext = jnp.broadcast_to(value_mark, moving_ext.shape)
            r1_ext, r2_ext = stay_ext, stay_ext
        scores = dot(
            jnp.concatenate([m1, m1_ext], axis=1), jnp.concatenate([r1, r1_ext], axis=1), NT
        )
        if mask is not None:
            scores = jnp.where(mask, scores, -BIG)
        prob = jnp.exp2(scores * to_log2)
        dprob = dot(
            jnp.concatenate([m2, m2_ext], axis=1), jnp.concatenate([r2, r2_ext], axis=1), NT
        )
        dscore = (prob * dprob * scale).astype(BF16)
        prob = prob.astype(BF16)
        emit(0, cols, dot(dscore, r1, NN))
        add(0, cols, dot(dscore, m1, TN))
        if down:
            add(1, cols, dot(prob, m2, TN))
        else:
            emit(1, cols, dot(prob, r2, NN))


class Store:
    def __init__(self, slots, targets, fresh, olds=None):
        self.slots, self.targets, self.fresh = slots, targets, fresh
        self.olds = olds or [ref for ref, _ in targets]

    def __call__(self, which, cols, term):
        for i, (ref, base) in enumerate(self.targets):
            rows = pl.ds(base + which * self.slots, self.slots)
            part = term[i * self.slots:(i + 1) * self.slots]
            part = part if self.fresh else self.olds[i][rows, cols] + part
            ref[rows, cols] = part.astype(ref.dtype)


def causal(down, slots, shard=None):
    shape = (slots, slots if shard is None else 2 * slots)
    row = lax.broadcasted_iota(jnp.int32, shape, 0)
    place = lax.broadcasted_iota(jnp.int32, shape, 1)
    if shard is not None:
        place = jnp.where(place < slots, place, slots - shard % 2 * (slots + 1))
    return place <= row if down else place >= row


def router_part(positions, logit, dots, slots, shard):
    gate = jax.nn.sigmoid(logit[...])
    lane = lax.broadcasted_iota(jnp.int32, (1, slots), 1).astype(F32)
    used = lane < used_slots(positions, shard, slots)
    return jnp.where(used, gate * (1.0 - gate) * dots, 0.0)


FOUR_PLAN = (
    lambda level: [jnp.where(level < 2, 0, 2), jnp.where(level < 2, 1, 3)],
    lambda level: [jnp.where(level < 2, 2, 0), jnp.where(level < 2, 3, 1)],
    lambda level: [jnp.where(level % 2 == 0, 0, 3)],
    lambda level: [jnp.where(level < 2, 1, 2)],
)


def four_home_kernel(heads, positions, mine, own, turn, grads, own_total):
    slots = grads.shape[0] // 4
    rows = 2 * slots + TILE
    shard = lax.axis_index("seq")
    turn[...] = jnp.zeros(turn.shape, F32)
    for down in (True, False):

        @pl.when((shard < 4) == down)
        def _():
            for at in range(2):
                base = 2 * slots * at
                meet(
                    down, [(mine, at * rows, shard)], [(own, at * rows, shard)],
                    positions, heads, causal(down, slots),
                    Store(slots, [(grads, base)], True),
                    Store(slots, [(own_total, base)], True),
                )


def meets_pair(shard):
    return (shard % 2 == 1) == (shard < 4)


def follow_kernel(block, after, out):
    pass


def four_pair_kernel(
    heads, positions, after, mine, other, turn, grads_pair, met_total, early, early_total
):
    slots = early.shape[0] // 2
    rows = 2 * slots + TILE
    shard = lax.axis_index("seq")
    meets = meets_pair(shard)
    turn[...] = after[...]
    for level in range(4):

        @pl.when(meets & (shard // 2 == level))
        def _():
            for at in range(2):
                met = at == (1, 0, 1, 0)[level]
                meet(
                    level < 2, [(mine, at * rows, shard)], [(other, at * rows, shard ^ 1)],
                    positions, heads, None,
                    Store(slots, [(grads_pair, 2 * slots * at)], True),
                    Store(slots, [(met_total if met else early_total, 0)], True),
                )
            early[...] = early_total[...].astype(BF16)

    @pl.when(jnp.logical_not(meets))
    def _():
        early[...] = jnp.zeros(early.shape, BF16)


def four_skip_kernel(
    heads, positions, after, mine, own, other, near, skip,
    turn, own_near, other_near, back, near_total, grads_guest, skip_part
):
    slots = back.shape[0] // 2
    rows = 2 * slots + TILE
    shard = lax.axis_index("seq")
    turn[...] = after[...]
    for level in range(4):
        at = (1, 0, 1, 0)[level]

        @pl.when(shard // 2 == level)
        def _():
            pair = [(own, at * rows, shard), (other, at * rows, shard ^ 1)]
            totals = Store(slots, [(own_near, 0), (other_near, 0)], True)
            guest = [(near, 0, shard - 2)]
            if level in (0, 3):
                meet(
                    level == 0, guest, pair, positions, heads, None,
                    Store(slots, [(back, 0)], True), totals,
                )
                return
            far = [(skip, 0, shard - 4)]
            meet(
                level == 1, [(mine, at * rows, shard)] + far, guest, positions, heads, None,
                Store(slots, [(grads_guest, 0), (skip_part, 0)], True),
                Store(slots, [(near_total, 0)], True),
            )
            meet(
                level == 1, far, pair, positions, heads, None,
                Store(slots, [(skip_part, 0)], False), totals,
            )


def four_near_kernel(
    heads, positions, after, dots, dots_near, near, middle, back, near_total,
    dots_sum, near_low, middle_part
):
    slots = near_low.shape[0] // 2
    shard = lax.axis_index("seq")
    dots_sum[...] = dots[...] + dots_near[...]
    for level in range(4):

        @pl.when(shard // 2 == level)
        def _():
            if level in (0, 3):
                near_low[...] = back[...]
                return
            meet(
                level == 1, [(middle, 0, shard - 2)], [(near, 0, shard - 2)],
                positions, heads, None,
                Store(slots, [(middle_part, 0)], True),
                Store(slots, [(near_low, 0)], False, [near_total]),
            )


def four_last_kernel(
    heads, positions, dots_in, mine, own, other, cross, skip, middle,
    grads_in, skip_in, middle_in, met_pair, own_in, other_in,
    dots, grads_guest, skip_back, cross_low, middle_back, late, own_near,
    middle_part, other_near,
):
    slots = grads_in.shape[0] // 2
    rows = 2 * slots + TILE
    shard = lax.axis_index("seq")
    meets = meets_pair(shard)
    dots[...] = dots_in[...]
    for level in range(4):
        at = (1, 0, 1, 0)[level]

        @pl.when(shard // 2 == level)
        def _():
            if level in (0, 3):
                own_near[...] = own_in[...]
                other_near[...] = other_in[...]
            else:
                far = [(skip, 0, shard - 4), (middle, 0, shard - 2)]
                meet(
                    level == 1, far[1:], [(own, at * rows, shard), (other, at * rows, shard ^ 1)],
                    positions, heads, None,
                    Store(slots, [(middle_part, 0)], False, [middle_in]),
                    Store(slots, [(own_near, 0), (other_near, 0)], False, [own_in, other_in]),
                )
                meet(
                    level == 1, [(mine, at * rows, shard)] + far, [(cross, 0, (shard - 2) ^ 1)],
                    positions, heads, None,
                    Store(
                        slots, [(grads_guest, 0), (skip_back, 0), (middle_back, 0)], False,
                        [grads_in, skip_in, middle_part],
                    ),
                    Store(slots, [(cross_low, 0)], True),
                )

    late[...] = (other_near[...] + jnp.where(meets, met_pair[...], 0.0)).astype(BF16)


def four_sum_kernel(heads, grads, grads_pair, own, near, early, moving_sum, staying_sum):
    slots = grads.shape[0] // 4
    shard = lax.axis_index("seq")
    meets = meets_pair(shard)
    for level in range(4):

        @pl.when(shard // 2 == level)
        def _():
            for at in range(2):
                part = pl.ds(2 * slots * at, 2 * slots)
                moving = grads[part, :] + jnp.where(meets, grads_pair[part, :], 0.0)
                staying = own[part, :]
                if at != (1, 0, 1, 0)[level]:
                    staying = staying + early[...].astype(F32)
                    if level in (1, 2):
                        moving = moving + near[...].astype(F32)
                    else:
                        staying = staying + near[...].astype(F32)
                moving_sum[part, :] = moving
                staying_sum[part, :] = staying


def four_join_kernel(
    heads, positions, logit, dots, dots_far, moving_sum, staying_sum, grads_guest, own_near,
    middle, cross, skip, late, query_grad, key_grad, value_grad, router
):
    slots, half = moving_sum.shape[0] // 4, moving_sum.shape[1]
    shard = lax.axis_index("seq")
    router[...] = router_part(positions, logit, dots[...] + dots_far[...], slots, shard)
    for level in range(4):
        inner = level in (1, 2)

        @pl.when(shard // 2 == level)
        def _():
            if level < 2:
                moving, staying = [query_grad], [key_grad, value_grad]
            else:
                moving, staying = [key_grad, value_grad], [query_grad]
            for at in range(2):
                cols = pl.ds(at * half, half)
                met = at == (1, 0, 1, 0)[level]
                plus = [grads_guest] if inner and met else []
                if inner:
                    extra = [own_near, late] if met else [middle]
                else:
                    extra = [own_near, skip, late] if met else [cross]
                for outs, base, more in ((moving, moving_sum, plus), (staying, staying_sum, extra)):
                    for which, out in enumerate(outs):
                        rows = pl.ds((2 * at + which) * slots, slots)
                        total = base[rows, :]
                        for ref in more:
                            total = total + ref[pl.ds(which * slots, slots), :].astype(F32)
                        out[:, cols] = total.astype(BF16)


def four_levels(prep, shape, positions, logit, slots, heads, width):
    double, block, total = shape(4 * slots + 2 * TILE), shape(2 * slots + TILE), shape(2 * slots, F32)
    totals, low = shape(4 * slots, F32), shape(2 * slots)
    own, mine, near_send, far_send, dots = prep(FOUR_PLAN, [double, double, block, block])
    def pairs(levels, flip=0):
        return [(2 * a + c, 2 * b + (c ^ flip)) for a, b in levels for c in range(2)]

    near = lax.ppermute(near_send, "seq", pairs([(0, 1), (1, 0), (2, 3), (3, 2)]))
    other = lax.ppermute(own, "seq", pairs([(i, i) for i in range(4)], 1))
    skip = lax.ppermute(far_send, "seq", pairs([(0, 2), (3, 1)]))
    middle = lax.ppermute(far_send, "seq", pairs([(1, 2), (2, 1)]))
    row = shape(1, F32, slots)
    turn, grads, own_total = call(
        functools.partial(four_home_kernel, heads),
        [row] + [totals] * 2,
        positions, mine, own,
    )
    (near,) = call(
        follow_kernel, [block], near, turn, ins=[pl.ANY, pltpu.VMEM], outs=[pl.ANY], aliases={0: 0}
    )
    cross = lax.ppermute(near, "seq", pairs([(1, 1), (2, 2)], 1))
    turn, grads_pair, met_pair, early = call(
        functools.partial(four_pair_kernel, heads),
        [row, totals, total, low],
        positions, turn, mine, other,
        scratch=[pltpu.VMEM(total.shape, F32)],
    )
    early = lax.ppermute(early, "seq", pairs([(i, i) for i in range(4)], 1))
    turn, own_near, other_near, step_back, near_total, grads_guest, skip_part = call(
        functools.partial(four_skip_kernel, heads),
        [row, total, total, low, total, total, total],
        positions, turn, mine, own, other, near, skip,
    )
    dots_near = lax.ppermute(dots, "tp", [(i, i ^ 1) for i in range(4)])
    dots, near_low, middle_part = call(
        functools.partial(four_near_kernel, heads),
        [row, low, total],
        positions, turn, dots, dots_near, near, middle, step_back, near_total,
    )
    near = lax.ppermute(near_low, "seq", pairs([(0, 1), (1, 0), (2, 3), (3, 2)]))
    dots, grads_guest, skip_back, cross_low, middle_back, late, own_near = call(
        functools.partial(four_last_kernel, heads),
        [row, total, low, low, low, low, total],
        positions, dots, mine, own, other, cross, skip, middle,
        grads_guest, skip_part, middle_part, met_pair, own_near, other_near,
        scratch=[pltpu.VMEM(total.shape, F32)] * 2,
    )
    dots_far = lax.ppermute(dots, "tp", [(i, i ^ 2) for i in range(4)])
    skip = lax.ppermute(skip_back, "seq", pairs([(2, 0), (1, 3)]))
    cross = lax.ppermute(cross_low, "seq", pairs([(1, 0), (2, 3)], 1))
    middle = lax.ppermute(middle_back, "seq", pairs([(1, 2), (2, 1)]))
    late = lax.ppermute(late, "seq", pairs([(i, i) for i in range(4)], 1))
    moving_sum, staying_sum = call(
        functools.partial(four_sum_kernel, heads),
        [totals] * 2,
        grads, grads_pair, own_total, near, early,
        flops=SUM_FLOPS,
    )
    return call(
        functools.partial(four_join_kernel, heads),
        [shape(slots, BF16, width)] * 3 + [row],
        positions, logit, dots, dots_far, moving_sum, staying_sum, grads_guest, own_near,
        middle, cross, skip, late,
    )


def ring_plan(levels):
    sends = [
        lambda level, step=step: [jnp.where(level >= step, 2, 1)] for step in range(1, levels)
    ]
    return (lambda level: [0, 3], lambda level: [2], lambda level: [1], *sends)


def ring_home_kernel(
    heads, positions, logit, dots, down, up, own, other, grads, own_total, other_total, router
):
    slots = grads.shape[0] // 3
    rows = 2 * slots + TILE
    shard = lax.axis_index("seq")
    for goes_down, mine, at, base, stay_base in ((True, down, 0, 0, 0), (False, up, rows, 1, 2)):
        meet(
            goes_down, [(mine, 0, shard)], [(own, at, shard), (other, at, shard ^ 1)],
            positions, heads, causal(goes_down, slots, shard),
            Store(slots, [(grads, base * slots)], True),
            Store(slots, [(own_total, stay_base * slots), (other_total, stay_base * slots)], True),
        )
    router[...] = router_part(positions, logit, dots[...], slots, shard)


def ring_away_kernel(
    step, levels, heads, positions, own, other, block, own_in, other_in,
    back, own_total, other_total, *low
):
    slots = own_in.shape[0] // 3
    own_total[...] = own_in[...]
    other_total[...] = other_in[...]
    rows = 2 * slots + TILE
    shard = lax.axis_index("seq")
    for goes_down, at, base in ((True, 0, 0), (False, rows, 2 * slots)):

        @pl.when((shard // 2 + step < levels) == goes_down)
        def _():
            meet(
                goes_down, [(block, 0, shard + 2 * (step - levels))],
                [(own, at, shard), (other, at, shard ^ 1)],
                positions, heads, None,
                Store(slots, [(back, 0)], True),
                Store(slots, [(own_total, base), (other_total, base)], False),
            )

    for ref in low:
        ref[...] = other_total[...].astype(BF16)


def ring_join_kernel(heads, grads, own, other, *refs):
    back, (query_grad, key_grad, value_grad) = refs[:-3], refs[-3:]
    slots, half = grads.shape[0] // 3, grads.shape[1]
    level = lax.axis_index("seq") // 2
    low, high = pl.ds(0, half), pl.ds(half, half)
    parts = [pl.ds(i * slots, slots) for i in range(3)]
    stays = [(own[rows, :] + other[rows, :].astype(F32)).astype(BF16) for rows in parts]
    key_grad[:, low], value_grad[:, low], query_grad[:, high] = stays
    query_sum, key_sum, value_sum = [grads[rows, :] for rows in parts]
    for step, ref in enumerate(back, 1):
        went_down = level >= step
        first, second = ref[parts[0], :].astype(F32), ref[parts[1], :].astype(F32)
        query_sum = query_sum + jnp.where(went_down, first, 0.0)
        key_sum = key_sum + jnp.where(went_down, 0.0, first)
        value_sum = value_sum + jnp.where(went_down, 0.0, second)
    query_grad[:, low] = query_sum.astype(BF16)
    key_grad[:, high] = key_sum.astype(BF16)
    value_grad[:, high] = value_sum.astype(BF16)


def ring_levels(prep, shape, positions, logit, slots, heads, width, shards):
    levels = shards // 2
    block, total = shape(2 * slots + TILE), shape(3 * slots, F32)
    own, down, up, *sends, dots = prep(
        ring_plan(levels), [shape(4 * slots + 2 * TILE)] + [block] * (levels + 1)
    )
    pair = [(s, s ^ 1) for s in range(shards)]
    arrived = [
        lax.ppermute(send, "seq", [(s, (s - 2 * step) % shards) for s in range(shards)])
        for step, send in enumerate(sends, 1)
    ]
    other = lax.ppermute(own, "seq", pair)
    dots = sum_over(dots, "tp")
    grads, own_total, other_total, router = call(
        functools.partial(ring_home_kernel, heads),
        [total] * 3 + [shape(1, F32, slots)],
        positions, logit, dots, down, up, own, other,
    )
    backs, low = [], [other_total.astype(BF16)]
    for step, arrival in enumerate(arrived, 1):
        back, own_total, other_total, *low = call(
            functools.partial(ring_away_kernel, step, levels, heads),
            [shape(2 * slots), total, total] + [shape(3 * slots)] * (step == levels - 1),
            positions, own, other, arrival, own_total, other_total,
            )
        backs.append(
            lax.ppermute(back, "seq", [(s, (s + 2 * step) % shards) for s in range(shards)])
        )
    outs = call(
        functools.partial(ring_join_kernel, heads),
        [shape(slots, BF16, width)] * 3,
        grads, own_total, lax.ppermute(low[0], "seq", pair), *backs,
    )
    return *outs, router


def call(kernel, out_shape, *args, scratch=(), ins=None, outs=None, limit=VMEM, flops=1024, aliases=None):
    ins = ins or [pltpu.VMEM] * len(args)
    outs = outs or [pltpu.VMEM] * len(out_shape)
    return pl.pallas_call(
        kernel,
        out_shape=out_shape,
        in_specs=[pl.BlockSpec(memory_space=space) for space in ins],
        out_specs=[pl.BlockSpec(memory_space=space) for space in outs],
        scratch_shapes=list(scratch),
        input_output_aliases=aliases or {},
        compiler_params=pltpu.CompilerParams(vmem_limit_bytes=limit),
        cost_estimate=pl.CostEstimate(flops=flops, bytes_accessed=1024, transcendentals=0),
    )(*args)


def sum_over(values, axis):
    size = lax.axis_size(axis)
    if size & (size - 1):
        return lax.psum(values, axis)
    reach = 1
    while reach < size:
        pairs = [(i, i ^ reach) for i in range(size)]
        values = values + lax.ppermute(values, axis, pairs)
        reach *= 2
    return values


def body(
    query_proj, key_proj, value_proj, attn_output, out_grad, log_norm, router_logit, keep_positions
):
    slots, width = query_proj.shape
    heads = log_norm.shape[1]
    half = width // 2
    shards = lax.axis_size("seq")
    logit = router_logit.reshape(1, slots)
    positions = keep_positions.reshape(-1, LANES)

    def shape(rows, dtype=BF16, columns=half):
        return jax.ShapeDtypeStruct((rows, columns), dtype)

    sources = (
        attn_output, out_grad, logit, log_norm.T, positions, query_proj, key_proj, value_proj
    )

    def prep(plan, shapes):
        dots, *outs = call(
            functools.partial(prep_kernel, plan, heads),
            [shape(1, F32, slots)] + shapes,
            *sources,
            scratch=[pltpu.VMEM(a.shape, a.dtype) for a in sources[:5]]
            + [pltpu.VMEM((4 * (2 * slots + TILE), half), BF16)]
            + [pltpu.SemaphoreType.DMA((11,)), pltpu.SemaphoreType.DMA((2 * len(plan),))],
            ins=[pltpu.HBM] * len(sources),
            outs=[pltpu.VMEM] + [pltpu.HBM] * len(shapes),
            limit=PREP_VMEM,
        )
        return *outs, dots

    if shards == 8 and lax.axis_size("tp") == 4:
        query_grad, key_grad, value_grad, router = four_levels(
            prep, shape, positions, logit, slots, heads, width
        )
    else:
        query_grad, key_grad, value_grad, router = ring_levels(
            prep, shape, positions, logit, slots, heads, width, shards
        )
    return query_grad, key_grad, value_grad, router.reshape(slots)


def solution(mesh):
    wide = P("seq", "tp")
    return jax.shard_map(
        body,
        mesh=mesh,
        in_specs=(wide,) * 6 + (P("seq"), P()),
        out_specs=(wide, wide, wide, P("seq")),
        check_vma=False,
    )
```

```python
import functools
import math

import jax
import jax.numpy as jnp
from jax import lax
from jax.experimental import pallas as pl
from jax.experimental.pallas import tpu as pltpu
from jax.sharding import PartitionSpec as P


LANES = 128
PIECE = 8
GROUP = 4
ONE = 6 * GROUP
PACK = 4
TILE = 16
BIG = 1e30
VMEM = 24 * 1024 * 1024
SUM_FLOPS = 5_000_000_000
PREP_VMEM = 63 * 1024 * 1024
F32 = jnp.float32
BF16 = jnp.bfloat16
NT = (((1,), (1,)), ((), ()))
NN = (((1,), (0,)), ((), ()))
TN = (((0,), (0,)), ((), ()))


def dot(left, right, dims):
    return lax.dot_general(left, right, dims, preferred_element_type=F32)


def pieces(rows):
    high = rows.astype(BF16).astype(F32)
    rest = rows - high
    middle = rest.astype(BF16).astype(F32)
    return [high, middle, rest - middle]


def split_exact(product):
    high = product.astype(BF16)
    return high, (product - high.astype(F32)).astype(BF16)


def used_slots(positions, shard, slots):
    table = positions[...]
    place = lax.broadcasted_iota(jnp.int32, table.shape, 0) * LANES
    place = place + lax.broadcasted_iota(jnp.int32, table.shape, 1)
    mine = (place >= shard * slots) & (place < (shard + 1) * slots) & (table >= 0)
    count = jnp.sum(jnp.where(mine, 1.0, 0.0), axis=1, keepdims=True)
    return jnp.sum(count, axis=0, keepdims=True)


def pack(ext):
    quarter = ext.shape[0] // PACK
    total = ext[:quarter]
    for part in range(1, PACK):
        rows = ext[part * quarter:(part + 1) * quarter]
        total = total + pltpu.roll(rows, part * LANES // PACK, 1)
    groups = [total[at:at + TILE] for at in range(0, quarter, TILE)]
    return jnp.concatenate(groups, axis=1).astype(BF16)


def unpack(packed):
    wide = packed.astype(F32)
    groups = [wide[:, at:at + LANES] for at in range(0, wide.shape[1], LANES)]
    total = jnp.concatenate(groups, axis=0)
    parts = [total]
    for part in range(1, PACK):
        parts.append(pltpu.roll(total, LANES - part * LANES // PACK, 1))
    return jnp.concatenate(parts, axis=0).astype(BF16)


def key_ext(positions, shard, slots):
    count = used_slots(positions, shard, slots)
    slot = lax.broadcasted_iota(jnp.int32, (slots, LANES), 0).astype(F32)
    lane = lax.broadcasted_iota(jnp.int32, (slots, LANES), 1)
    return jnp.where((lane == ONE) & (slot >= count), -BIG, 0.0).astype(BF16)


def prep_kernel(plan, heads, *refs):
    sources, (query, key, value), rest = refs[:5], refs[5:8], refs[8:]
    dots, outs, rest = rest[0], rest[1:len(plan) + 1], rest[len(plan) + 1:]
    held, (bank, sems, done) = rest[:5], rest[5:]
    output, grad, logit, norm, positions = held
    slots, width = grad.shape
    half = width // 2
    rows = 2 * slots + TILE
    copies = [
        pltpu.make_async_copy(source, dest, sems.at[i])
        for i, (source, dest) in enumerate(zip(sources, held))
    ]
    for at in range(2):
        for source, base in ((key, at), (value, at + 0.5), (query, at + 2)):
            first = int(base) * rows + (slots if base % 1 else 0)
            copies.append(
                pltpu.make_async_copy(
                    source.at[:, pl.ds(at * half, half)],
                    bank.at[pl.ds(first, slots), :],
                    sems.at[len(copies)],
                )
            )
    for copy in copies:
        copy.start()
    for copy in copies[5:]:
        copy.wait()
    for at in range(2):
        bank[pl.ds(at * rows + 2 * slots, TILE), :] = jnp.zeros((TILE, half), BF16)
    level = lax.axis_index("seq") // 2
    moves = []
    for out, blocks in zip(outs, plan):
        for place, block in enumerate(blocks(level)):
            block = jnp.int32(block)
            move = pltpu.make_async_copy(
                bank.at[pl.ds(pl.multiple_of(block * rows, TILE), rows), :],
                out.at[pl.ds(place * rows, rows), :],
                done.at[len(moves)],
            )
            moves.append((block, move))

    def each(some, early):
        for block, move in some:

            @pl.when((block < 2) == early)
            def _():
                move.start()

    each(moves, True)
    for copy in copies[:5]:
        copy.wait()
    head_dim = width // heads
    root = math.sqrt(head_dim)
    shard = lax.axis_index("seq")
    count = used_slots(positions, shard, slots)
    lane = lax.broadcasted_iota(jnp.int32, (PIECE, slots), 1).astype(F32)
    used = lane < count
    gate_row = jax.nn.sigmoid(logit[...])
    gate = jnp.transpose(jnp.broadcast_to(gate_row, (LANES, slots)))
    head_of = lax.broadcasted_iota(jnp.int32, (PIECE, width), 1) // head_dim
    head_row = lax.broadcasted_iota(jnp.int32, (PIECE, width), 0)
    pick = (head_of == head_row).astype(BF16)
    ones = jnp.ones((PIECE, width), BF16)
    dout_parts, delta_parts, dot_parts = [], [], []
    for h in range(heads):
        cols = pl.ds(h * head_dim, head_dim)
        wide = grad[:, cols].astype(F32)
        out = output[:, cols].astype(F32)
        dout = (wide * gate).astype(BF16)
        dout_parts.append(dout)
        delta_parts.append(dout.astype(F32) * out)
        dot_parts.append(wide * out)
    delta_high, delta_low = split_exact(jnp.concatenate(delta_parts, axis=1))
    delta = dot(pick, delta_high, NT) + dot(pick, delta_low, NT)
    dot_high, dot_low = split_exact(jnp.concatenate(dot_parts, axis=1))
    dots[...] = (dot(ones, dot_high, NT) + dot(ones, dot_low, NT))[:1]

    pad = jnp.zeros((PIECE - heads, slots), F32)
    scaled = jnp.where(used, jnp.concatenate([norm[...] * root, pad], axis=0), BIG)
    delta = jnp.where(used, delta, 0.0)
    first = lax.broadcasted_iota(jnp.int32, (PIECE, slots), 0) == 0
    stack = pieces(scaled) + pieces(delta) + [jnp.where(first, 1.0, 0.0)]
    stack.append(jnp.zeros((PIECE * (PIECE - len(stack)), slots), F32))
    stats = jnp.concatenate(stack, axis=0).astype(BF16)
    source = lax.broadcasted_iota(jnp.int32, (PIECE * PIECE, LANES), 0)
    target = lax.broadcasted_iota(jnp.int32, (PIECE * PIECE, LANES), 1)
    piece, head = source // PIECE, source % PIECE

    def ext(first_head):
        local = head - first_head
        taken = (local >= 0) & (local < heads // 2) & (piece < 6)
        column = jnp.where(taken, piece * GROUP + local, -1)
        column = jnp.where(source == 6 * PIECE, ONE, column)
        return dot(stats, (column == target).astype(BF16), TN)

    per = heads // 2
    for at in range(2):
        base = (2 + at) * rows
        bank[pl.ds(base + slots, slots), :] = jnp.concatenate(
            dout_parts[at * per:(at + 1) * per], axis=1
        )
        bank[pl.ds(base + 2 * slots, TILE), :] = pack(ext(at * per))
    each(moves, False)
    for _, move in moves:
        move.wait()


def head_marks(head, is_value):
    lane = lax.broadcasted_iota(jnp.int32, (1, LANES), 1)
    base = (3 * GROUP if is_value else 0) + head
    marked = (lane == base) | (lane == base + GROUP) | (lane == base + 2 * GROUP)
    return jnp.where(marked, -1.0, 0.0).astype(BF16)


def meet(down, movings, stays, positions, heads, mask, emit, add):
    half = movings[0][0].shape[1]
    slots = emit.slots
    head_dim = half // (heads // 2)
    scale = head_dim ** -0.5
    to_log2 = scale * math.log2(math.e)

    def stats(blocks, queries):
        parts = []
        for ref, at, shard in blocks:
            if queries:
                parts.append(unpack(ref[pl.ds(at + 2 * slots, TILE), :]))
            else:
                parts.append(key_ext(positions, shard, slots))
        return jnp.concatenate(parts, axis=0)

    def load(blocks, which, cols):
        parts = [ref[pl.ds(at + which * slots, slots), cols] for ref, at, _ in blocks]
        return jnp.concatenate(parts, axis=0)

    moving_ext, stay_ext = stats(movings, down), stats(stays, not down)
    for h in range(heads // 2):
        cols = pl.ds(h * head_dim, head_dim)
        m1, m2 = load(movings, 0, cols), load(movings, 1, cols)
        r1, r2 = load(stays, 0, cols), load(stays, 1, cols)
        key_mark, value_mark = head_marks(h, False), head_marks(h, True)
        if down:
            m1_ext, m2_ext = moving_ext, moving_ext
            r1_ext = stay_ext + key_mark
            r2_ext = jnp.broadcast_to(value_mark, stay_ext.shape)
        else:
            m1_ext = moving_ext + key_mark
            m2_ext = jnp.broadcast_to(value_mark, moving_ext.shape)
            r1_ext, r2_ext = stay_ext, stay_ext
        scores = dot(
            jnp.concatenate([m1, m1_ext], axis=1), jnp.concatenate([r1, r1_ext], axis=1), NT
        )
        if mask is not None:
            scores = jnp.where(mask, scores, -BIG)
        prob = jnp.exp2(scores * to_log2)
        dprob = dot(
            jnp.concatenate([m2, m2_ext], axis=1), jnp.concatenate([r2, r2_ext], axis=1), NT
        )
        dscore = (prob * dprob * scale).astype(BF16)
        prob = prob.astype(BF16)
        emit(0, cols, dot(dscore, r1, NN))
        add(0, cols, dot(dscore, m1, TN))
        if down:
            add(1, cols, dot(prob, m2, TN))
        else:
            emit(1, cols, dot(prob, r2, NN))


class Store:
    def __init__(self, slots, targets, fresh, olds=None):
        self.slots, self.targets, self.fresh = slots, targets, fresh
        self.olds = olds or [ref for ref, _ in targets]

    def __call__(self, which, cols, term):
        for i, (ref, base) in enumerate(self.targets):
            rows = pl.ds(base + which * self.slots, self.slots)
            part = term[i * self.slots:(i + 1) * self.slots]
            part = part if self.fresh else self.olds[i][rows, cols] + part
            ref[rows, cols] = part.astype(ref.dtype)


def causal(down, slots, shard=None):
    shape = (slots, slots if shard is None else 2 * slots)
    row = lax.broadcasted_iota(jnp.int32, shape, 0)
    place = lax.broadcasted_iota(jnp.int32, shape, 1)
    if shard is not None:
        place = jnp.where(place < slots, place, slots - shard % 2 * (slots + 1))
    return place <= row if down else place >= row


def router_part(positions, logit, dots, slots, shard):
    gate = jax.nn.sigmoid(logit[...])
    lane = lax.broadcasted_iota(jnp.int32, (1, slots), 1).astype(F32)
    used = lane < used_slots(positions, shard, slots)
    return jnp.where(used, gate * (1.0 - gate) * dots, 0.0)


FOUR_PLAN = (
    lambda level: [jnp.where(level < 2, 0, 2), jnp.where(level < 2, 1, 3)],
    lambda level: [jnp.where(level < 2, 2, 0), jnp.where(level < 2, 3, 1)],
    lambda level: [jnp.where(level % 2 == 0, 0, 3)],
    lambda level: [jnp.where(level < 2, 1, 2)],
)


def four_home_kernel(heads, positions, mine, own, turn, grads, own_total):
    slots = grads.shape[0] // 4
    rows = 2 * slots + TILE
    shard = lax.axis_index("seq")
    turn[...] = jnp.zeros(turn.shape, F32)
    for down in (True, False):

        @pl.when((shard < 4) == down)
        def _():
            for at in range(2):
                base = 2 * slots * at
                meet(
                    down, [(mine, at * rows, shard)], [(own, at * rows, shard)],
                    positions, heads, causal(down, slots),
                    Store(slots, [(grads, base)], True),
                    Store(slots, [(own_total, base)], True),
                )


def meets_pair(shard):
    return (shard % 2 == 1) == (shard < 4)


def follow_kernel(block, after, out):
    pass


def four_pair_kernel(
    heads, positions, after, mine, other, turn, grads_pair, met_total, early, early_total
):
    slots = early.shape[0] // 2
    rows = 2 * slots + TILE
    shard = lax.axis_index("seq")
    meets = meets_pair(shard)
    turn[...] = after[...]
    for level in range(4):

        @pl.when(meets & (shard // 2 == level))
        def _():
            for at in range(2):
                met = at == (1, 0, 1, 0)[level]
                meet(
                    level < 2, [(mine, at * rows, shard)], [(other, at * rows, shard ^ 1)],
                    positions, heads, None,
                    Store(slots, [(grads_pair, 2 * slots * at)], True),
                    Store(slots, [(met_total if met else early_total, 0)], True),
                )
            early[...] = early_total[...].astype(BF16)

    @pl.when(jnp.logical_not(meets))
    def _():
        early[...] = jnp.zeros(early.shape, BF16)


def four_skip_kernel(
    heads, positions, after, mine, own, other, near, skip,
    turn, own_near, other_near, back, near_total, grads_guest, skip_part
):
    slots = back.shape[0] // 2
    rows = 2 * slots + TILE
    shard = lax.axis_index("seq")
    turn[...] = after[...]
    for level in range(4):
        at = (1, 0, 1, 0)[level]

        @pl.when(shard // 2 == level)
        def _():
            pair = [(own, at * rows, shard), (other, at * rows, shard ^ 1)]
            totals = Store(slots, [(own_near, 0), (other_near, 0)], True)
            guest = [(near, 0, shard - 2)]
            if level in (0, 3):
                meet(
                    level == 0, guest, pair, positions, heads, None,
                    Store(slots, [(back, 0)], True), totals,
                )
                return
            far = [(skip, 0, shard - 4)]
            meet(
                level == 1, [(mine, at * rows, shard)] + far, guest, positions, heads, None,
                Store(slots, [(grads_guest, 0), (skip_part, 0)], True),
                Store(slots, [(near_total, 0)], True),
            )
            meet(
                level == 1, far, pair, positions, heads, None,
                Store(slots, [(skip_part, 0)], False), totals,
            )


def four_near_kernel(
    heads, positions, after, dots, dots_near, near, middle, back, near_total,
    dots_sum, near_low, middle_part
):
    slots = near_low.shape[0] // 2
    shard = lax.axis_index("seq")
    dots_sum[...] = dots[...] + dots_near[...]
    for level in range(4):

        @pl.when(shard // 2 == level)
        def _():
            if level in (0, 3):
                near_low[...] = back[...]
                return
            meet(
                level == 1, [(middle, 0, shard - 2)], [(near, 0, shard - 2)],
                positions, heads, None,
                Store(slots, [(middle_part, 0)], True),
                Store(slots, [(near_low, 0)], False, [near_total]),
            )


def four_last_kernel(
    heads, positions, dots_in, mine, own, other, cross, skip, middle,
    grads_in, skip_in, middle_in, met_pair, own_in, other_in,
    dots, grads_guest, skip_back, cross_low, middle_back, late, own_near,
    middle_part, other_near,
):
    slots = grads_in.shape[0] // 2
    rows = 2 * slots + TILE
    shard = lax.axis_index("seq")
    meets = meets_pair(shard)
    dots[...] = dots_in[...]
    for level in range(4):
        at = (1, 0, 1, 0)[level]

        @pl.when(shard // 2 == level)
        def _():
            if level in (0, 3):
                own_near[...] = own_in[...]
                other_near[...] = other_in[...]
            else:
                far = [(skip, 0, shard - 4), (middle, 0, shard - 2)]
                meet(
                    level == 1, far[1:], [(own, at * rows, shard), (other, at * rows, shard ^ 1)],
                    positions, heads, None,
                    Store(slots, [(middle_part, 0)], False, [middle_in]),
                    Store(slots, [(own_near, 0), (other_near, 0)], False, [own_in, other_in]),
                )
                meet(
                    level == 1, [(mine, at * rows, shard)] + far, [(cross, 0, (shard - 2) ^ 1)],
                    positions, heads, None,
                    Store(
                        slots, [(grads_guest, 0), (skip_back, 0), (middle_back, 0)], False,
                        [grads_in, skip_in, middle_part],
                    ),
                    Store(slots, [(cross_low, 0)], True),
                )

    late[...] = (other_near[...] + jnp.where(meets, met_pair[...], 0.0)).astype(BF16)


def four_sum_kernel(heads, grads, grads_pair, own, near, early, moving_sum, staying_sum):
    slots = grads.shape[0] // 4
    shard = lax.axis_index("seq")
    meets = meets_pair(shard)
    for level in range(4):

        @pl.when(shard // 2 == level)
        def _():
            for at in range(2):
                part = pl.ds(2 * slots * at, 2 * slots)
                moving = grads[part, :] + jnp.where(meets, grads_pair[part, :], 0.0)
                staying = own[part, :]
                if at != (1, 0, 1, 0)[level]:
                    staying = staying + early[...].astype(F32)
                    if level in (1, 2):
                        moving = moving + near[...].astype(F32)
                    else:
                        staying = staying + near[...].astype(F32)
                moving_sum[part, :] = moving
                staying_sum[part, :] = staying


def four_join_kernel(
    heads, positions, logit, dots, dots_far, moving_sum, staying_sum, grads_guest, own_near,
    middle, late, skip, cross, query_grad, key_grad, value_grad, router
):
    slots, half = moving_sum.shape[0] // 4, moving_sum.shape[1]
    shard = lax.axis_index("seq")
    router[...] = router_part(positions, logit, dots[...] + dots_far[...], slots, shard)
    for level in range(4):
        inner = level in (1, 2)

        @pl.when(shard // 2 == level)
        def _():
            if level < 2:
                moving, staying = [query_grad], [key_grad, value_grad]
            else:
                moving, staying = [key_grad, value_grad], [query_grad]
            for at in range(2):
                cols = pl.ds(at * half, half)
                met = at == (1, 0, 1, 0)[level]
                plus = [grads_guest] if inner and met else []
                if inner:
                    extra = [own_near, late] if met else [middle]
                else:
                    extra = [own_near, skip, late] if met else [cross]
                for outs, base, more in ((moving, moving_sum, plus), (staying, staying_sum, extra)):
                    for which, out in enumerate(outs):
                        rows = pl.ds((2 * at + which) * slots, slots)
                        total = base[rows, :]
                        for ref in more:
                            total = total + ref[pl.ds(which * slots, slots), :].astype(F32)
                        out[:, cols] = total.astype(BF16)


def four_levels(prep, shape, positions, logit, slots, heads, width):
    double, block, total = shape(4 * slots + 2 * TILE), shape(2 * slots + TILE), shape(2 * slots, F32)
    totals, low = shape(4 * slots, F32), shape(2 * slots)
    own, mine, near_send, far_send, dots = prep(FOUR_PLAN, [double, double, block, block])
    def pairs(levels, flip=0):
        return [(2 * a + c, 2 * b + (c ^ flip)) for a, b in levels for c in range(2)]

    near = lax.ppermute(near_send, "seq", pairs([(0, 1), (1, 0), (2, 3), (3, 2)]))
    other = lax.ppermute(own, "seq", pairs([(i, i) for i in range(4)], 1))
    skip = lax.ppermute(far_send, "seq", pairs([(0, 2), (3, 1)]))
    middle = lax.ppermute(far_send, "seq", pairs([(1, 2), (2, 1)]))
    row = shape(1, F32, slots)
    turn, grads, own_total = call(
        functools.partial(four_home_kernel, heads),
        [row] + [totals] * 2,
        positions, mine, own,
    )
    (near,) = call(
        follow_kernel, [block], near, turn, ins=[pl.ANY, pltpu.VMEM], outs=[pl.ANY], aliases={0: 0}
    )
    cross = lax.ppermute(near, "seq", pairs([(1, 1), (2, 2)], 1))
    turn, grads_pair, met_pair, early = call(
        functools.partial(four_pair_kernel, heads),
        [row, totals, total, low],
        positions, turn, mine, other,
        scratch=[pltpu.VMEM(total.shape, F32)],
    )
    early = lax.ppermute(early, "seq", pairs([(i, i) for i in range(4)], 1))
    turn, own_near, other_near, step_back, near_total, grads_guest, skip_part = call(
        functools.partial(four_skip_kernel, heads),
        [row, total, total, low, total, total, total],
        positions, turn, mine, own, other, near, skip,
    )
    dots_near = lax.ppermute(dots, "tp", [(i, i ^ 1) for i in range(4)])
    dots, near_low, middle_part = call(
        functools.partial(four_near_kernel, heads),
        [row, low, total],
        positions, turn, dots, dots_near, near, middle, step_back, near_total,
    )
    near = lax.ppermute(near_low, "seq", pairs([(0, 1), (1, 0), (2, 3), (3, 2)]))
    dots, grads_guest, skip_back, cross_low, middle_back, late, own_near = call(
        functools.partial(four_last_kernel, heads),
        [row, total, low, low, low, low, total],
        positions, dots, mine, own, other, cross, skip, middle,
        grads_guest, skip_part, middle_part, met_pair, own_near, other_near,
        scratch=[pltpu.VMEM(total.shape, F32)] * 2,
    )
    dots_far = lax.ppermute(dots, "tp", [(i, i ^ 2) for i in range(4)])
    skip = lax.ppermute(skip_back, "seq", pairs([(2, 0), (1, 3)]))
    cross = lax.ppermute(cross_low, "seq", pairs([(1, 0), (2, 3)], 1))
    middle = lax.ppermute(middle_back, "seq", pairs([(1, 2), (2, 1)]))
    late = lax.ppermute(late, "seq", pairs([(i, i) for i in range(4)], 1))
    moving_sum, staying_sum = call(
        functools.partial(four_sum_kernel, heads),
        [totals] * 2,
        grads, grads_pair, own_total, near, early,
        flops=SUM_FLOPS,
    )
    return call(
        functools.partial(four_join_kernel, heads),
        [shape(slots, BF16, width)] * 3 + [row],
        positions, logit, dots, dots_far, moving_sum, staying_sum, grads_guest, own_near,
        middle, late, skip, cross,
    )


def ring_plan(levels):
    sends = [
        lambda level, step=step: [jnp.where(level >= step, 2, 1)] for step in range(1, levels)
    ]
    return (lambda level: [0, 3], lambda level: [2], lambda level: [1], *sends)


def ring_home_kernel(
    heads, positions, logit, dots, down, up, own, other, grads, own_total, other_total, router
):
    slots = grads.shape[0] // 3
    rows = 2 * slots + TILE
    shard = lax.axis_index("seq")
    for goes_down, mine, at, base, stay_base in ((True, down, 0, 0, 0), (False, up, rows, 1, 2)):
        meet(
            goes_down, [(mine, 0, shard)], [(own, at, shard), (other, at, shard ^ 1)],
            positions, heads, causal(goes_down, slots, shard),
            Store(slots, [(grads, base * slots)], True),
            Store(slots, [(own_total, stay_base * slots), (other_total, stay_base * slots)], True),
        )
    router[...] = router_part(positions, logit, dots[...], slots, shard)


def ring_away_kernel(
    step, levels, heads, positions, own, other, block, own_in, other_in,
    back, own_total, other_total, *low
):
    slots = own_in.shape[0] // 3
    own_total[...] = own_in[...]
    other_total[...] = other_in[...]
    rows = 2 * slots + TILE
    shard = lax.axis_index("seq")
    for goes_down, at, base in ((True, 0, 0), (False, rows, 2 * slots)):

        @pl.when((shard // 2 + step < levels) == goes_down)
        def _():
            meet(
                goes_down, [(block, 0, shard + 2 * (step - levels))],
                [(own, at, shard), (other, at, shard ^ 1)],
                positions, heads, None,
                Store(slots, [(back, 0)], True),
                Store(slots, [(own_total, base), (other_total, base)], False),
            )

    for ref in low:
        ref[...] = other_total[...].astype(BF16)


def ring_join_kernel(heads, grads, own, other, *refs):
    back, (query_grad, key_grad, value_grad) = refs[:-3], refs[-3:]
    slots, half = grads.shape[0] // 3, grads.shape[1]
    level = lax.axis_index("seq") // 2
    low, high = pl.ds(0, half), pl.ds(half, half)
    parts = [pl.ds(i * slots, slots) for i in range(3)]
    stays = [(own[rows, :] + other[rows, :].astype(F32)).astype(BF16) for rows in parts]
    key_grad[:, low], value_grad[:, low], query_grad[:, high] = stays
    query_sum, key_sum, value_sum = [grads[rows, :] for rows in parts]
    for step, ref in enumerate(back, 1):
        went_down = level >= step
        first, second = ref[parts[0], :].astype(F32), ref[parts[1], :].astype(F32)
        query_sum = query_sum + jnp.where(went_down, first, 0.0)
        key_sum = key_sum + jnp.where(went_down, 0.0, first)
        value_sum = value_sum + jnp.where(went_down, 0.0, second)
    query_grad[:, low] = query_sum.astype(BF16)
    key_grad[:, high] = key_sum.astype(BF16)
    value_grad[:, high] = value_sum.astype(BF16)


def ring_levels(prep, shape, positions, logit, slots, heads, width, shards):
    levels = shards // 2
    block, total = shape(2 * slots + TILE), shape(3 * slots, F32)
    own, down, up, *sends, dots = prep(
        ring_plan(levels), [shape(4 * slots + 2 * TILE)] + [block] * (levels + 1)
    )
    pair = [(s, s ^ 1) for s in range(shards)]
    arrived = [
        lax.ppermute(send, "seq", [(s, (s - 2 * step) % shards) for s in range(shards)])
        for step, send in enumerate(sends, 1)
    ]
    other = lax.ppermute(own, "seq", pair)
    dots = sum_over(dots, "tp")
    grads, own_total, other_total, router = call(
        functools.partial(ring_home_kernel, heads),
        [total] * 3 + [shape(1, F32, slots)],
        positions, logit, dots, down, up, own, other,
    )
    backs, low = [], [other_total.astype(BF16)]
    for step, arrival in enumerate(arrived, 1):
        back, own_total, other_total, *low = call(
            functools.partial(ring_away_kernel, step, levels, heads),
            [shape(2 * slots), total, total] + [shape(3 * slots)] * (step == levels - 1),
            positions, own, other, arrival, own_total, other_total,
            )
        backs.append(
            lax.ppermute(back, "seq", [(s, (s + 2 * step) % shards) for s in range(shards)])
        )
    outs = call(
        functools.partial(ring_join_kernel, heads),
        [shape(slots, BF16, width)] * 3,
        grads, own_total, lax.ppermute(low[0], "seq", pair), *backs,
    )
    return *outs, router


def call(kernel, out_shape, *args, scratch=(), ins=None, outs=None, limit=VMEM, flops=1024, aliases=None):
    ins = ins or [pltpu.VMEM] * len(args)
    outs = outs or [pltpu.VMEM] * len(out_shape)
    return pl.pallas_call(
        kernel,
        out_shape=out_shape,
        in_specs=[pl.BlockSpec(memory_space=space) for space in ins],
        out_specs=[pl.BlockSpec(memory_space=space) for space in outs],
        scratch_shapes=list(scratch),
        input_output_aliases=aliases or {},
        compiler_params=pltpu.CompilerParams(vmem_limit_bytes=limit),
        cost_estimate=pl.CostEstimate(flops=flops, bytes_accessed=1024, transcendentals=0),
    )(*args)


def sum_over(values, axis):
    size = lax.axis_size(axis)
    if size & (size - 1):
        return lax.psum(values, axis)
    reach = 1
    while reach < size:
        pairs = [(i, i ^ reach) for i in range(size)]
        values = values + lax.ppermute(values, axis, pairs)
        reach *= 2
    return values


def body(
    query_proj, key_proj, value_proj, attn_output, out_grad, log_norm, router_logit, keep_positions
):
    slots, width = query_proj.shape
    heads = log_norm.shape[1]
    half = width // 2
    shards = lax.axis_size("seq")
    logit = router_logit.reshape(1, slots)
    positions = keep_positions.reshape(-1, LANES)

    def shape(rows, dtype=BF16, columns=half):
        return jax.ShapeDtypeStruct((rows, columns), dtype)

    sources = (
        attn_output, out_grad, logit, log_norm.T, positions, query_proj, key_proj, value_proj
    )

    def prep(plan, shapes):
        dots, *outs = call(
            functools.partial(prep_kernel, plan, heads),
            [shape(1, F32, slots)] + shapes,
            *sources,
            scratch=[pltpu.VMEM(a.shape, a.dtype) for a in sources[:5]]
            + [pltpu.VMEM((4 * (2 * slots + TILE), half), BF16)]
            + [pltpu.SemaphoreType.DMA((11,)), pltpu.SemaphoreType.DMA((2 * len(plan),))],
            ins=[pltpu.HBM] * len(sources),
            outs=[pltpu.VMEM] + [pltpu.HBM] * len(shapes),
            limit=PREP_VMEM,
        )
        return *outs, dots

    if shards == 8 and lax.axis_size("tp") == 4:
        query_grad, key_grad, value_grad, router = four_levels(
            prep, shape, positions, logit, slots, heads, width
        )
    else:
        query_grad, key_grad, value_grad, router = ring_levels(
            prep, shape, positions, logit, slots, heads, width, shards
        )
    return query_grad, key_grad, value_grad, router.reshape(slots)


def solution(mesh):
    wide = P("seq", "tp")
    return jax.shard_map(
        body,
        mesh=mesh,
        in_specs=(wide,) * 6 + (P("seq"), P()),
        out_specs=(wide, wide, wide, P("seq")),
        check_vma=False,
    )
```
